32 devices in a mesh: dp: 8 (over z, x), seq: 4 (over y, core).
Axes of the slice: x: 2, y: 2, z: 4, core: 2. Of those that a mesh axis runs over, the one named last changes fastest.
Arguments:
- words: bfloat16 [32, 1024, 1024], P('dp', 'seq'), may hold values from -6 to 6
- patches: bfloat16 [32, 2048, 1024], P('dp', 'seq'), may hold values from -6 to 6
- proj: bfloat16 [1024, 1024], P('dp'), may hold values from -0.1875 to 0.1875
- routes: int32 [32, 1024, 1], P('dp', 'seq'), may hold values from 0 to 3; in each aligned block of 256 rows (0 to 255, 256 to 511, ..., all dimensions but the last counted through in order) at most 128 rows name the same one
- targets: int32 [32, 1024], P('dp', 'seq'), may hold values from 0 to 511
- counts: int32 [32], P('dp'), may hold values from 512 to 1024
- flags: int32 [32, 16, 32], P('dp'), may hold values 0 or 1
Outputs:
- word_loss: float32 [32, 1024], P('dp', 'seq')
- proj_grad: float32 [1024, 1024], P('dp', 'seq')
The draws below stay inside these ranges and needn't reach their ends.
Inputs may be any that keep to these rules, and one draw needn't show every extreme that they name: `routes`: among the 256 words of one page held by one index of seq, at most 128 name the same shard; some block reaches 128.
All inputs are finite; a program needn't handle non-finite values. No bound on the sum of `flags` on one device may be relied on, other than what follows from the above.
Results may differ from the reference program's by a relative error of at most 0.0065.
Values may be sent and summed in bfloat16 or wider, within the bound.
No kernel may reach another device: no remote copies, remote signals or barrier semaphores. Data moves between devices by JAX's collectives and lax.ppermute only.
A program may use at most 64 MiB of HBM per device.

```python
import math
import jax
import jax.numpy as jnp
import numpy as np
from jax import lax

D = 1024
P_SIZE = 2048
PAGE_WORD_SLOTS = 1024
MARGIN_BLOCK_SIZE = 64
PAGES = 32
W_DEV = 256
PPS = 512
CAP = 128
WB = 16
PB = 32
N_SEQ = 4


def draw_counts(key, part):
    drawn = jax.random.randint(key, (PAGES,), PAGE_WORD_SLOTS // 2, PAGE_WORD_SLOTS + 1, dtype=jnp.int32)
    return drawn.at[0].set(PAGE_WORD_SLOTS)


def with_ends(values, key, least, top_value):
    longest = values.shape.index(max(values.shape))
    spots = []
    for shift in (0, 1):
        where = [jax.random.randint(jax.random.fold_in(key, axis), (), 0, length) for axis, length in enumerate(values.shape)]
        where[longest] = (where[longest] + shift) % values.shape[longest]
        spots.append(tuple(where))
    return values.at[spots[0]].set(least).at[spots[1]].set(top_value)


def spiked(values, stream_key, source, target, blocks, factor):
    def block_of(position):
        return (jnp.arange(values.shape[position]) // (values.shape[position] // blocks)).reshape((-1,) + (1,) * (values.ndim - 1 - position))

    one_side = jax.random.permutation(stream_key, blocks)[block_of(target)]
    second = (block_of(target) + blocks // 2) % blocks
    return jnp.where((block_of(source) == one_side) | (block_of(source) == second), factor * values, values)


def level_of(rng, dims, split, least, high):
    loudness = 1.0
    for position, shards_of in split:
        steps = jax.random.uniform(jax.random.fold_in(jax.random.fold_in(rng, 6), position), (shards_of,), jnp.float32, least / len(split), high / len(split))
        loudness = loudness * jnp.repeat(jnp.exp(steps), dims[position] // shards_of).reshape((-1,) + (1,) * (len(dims) - 1 - position))
    return loudness


def shared_out(stream_key, own, number, rows, number_of, top, reach, skew):
    order = jax.random.permutation(stream_key, number_of)
    heavy_load, common = load_shares(number_of, rows * top, reach, skew, True), load_shares(number_of, rows * top, reach, skew, False)
    places = jnp.arange(number_of)

    def named(lengths, rotation):
        used = int((lengths > 0).sum())
        fixed = max(1, used // 4)
        shifted = fixed + (places - fixed + rotation * (used - fixed)) % max(1, number_of - fixed)
        return jnp.zeros((number_of,), jnp.int32).at[order[jnp.where(places < fixed, places, shifted)]].set(jnp.asarray(lengths, jnp.int32))

    lengths = jnp.where(number % 4 == 0, named(heavy_load, number // 4), named(common, number - number // 4 - 1))
    mixed = jax.random.permutation(jax.random.fold_in(own, 3), number_of)
    donor, receiver = mixed[0:number_of // 2 * 2:2], mixed[1:number_of // 2 * 2:2]
    room = jnp.minimum(lengths[donor] - 1, reach - lengths[receiver]) // 2
    room = jnp.where((donor == order[0]) | (receiver == order[0]) | (lengths[receiver] == 0), 0, jnp.maximum(room, 0))
    shifted = jax.random.randint(jax.random.fold_in(own, 4), (number_of // 2,), 0, 1 << 20) % (room + 1)
    lengths = lengths.at[donor].add(-shifted).at[receiver].add(shifted)
    members = jnp.searchsorted(jnp.cumsum(lengths), jnp.arange(rows * top), side="right").astype(jnp.int32)
    grid = members.reshape(top, rows).T
    grid = grid[jax.random.permutation(jax.random.fold_in(own, 1), rows)]
    rotation = jax.random.randint(jax.random.fold_in(own, 2), (rows, 1), 0, top)
    return jnp.take_along_axis(grid, (jnp.arange(top)[None, :] + rotation) % top, axis=1)


def load_shares(amount, total, reach, lean, full):
    weights = [(1 << 20) // math.isqrt(standing ** lean) + 1 for standing in range(1, amount + 1)]
    largest = reach if full else min(reach, max(-(-total // amount), total * weights[0] // sum(weights)))
    least = 1 if total - largest >= amount - 1 else 0
    holding, surplus = [largest] + [least] * (amount - 1), total - largest - least * (amount - 1)
    while surplus > 0:
        free = [i for i in range(1, amount) if holding[i] < largest] or [i for i in range(1, amount) if holding[i] < reach]
        mass, remaining = sum([weights[i] for i in free]), surplus
        for i in free:
            addition = min(reach - holding[i], max(1, remaining * weights[i] // mass), surplus)
            holding[i] = holding[i] + addition
            surplus = surplus - addition
    return np.array(holding)


def normal_values(key, extent, deviation, reach, cuts=(), kind=jnp.bfloat16):
    factor_of = level_of(key, extent, cuts, -0.22, 0.18) if cuts else 1.0
    entries = jax.random.normal(key, extent, jnp.float32) * deviation * factor_of
    return jnp.minimum(jnp.maximum(entries, -reach), reach).astype(kind)


def bell_draw_with(own_key, extent, width, limit, shards, heavy, held_as=jnp.bfloat16):
    values = width * jax.random.normal(own_key, extent, jnp.float32)
    if shards:
        values = values * level_of(own_key, extent, shards, -0.22, 0.18)
    return jnp.clip(spiked(values, jax.random.fold_in(own_key, 3), *heavy), -limit, limit).astype(held_as)


def setup_inputs(seed: int = 0) -> dict:
    arg_keys = jax.random.split(jax.random.key(seed), 8)
    words = bell_draw_with(arg_keys[0], (PAGES, PAGE_WORD_SLOTS, D), 1.0, 6.0, ((0, 8), (1, 4)), (0, 2, 8, 2.0))
    patches = normal_values(arg_keys[1], (PAGES, P_SIZE, D), 1.0, 6.0, ((0, 8), (1, 4)))
    proj = normal_values(arg_keys[2], (D, D), D ** -0.5, 0.1875, ((0, 8),))
    routes_keys = jax.random.split(jax.random.fold_in(arg_keys[3], 1), PAGES * PAGE_WORD_SLOTS // W_DEV)
    routes_turns = jax.random.permutation(jax.random.fold_in(arg_keys[3], 3), PAGES * PAGE_WORD_SLOTS // W_DEV)
    routes = jax.vmap(lambda own, number: shared_out(jax.random.fold_in(arg_keys[3], 2), own, number, W_DEV, N_SEQ, 1, CAP, 2))(routes_keys, routes_turns).reshape((PAGES, PAGE_WORD_SLOTS, 1))
    targets = with_ends(jax.random.randint(arg_keys[4], (PAGES, PAGE_WORD_SLOTS), 0, PPS), jax.random.fold_in(arg_keys[4], 1), 0, PPS - 1).astype(jnp.int32)
    counts = draw_counts(jax.random.fold_in(arg_keys[7], 71), 0)
    flags = with_ends((jax.random.randint(arg_keys[6], (PAGES, WB, PB), 0, 4) < 1).astype(jnp.int32), jax.random.fold_in(arg_keys[6], 1), 0, 1)
    return {"words": words, "patches": patches, "proj": proj, "routes": routes, "targets": targets, "counts": counts, "flags": flags}


def reference(words, patches, proj, routes, targets, counts, flags):
    scale = 2.0 / math.sqrt(D)
    capacity_limit = 2 * PAGE_WORD_SLOTS // (N_SEQ * N_SEQ)
    wdev = PAGE_WORD_SLOTS // N_SEQ
    pps = P_SIZE // N_SEQ
    bps = pps // MARGIN_BLOCK_SIZE
    nblk = PAGE_WORD_SLOTS // MARGIN_BLOCK_SIZE

    def page(grad, inputs):
        feats, patch, route, target, routed_count, flag = inputs
        query = jnp.dot(feats, proj, preferred_element_type=jnp.float32).astype(jnp.bfloat16)
        destination_slot = route[:, 0]
        home = jnp.arange(PAGE_WORD_SLOTS, dtype=jnp.int32) // wdev
        onehot = (destination_slot[:, None] == jnp.arange(N_SEQ, dtype=jnp.int32)[None, :]).astype(jnp.int32)
        onehot = onehot.reshape(N_SEQ, wdev, N_SEQ)
        rank = jnp.cumsum(onehot, axis=1) - onehot
        slot = lax.optimization_barrier(jnp.sum(rank * onehot, axis=2)).reshape(PAGE_WORD_SLOTS)
        column_offset = home * capacity_limit + slot
        qbuf = jnp.zeros((N_SEQ, N_SEQ * capacity_limit, D), jnp.bfloat16).at[destination_slot, column_offset].set(query)
        tbuf = jnp.zeros((N_SEQ, N_SEQ * capacity_limit), jnp.int32).at[destination_slot, column_offset].set(target)
        index_buffer = jnp.full((N_SEQ, N_SEQ * capacity_limit), -1, jnp.int32).at[destination_slot, column_offset].set(jnp.arange(PAGE_WORD_SLOTS, dtype=jnp.int32))
        patch_s = patch.reshape(N_SEQ, pps, D)
        scores = jnp.einsum('sud,skd->suk', qbuf.astype(jnp.float32), patch_s.astype(jnp.float32)) * scale
        table = flag.reshape(nblk, N_SEQ, bps).transpose(1, 0, 2)
        word_block = jnp.maximum(index_buffer, 0) // MARGIN_BLOCK_SIZE
        hit = jnp.take_along_axis(table, jnp.broadcast_to(word_block[:, :, None], (N_SEQ, N_SEQ * capacity_limit, bps)), axis=1)
        allowed = (hit > 0) | ((tbuf // MARGIN_BLOCK_SIZE)[:, :, None] == jnp.arange(bps, dtype=jnp.int32)[None, None, :])
        mask = jnp.broadcast_to(allowed[..., None], allowed.shape + (MARGIN_BLOCK_SIZE,)).reshape(scores.shape)
        expo = jnp.where(mask, jnp.exp(scores), jnp.float32(0.0))
        total = lax.optimization_barrier(jnp.sum(expo, axis=-1))
        is_target = jnp.arange(pps, dtype=jnp.int32)[None, None, :] == tbuf[:, :, None]
        target_score = lax.optimization_barrier(jnp.sum(jnp.where(is_target, scores, jnp.float32(0.0)), axis=-1))
        valid_mask = (index_buffer >= 0) & (index_buffer < routed_count)
        loss = jnp.where(valid_mask, jnp.log(total) - target_score, jnp.float32(0.0))
        coef = jnp.where(valid_mask, jnp.float32(64.0) / routed_count.astype(jnp.float32), jnp.float32(0.0))
        dscore = (coef[..., None] * (expo / total[..., None] - is_target.astype(jnp.float32))).astype(jnp.bfloat16)
        dquery = (jnp.einsum('suk,skd->sud', dscore.astype(jnp.float32), patch_s.astype(jnp.float32)) * scale).astype(jnp.bfloat16)
        dq_words = dquery[destination_slot, column_offset]
        loss_words = loss[destination_slot, column_offset]
        grad = grad + jnp.dot(feats.T, dq_words, preferred_element_type=jnp.float32)
        return (grad, loss_words)
    grad, losses = lax.scan(page, jnp.zeros((D, D), jnp.float32), (words, patches, routes, targets, counts, flags))
    return (losses, grad)
```

```python
import functools
import math

import jax
import jax.numpy as jnp
from jax import lax
from jax.experimental import pallas as pl
from jax.experimental.pallas import tpu as pltpu
from jax.sharding import PartitionSpec as P

MARGIN_BLOCK_SIZE = 64
VMEM_LIMIT = 48 * 1024 * 1024


def page_kernel(n_homes, n_proj, cap, first, scale, info, *refs):
    refs = list(refs)
    meta, fexp, patches = refs[:3]
    words = refs[3 : 3 + n_homes]
    gathered = refs[3 + n_homes : 3 + n_homes + n_proj]
    rest = refs[3 + n_homes + n_proj :]
    acc_in = None
    if not first:
        acc_in, rest = rest[0], rest[1:]
    acc, loss, proj, rows_x, rows_dq, sems = rest
    page = pl.program_id(0)
    me, my_dp, core = info[0], info[1], info[2]
    wdev = meta.shape[-1]
    pps = patches.shape[-2]
    nblk = fexp.shape[-2]
    n_cols, _, wcol = acc.shape
    half = proj.shape[-1]

    def proj_copies():
        copies = []
        for g, ref in enumerate(gathered):
            other_core, low = g // 2, g % 2
            for hi in range(ref.shape[0]):
                shard = jnp.bitwise_xor(my_dp, hi * 2 + low)
                rows = ref.shape[1]
                copies.append(
                    pltpu.make_async_copy(
                        ref.at[hi],
                        proj.at[
                            jnp.bitwise_xor(core, other_core),
                            pl.ds(pl.multiple_of(shard * rows, rows), rows),
                        ],
                        sems.at[len(copies)],
                    )
                )
        return copies

    @pl.when(page == 0)
    def _():
        for copy in proj_copies():
            copy.start()
        if first:
            acc[...] = jnp.zeros_like(acc)
        else:
            acc[...] = acc_in[...]

    m = (meta[0, 0] == me).astype(jnp.float32)
    before = lax.broadcasted_iota(jnp.int32, (wdev, wdev), 0) < lax.broadcasted_iota(
        jnp.int32, (wdev, wdev), 1
    )
    rank = jnp.dot(
        m.astype(jnp.bfloat16), before.astype(jnp.bfloat16), preferred_element_type=jnp.float32
    )
    rank = jnp.where(m > 0, rank, -1.0)
    slots = lax.broadcasted_iota(jnp.int32, (cap, wdev), 0).astype(jnp.float32)
    here = lax.broadcasted_iota(jnp.int32, (cap, wdev), 1)
    picks, t_rows, i_rows = [], [], []
    for r in range(n_homes):
        pick = (slots == rank[r : r + 1, :]).astype(jnp.float32)
        rows_x[pl.ds(r * cap, cap), :] = jnp.dot(
            pick.astype(jnp.bfloat16),
            words[r][...].reshape(wdev, -1),
            preferred_element_type=jnp.float32,
        ).astype(jnp.bfloat16)
        target = meta[0, 1][r : r + 1, :].astype(jnp.float32)
        place = (here + info[4 + r] * wdev + 1).astype(jnp.float32)
        t_rows.append(jnp.sum(pick * target, axis=1, keepdims=True))
        i_rows.append(jnp.sum(pick * place, axis=1, keepdims=True))
        picks.append(pick)
    t = jnp.concatenate(t_rows, axis=0).astype(jnp.int32)
    idx = jnp.concatenate(i_rows, axis=0).astype(jnp.int32) - 1
    n_rows = n_homes * cap

    @pl.when(page == 0)
    def _():
        for copy in proj_copies():
            copy.wait()

    x = rows_x[...]
    pat = patches[...].reshape(pps, -1)
    scores = jnp.zeros((n_rows, pps), jnp.float32)
    for h in range(2):
        q = jnp.dot(x, proj[h], preferred_element_type=jnp.float32).astype(jnp.bfloat16)
        scores = scores + lax.dot_general(
            q,
            pat[:, h * half : (h + 1) * half],
            (((1,), (1,)), ((), ())),
            preferred_element_type=jnp.float32,
        )
    scores = scores * scale
    blocks = lax.broadcasted_iota(jnp.int32, (n_rows, nblk), 1)
    word_block = (jnp.maximum(idx, 0) // MARGIN_BLOCK_SIZE == blocks).astype(jnp.bfloat16)
    hit = jnp.dot(word_block, fexp[0], preferred_element_type=jnp.float32)
    k = lax.broadcasted_iota(jnp.int32, (n_rows, pps), 1)
    allowed = (hit > 0.5) | (k // MARGIN_BLOCK_SIZE == t // MARGIN_BLOCK_SIZE)
    is_target = k == t
    top = jnp.max(jnp.where(allowed, scores, -jnp.inf), axis=1, keepdims=True)
    expo = jnp.where(allowed, jnp.exp(scores - top), 0.0)
    total = jnp.sum(expo, axis=1, keepdims=True)
    target_score = jnp.sum(jnp.where(is_target, scores, 0.0), axis=1, keepdims=True)
    count = info[4 + n_homes + page]
    valid = (idx >= 0) & (idx < count)
    row_loss = jnp.where(valid, top + jnp.log(total) - target_score, 0.0)
    coef = jnp.where(valid, 64.0 / count.astype(jnp.float32), 0.0)
    dscore = (coef * (expo * (1.0 / total) - is_target.astype(jnp.float32))).astype(jnp.bfloat16)
    for r in range(n_homes):
        loss[0, r : r + 1, :] = jnp.sum(
            picks[r] * row_loss[r * cap : (r + 1) * cap], axis=0, keepdims=True
        )
    rows_dq[...] = (
        jnp.dot(dscore, pat, preferred_element_type=jnp.float32) * scale
    ).astype(jnp.bfloat16)
    for j in range(n_cols):
        acc[j] += lax.dot_general(
            x,
            rows_dq[:, j * wcol : (j + 1) * wcol],
            (((0,), (0,)), ((), ())),
            preferred_element_type=jnp.float32,
        )


def run_pages(info, meta, fexp, patches, words, gathered, acc, cap, n_cols, first_page, n_pages):
    n_homes = len(words)
    wdev, width = words[0].shape[-2:]
    pps = patches.shape[1]
    nblk = fexp.shape[1]
    wcol = width // n_cols
    rows = n_homes * cap
    first = acc is None
    n_copies = sum(g.shape[0] for g in gathered)
    take = lambda p, info: (p + first_page, 0, 0)
    any_space = pl.BlockSpec(memory_space=pl.ANY)
    in_specs = [
        pl.BlockSpec((1,) + meta.shape[1:], lambda p, info: (p + first_page, 0, 0, 0)),
        pl.BlockSpec((1, nblk, pps), take),
        pl.BlockSpec((1, pps, width), take),
    ]
    for w in words:
        if w.shape[0] == 1:
            in_specs.append(pl.BlockSpec((1, wdev, width), lambda p, info: (0, 0, 0)))
        else:
            in_specs.append(pl.BlockSpec((1, wdev, width), take))
    in_specs += [any_space] * len(gathered)
    whole = pl.BlockSpec((n_cols, width, wcol), lambda p, info: (0, 0, 0))
    operands = [info, meta, fexp, patches, *words, *gathered]
    aliases = {}
    if not first:
        in_specs.append(whole)
        operands.append(acc)
        aliases = {len(operands) - 1: 0}
    flops = 2 * n_pages * rows * width * (2 * width + 2 * pps + wdev)
    bytes_accessed = n_pages * (n_homes * wdev + pps) * width * 2 + 2 * width * width + 8 * width * width
    return pl.pallas_call(
        functools.partial(
            page_kernel, n_homes, len(gathered), cap, first, 2.0 / math.sqrt(width)
        ),
        grid_spec=pltpu.PrefetchScalarGridSpec(
            num_scalar_prefetch=1,
            grid=(n_pages,),
            in_specs=in_specs,
            out_specs=[
                whole,
                pl.BlockSpec((1, n_homes, wdev), lambda p, info: (p, 0, 0)),
            ],
            scratch_shapes=[
                pltpu.VMEM((2, width, width // 2), jnp.bfloat16),
                pltpu.VMEM((rows, width), jnp.bfloat16),
                pltpu.VMEM((rows, width), jnp.bfloat16),
                pltpu.SemaphoreType.DMA((n_copies,)),
            ],
        ),
        out_shape=[
            jax.ShapeDtypeStruct((n_cols, width, wcol), jnp.float32),
            jax.ShapeDtypeStruct((n_pages, n_homes, wdev), jnp.float32),
        ],
        input_output_aliases=aliases,
        compiler_params=pltpu.CompilerParams(vmem_limit_bytes=VMEM_LIMIT),
        cost_estimate=pl.CostEstimate(
            flops=flops, bytes_accessed=bytes_accessed, transcendentals=n_pages * rows * pps
        ),
    )(*operands)


def exchange(x, axis, offset):
    n = lax.axis_size(axis)
    return lax.ppermute(x, axis, [(i, i ^ offset) for i in range(n)])


def local(words, patches, proj, routes, targets, counts, flags):
    pages, wdev, width = words.shape
    pps = patches.shape[1]
    n_seq = lax.axis_size("seq")
    n_dp = lax.axis_size("dp")
    me = lax.axis_index("seq")
    my_dp = lax.axis_index("dp")
    core = me % 2
    n_y = n_seq // 2
    cap = 2 * wdev // n_seq
    bps = pps // MARGIN_BLOCK_SIZE
    half = width // 2
    shard_rows = proj.shape[0]

    far = [[exchange(words[p : p + 1], "seq", 2 * k) for k in range(1, n_y)] for p in range(pages)]
    near = exchange(words, "seq", 1)

    mine = lax.dynamic_slice_in_dim(proj, core * half, half, 1)
    low0 = [mine] + [exchange(mine, "dp", 2 * k) for k in range(1, n_dp // 2)]
    low1 = [exchange(piece, "dp", 1) for piece in low0]
    low0, low1 = jnp.stack(low0), jnp.stack(low1)
    gathered = [low0, low1, exchange(low0, "seq", 1), exchange(low1, "seq", 1)]

    pair = jnp.stack([routes[:, :, 0], targets], axis=1)
    metas = jnp.stack([pair] + [exchange(pair, "seq", r) for r in range(1, n_seq)], axis=2)
    pad = lambda a: jnp.pad(a, ((0, 0), (0, 0), (0, -a.shape[2] % 8), (0, 0)), constant_values=-1)
    homes = jnp.bitwise_xor(me, jnp.arange(n_seq, dtype=jnp.int32))
    own = lax.dynamic_slice_in_dim(flags, me * bps, bps, 2)
    fexp = jnp.repeat(own, MARGIN_BLOCK_SIZE, axis=2).astype(jnp.bfloat16)
    base = jnp.stack([me, my_dp, core, jnp.zeros_like(me)]).astype(jnp.int32)

    info = jnp.concatenate([base, homes[:2], counts])
    acc, loss_near = run_pages(
        info, pad(metas[:, :, :2]), fexp, patches, [words, near], gathered, None, cap, n_seq, 0, pages
    )
    far_meta = pad(metas[:, :, 2:])
    losses = []
    for p in range(pages):
        blocks = []
        for block in far[p]:
            blocks += [block, exchange(block, "seq", 1)]
        info = jnp.concatenate([base, homes[2:], counts[p : p + 1]])
        acc, loss = run_pages(
            info, far_meta, fexp, patches, blocks, gathered, acc, cap, n_seq, p, 1
        )
        losses.append(loss)
    loss_far = jnp.concatenate(losses, axis=0)

    acc = acc.reshape(n_y, 2, width, width // n_seq)
    pick = lambda a, i, axis: lax.dynamic_index_in_dim(a, i, axis, keepdims=False)
    part = pick(acc, core, 1) + exchange(pick(acc, 1 - core, 1).astype(jnp.bfloat16), "seq", 1)
    y = me // 2
    total = pick(part, y, 0)
    for k in range(1, n_y):
        total = total + exchange(pick(part, jnp.bitwise_xor(y, k), 0).astype(jnp.bfloat16), "seq", 2 * k)
    total = total.reshape(n_dp, shard_rows, width // n_seq)
    grad = pick(total, my_dp, 0)
    for k in range(1, n_dp):
        grad = grad + exchange(pick(total, jnp.bitwise_xor(my_dp, k), 0).astype(jnp.bfloat16), "dp", k)

    word_loss = loss_near[:, 0] + exchange(loss_near[:, 1], "seq", 1)
    for r in range(2, n_seq):
        word_loss = word_loss + exchange(loss_far[:, r - 2], "seq", r)
    return (word_loss, grad)


def solution(mesh):
    in_specs = (
        P("dp", "seq", None),
        P("dp", "seq", None),
        P("dp", None),
        P("dp", "seq", None),
        P("dp", "seq"),
        P("dp"),
        P("dp", None, None),
    )
    out_specs = (P("dp", "seq"), P("dp", "seq"))
    return jax.shard_map(local, mesh=mesh, in_specs=in_specs, out_specs=out_specs, check_vma=False)
```

```python
import functools
import math

import jax
import jax.numpy as jnp
from jax import lax
from jax.experimental import pallas as pl
from jax.experimental.pallas import tpu as pltpu
from jax.sharding import PartitionSpec as P

MARGIN_BLOCK_SIZE = 64
VMEM_LIMIT = 40 * 1024 * 1024
ME, CORE, COUNTS = 0, 1, 2


def ranks(hits):
    n = hits.shape[1]
    before = lax.broadcasted_iota(jnp.int32, (n, n), 0) < lax.broadcasted_iota(jnp.int32, (n, n), 1)
    count = jnp.dot(
        hits.astype(jnp.bfloat16), before.astype(jnp.bfloat16), preferred_element_type=jnp.float32
    )
    return jnp.where(hits > 0, count, -1.0)


def dispatch_kernel(offsets, cap, info, routes, words, *outs):
    wdev = words.shape[1]
    route = jnp.broadcast_to(routes[0], (8, wdev))
    slots = lax.broadcasted_iota(jnp.int32, (cap, wdev), 0).astype(jnp.float32)
    row = lax.broadcasted_iota(jnp.int32, (8, wdev), 0)
    picks = []
    for first in range(0, len(offsets), 8):
        some = offsets[first : first + 8]
        to = jnp.full((8, wdev), -1, jnp.int32)
        for i, offset in enumerate(some):
            to = jnp.where(row == i, jnp.bitwise_xor(info[ME], offset), to)
        rank = ranks((route == to).astype(jnp.float32))
        picks += [(slots == rank[i : i + 1]).astype(jnp.bfloat16) for i in range(len(some))]
    rows = jnp.dot(
        jnp.concatenate(picks, axis=0), words[0], preferred_element_type=jnp.float32
    ).astype(jnp.bfloat16)
    for i, out in enumerate(outs):
        out[0] = rows[i * cap : (i + 1) * cap]


def dispatch(info, routes, words, offsets, cap, first_page, n_pages):
    _, wdev, width = words.shape
    n = len(offsets)
    take = lambda p, info: (p + first_page, 0, 0)
    return pl.pallas_call(
        functools.partial(dispatch_kernel, offsets, cap),
        grid_spec=pltpu.PrefetchScalarGridSpec(
            num_scalar_prefetch=1,
            grid=(n_pages,),
            in_specs=[pl.BlockSpec((1, 1, wdev), take), pl.BlockSpec((1, wdev, width), take)],
            out_specs=[pl.BlockSpec((1, cap, width), lambda p, info: (p, 0, 0))] * n,
        ),
        out_shape=[jax.ShapeDtypeStruct((n_pages, cap, width), jnp.bfloat16)] * n,
        compiler_params=pltpu.CompilerParams(vmem_limit_bytes=VMEM_LIMIT),
        cost_estimate=pl.CostEstimate(
            flops=0, bytes_accessed=0, transcendentals=0
        ),
    )(info, routes, words)


def page_kernel(offsets, n_proj, first_page, n_pages, has_acc, last, scale, info, *refs):
    n_homes = len(offsets)
    refs = list(refs)
    meta, flags, patches = refs[:3]
    words = refs[3 : 3 + n_homes]
    gathered = refs[3 + n_homes : 3 + n_homes + n_proj]
    rest = refs[3 + n_homes + n_proj :]
    acc_in = rest.pop(0) if has_acc else None
    outs, rest = (rest[:2], rest[2:]) if last else (rest[:1], rest[1:])
    loss, proj, x_t, dqs, sems = rest[:5]
    acc = rest[5] if has_acc else None
    page = pl.program_id(0)
    me, core = info[ME], info[CORE]
    wdev = meta.shape[-1]
    pps, width = patches.shape[-2:]
    nblk, all_blk = flags.shape[-2:]
    cap = words[0].shape[1]
    n_rows = n_homes * cap
    n_cols = meta.shape[0]
    wcol = width // n_cols
    half = width // 2
    bps = pps // MARGIN_BLOCK_SIZE

    def proj_copies():
        return [
            pltpu.make_async_copy(ref, proj.at[jnp.bitwise_xor(core, g)], sems.at[g])
            for g, ref in enumerate(gathered)
        ]

    acc_copy = lambda: pltpu.make_async_copy(acc_in, acc, sems.at[n_proj])

    @pl.when(page == 0)
    def _():
        for copy in proj_copies():
            copy.start()
        if has_acc:
            acc_copy().start()

    slots = lax.broadcasted_iota(jnp.int32, (cap, wdev), 0).astype(jnp.float32)
    here = lax.broadcasted_iota(jnp.int32, (cap, wdev), 1)
    row = lax.broadcasted_iota(jnp.int32, (8, wdev), 0)
    picks, t_rows, i_rows = [], [], []
    for first in range(0, n_homes, 8):
        some = offsets[first : first + 8]
        hits = jnp.zeros((8, wdev), jnp.float32)
        for i, offset in enumerate(some):
            route = meta[jnp.bitwise_xor(me, offset), page + first_page, 0:1, :]
            hits = jnp.where((row == i) & (route == me), 1.0, hits)
        rank = ranks(hits)
        for i, offset in enumerate(some):
            home = jnp.bitwise_xor(me, offset)
            pick = (slots == rank[i : i + 1]).astype(jnp.float32)
            target = meta[home, page + first_page, 1:2, :].astype(jnp.float32)
            place = (here + (home * wdev + 1)).astype(jnp.float32)
            t_rows.append(jnp.sum(pick * target, axis=1, keepdims=True))
            i_rows.append(jnp.sum(pick * place, axis=1, keepdims=True))
            picks.append(pick)
    t = jnp.concatenate(t_rows, axis=0).astype(jnp.int32)
    idx = jnp.concatenate(i_rows, axis=0).astype(jnp.int32) - 1

    x = jnp.concatenate([w[0] for w in words], axis=0)
    if x_t.shape[0] == n_pages:
        x_t[page] = x.T
    else:
        x_t[0, :, pl.ds(pl.multiple_of(page * n_rows, n_rows), n_rows)] = x.T

    blocks = lax.broadcasted_iota(jnp.int32, (n_rows, nblk), 1)
    word_block = (jnp.maximum(idx, 0) // MARGIN_BLOCK_SIZE == blocks).astype(jnp.bfloat16)
    margin = jnp.dot(
        word_block, flags[0].astype(jnp.bfloat16), preferred_element_type=jnp.float32
    ).astype(jnp.bfloat16)
    spread = (
        lax.broadcasted_iota(jnp.int32, (all_blk, pps), 0)
        == me * bps + lax.broadcasted_iota(jnp.int32, (all_blk, pps), 1) // MARGIN_BLOCK_SIZE
    ).astype(jnp.bfloat16)
    hit = jnp.dot(margin, spread, preferred_element_type=jnp.float32)
    k = lax.broadcasted_iota(jnp.int32, (n_rows, pps), 1)
    allowed = (hit > 0.5) | (k // MARGIN_BLOCK_SIZE == t // MARGIN_BLOCK_SIZE)
    is_target = k == t

    @pl.when(page == 0)
    def _():
        for copy in proj_copies():
            copy.wait()

    pat = patches[0]
    scores = jnp.zeros((n_rows, pps), jnp.float32)
    for h in range(2):
        q = jnp.dot(x, proj[h], preferred_element_type=jnp.float32).astype(jnp.bfloat16)
        scores = scores + lax.dot_general(
            q,
            pat[:, h * half : (h + 1) * half],
            (((1,), (1,)), ((), ())),
            preferred_element_type=jnp.float32,
        )
    scores = scores * scale
    top = jnp.max(jnp.where(allowed, scores, -jnp.inf), axis=1, keepdims=True)
    expo = jnp.where(allowed, jnp.exp(scores - top), 0.0)
    total = jnp.sum(expo, axis=1, keepdims=True)
    target_score = jnp.sum(jnp.where(is_target, scores, 0.0), axis=1, keepdims=True)
    count = info[COUNTS + first_page + page]
    valid = (idx >= 0) & (idx < count)
    row_loss = jnp.where(valid, top + jnp.log(total) - target_score, 0.0)
    coef = jnp.where(valid, 64.0 / count.astype(jnp.float32), 0.0)
    share = expo * (1.0 / total)
    dscore = (coef * jnp.where(is_target, share - 1.0, share)).astype(jnp.bfloat16)
    for r in range(n_homes):
        loss[0, r : r + 1, :] = jnp.sum(
            picks[r] * row_loss[r * cap : (r + 1) * cap], axis=0, keepdims=True
        )
    dqs[pl.ds(pl.multiple_of(page * n_rows, n_rows), n_rows), :] = (
        jnp.dot(dscore, pat, preferred_element_type=jnp.float32) * scale
    ).astype(jnp.bfloat16)

    @pl.when(page == n_pages - 1)
    def _():
        if has_acc:
            acc_copy().wait()

        def gradient(j):
            got = acc[j] if has_acc else 0.0
            depth = x_t.shape[2]
            for g in range(x_t.shape[0]):
                got += jnp.dot(
                    x_t[g],
                    dqs[g * depth : (g + 1) * depth, pl.ds(pl.multiple_of(j * wcol, wcol), wcol)],
                    preferred_element_type=jnp.float32,
                )
            return got

        def store(out, y, got):
            halves, _, lows, highs, cut, _ = out.shape
            for part in range(halves * lows * highs):
                high, low, h = part // (2 * lows), part // 2 % lows, part % 2
                out[h, y, low, high] = got[part * cut : (part + 1) * cut].astype(out.dtype)

        if last:
            keep, send = outs
            for y in range(n_cols // 2):
                store(send, y, gradient(2 * y + 1 - core))
            for y in range(n_cols // 2):
                store(keep, y, gradient(2 * y + core))
        else:
            for j in range(n_cols):
                outs[0][j] = gradient(j)


def run_pages(
    n_high, info, meta, flags, patches, words, offsets, gathered, acc, first_page, last
):
    n_pages, cap, width = words[0].shape
    n_seq, _, _, wdev = meta.shape
    pps = patches.shape[1]
    n_homes = len(offsets)
    wcol = width // n_seq
    n_rows = n_homes * cap
    has_acc = acc is not None
    take = lambda p, info: (p + first_page, 0, 0)
    in_specs = [
        pl.BlockSpec(meta.shape, lambda p, info: (0, 0, 0, 0)),
        pl.BlockSpec((1,) + flags.shape[1:], take),
        pl.BlockSpec((1, pps, width), take),
    ]
    in_specs += [pl.BlockSpec((1, cap, width), lambda p, info: (p, 0, 0))] * n_homes
    in_specs += [pl.BlockSpec(memory_space=pl.ANY)] * (len(gathered) + has_acc)
    operands = [info, meta, flags, patches, *words, *gathered] + ([acc] if has_acc else [])
    if last:
        form = (2, n_seq // 2, 2, n_high, width // (4 * n_high), wcol)
        out_shape = [jax.ShapeDtypeStruct(form, t) for t in (jnp.float32, jnp.bfloat16)]
    else:
        out_shape = [jax.ShapeDtypeStruct((n_seq, width, wcol), jnp.float32)]
    out_specs = [pl.BlockSpec(o.shape, lambda p, info, o=o: (0,) * len(o.shape)) for o in out_shape]
    groups = 1 if n_rows % 128 == 0 else n_pages
    scratch = [
        pltpu.VMEM((2, width, width // 2), jnp.bfloat16),
        pltpu.VMEM((groups, width, n_pages * n_rows // groups), jnp.bfloat16),
        pltpu.VMEM((n_pages * n_rows, width), jnp.bfloat16),
        pltpu.SemaphoreType.DMA((len(gathered) + 1,)),
    ]
    if has_acc:
        scratch.append(pltpu.VMEM((n_seq, width, wcol), jnp.float32))
    return pl.pallas_call(
        functools.partial(
            page_kernel,
            offsets,
            len(gathered),
            first_page,
            n_pages,
            has_acc,
            last,
            2.0 / math.sqrt(width),
        ),
        grid_spec=pltpu.PrefetchScalarGridSpec(
            num_scalar_prefetch=1,
            grid=(n_pages,),
            in_specs=in_specs,
            out_specs=out_specs
            + [pl.BlockSpec((1, n_homes, wdev), lambda p, info: (p, 0, 0))],
            scratch_shapes=scratch,
        ),
        out_shape=out_shape + [jax.ShapeDtypeStruct((n_pages, n_homes, wdev), jnp.float32)],
        compiler_params=pltpu.CompilerParams(vmem_limit_bytes=VMEM_LIMIT),
        cost_estimate=pl.CostEstimate(
            flops=0, bytes_accessed=0, transcendentals=0
        ),
    )(*operands)


def exchange(x, axis, offset):
    n = lax.axis_size(axis)
    return lax.ppermute(x, axis, [(i, i ^ offset) for i in range(n)])


def pick(x, i, axis=0):
    return lax.dynamic_index_in_dim(x, i, axis, keepdims=False)


def pick_sum(terms, i, axis=0):
    return sum(pick(t, i, axis).astype(jnp.float32) for t in terms)


def local(words, patches, proj, routes, targets, counts, flags):
    pages, wdev, width = words.shape
    n_seq = lax.axis_size("seq")
    n_dp = lax.axis_size("dp")
    me = lax.axis_index("seq")
    my_dp = lax.axis_index("dp")
    core, y, low, high = me % 2, me // 2, my_dp % 2, my_dp // 2
    n_y, n_high = n_seq // 2, n_dp // 2
    cap = 2 * wdev // n_seq
    half = width // 2
    shard_rows = proj.shape[0]
    wcol = width // n_seq
    near, far = (0, 1), tuple(range(2, n_seq))

    info = jnp.concatenate([jnp.stack([me, core]).astype(jnp.int32), counts])
    routes = routes.reshape(pages, 1, wdev)

    chunks = [(0, pages // 2)] + [(p, 1) for p in range(pages // 2, pages)]
    held = info
    arrived = []
    for first_page, n_pages in chunks:
        rows = dispatch(held, routes, words, far, cap, first_page, n_pages)
        held, rows = lax.optimization_barrier((held, rows))
        arrived.append([exchange(x, "seq", r) for x, r in zip(rows, far)])
    stay, across = dispatch(held, routes, words, near, cap, 0, pages)
    across = exchange(across, "seq", 1)

    pair = jnp.concatenate([routes, targets.reshape(pages, 1, wdev)], axis=1)
    meta = lax.all_to_all(jnp.broadcast_to(pair, (n_seq,) + pair.shape), "seq", 0, 0, tiled=True)

    mine = lax.dynamic_slice_in_dim(proj, core * half, half, 1)
    mine = lax.all_gather(mine, "dp", axis=0, tiled=True)
    mine, meta, arrived[0] = lax.optimization_barrier((mine, meta, arrived[0]))
    gathered = [mine, exchange(mine, "seq", 1)]

    run = functools.partial(run_pages, n_high, info, meta, flags, patches)
    acc, loss = run([stay, across], near, gathered, None, 0, False)
    word_loss = [loss[:, 0], exchange(loss[:, 1], "seq", 1)]
    losses = []
    for (first_page, n_pages), rows in zip(chunks, arrived):
        last = first_page + n_pages == pages
        *out, loss = run(rows, far, gathered, acc, first_page, last)
        acc = out[0]
        losses.append(loss)
    keep, send = out
    losses = jnp.concatenate(losses, axis=0)

    terms = [keep, exchange(send, "seq", 1)]

    def over_y(terms):
        total = pick_sum(terms, y)
        for k in range(1, n_y):
            other = pick_sum(terms, jnp.bitwise_xor(y, k)).astype(jnp.bfloat16)
            total = total + exchange(other, "seq", 2 * k)
        return total

    def over_low(terms, axis):
        other = pick_sum(terms, 1 - low, axis).astype(jnp.bfloat16)
        return pick_sum(terms, low, axis) + exchange(other, "dp", 1)

    one = over_low([over_y([t[0] for t in terms])], 0)
    two = over_y([over_low([t[1] for t in terms], 1)])
    grad = jnp.concatenate([pick(one, high), pick(two, high)], axis=0)
    for k in range(1, n_high):
        to = jnp.bitwise_xor(high, k)
        other = jnp.concatenate([pick(one, to), pick(two, to)], axis=0).astype(jnp.bfloat16)
        grad = grad + exchange(other, "dp", 2 * k)

    for i, r in enumerate(far):
        word_loss.append(exchange(losses[:, i], "seq", r))
    return (sum(word_loss), grad)


def solution(mesh):
    in_specs = (
        P("dp", "seq", None),
        P("dp", "seq", None),
        P("dp", None),
        P("dp", "seq", None),
        P("dp", "seq"),
        P("dp"),
        P("dp", None, None),
    )
    out_specs = (P("dp", "seq"), P("dp", "seq"))
    return jax.shard_map(local, mesh=mesh, in_specs=in_specs, out_specs=out_specs, check_vma=False)
```

```python
import functools
import math

import jax
import jax.numpy as jnp
from jax import lax
from jax.experimental import pallas as pl
from jax.experimental.pallas import tpu as pltpu
from jax.sharding import PartitionSpec as P

MARGIN_BLOCK_SIZE = 64
VMEM_LIMIT = 28 * 1024 * 1024
ME, CORE, DP, COUNTS = 0, 1, 2, 3
TARGET, COEF = 0, 1
FREE = pl.CostEstimate(flops=0, bytes_accessed=0, transcendentals=0)
F32, BF16 = jnp.float32, jnp.bfloat16


def dot(a, b, contract=((1,), (0,))):
    return lax.dot_general(a, b, (contract, ((), ())), preferred_element_type=F32)


def iota(shape, axis):
    return lax.broadcasted_iota(jnp.int32, shape, axis)


def ranks(hits):
    n = hits.shape[1]
    before = (iota((n, n), 0) < iota((n, n), 1)).astype(BF16)
    return jnp.where(hits > 0, dot(hits.astype(BF16), before), -1.0)


def call(kernel, n_pages, in_specs, out_specs, out_shape, operands, scratch=(), cost=FREE):
    return pl.pallas_call(
        kernel,
        grid_spec=pltpu.PrefetchScalarGridSpec(
            num_scalar_prefetch=1,
            grid=(n_pages,),
            in_specs=in_specs,
            out_specs=out_specs,
            scratch_shapes=scratch,
        ),
        out_shape=out_shape,
        compiler_params=pltpu.CompilerParams(vmem_limit_bytes=VMEM_LIMIT),
        cost_estimate=cost,
    )(*operands)


def page_of(array, first_page=0):
    rest = array.shape[1:]
    return pl.BlockSpec((1,) + rest, lambda p, info: (p + first_page,) + (0,) * len(rest))


def all_of(array):
    return pl.BlockSpec(array.shape, lambda p, info: (0,) * len(array.shape))


def dispatch_kernel(offsets, cap, info, routes, words, *outs):
    wdev = words.shape[1]
    route = jnp.broadcast_to(routes[0], (8, wdev))
    slots = iota((cap, wdev), 0).astype(F32)
    row = iota((8, wdev), 0)
    to = jnp.full((8, wdev), -1, jnp.int32)
    for i, offset in enumerate(offsets):
        to = jnp.where(row == i, jnp.bitwise_xor(info[ME], offset), to)
    rank = ranks((route == to).astype(F32))
    picks = [(slots == rank[i : i + 1]).astype(BF16) for i in range(len(offsets))]
    rows = dot(jnp.concatenate(picks, axis=0), words[0]).astype(BF16)
    n = len(offsets) // len(outs)
    for i in range(len(offsets)):
        outs[i // n][i % n, 0] = rows[i * cap : (i + 1) * cap]


def dispatch(info, routes, words, offsets, cap, first_page, n_pages, together=1):
    width = words.shape[2]
    n = len(offsets) // together
    out = jax.ShapeDtypeStruct((together, n_pages, cap, width), BF16)
    spec = pl.BlockSpec((together, 1, cap, width), lambda p, info: (0, p, 0, 0))
    return call(
        functools.partial(dispatch_kernel, offsets, cap),
        n_pages,
        [page_of(routes, first_page), page_of(words, first_page)],
        [spec] * n,
        [out] * n,
        (info, routes, words),
    )


def table_kernel(offsets, cap, info, meta, flags, bias, table, rank_out):
    page = pl.program_id(0)
    me = info[ME]
    wdev = meta.shape[-1]
    nblk, all_blk = flags.shape[1:]
    n_rows, pps = bias.shape[1:]
    slots = iota((cap, wdev), 0).astype(F32)
    row = iota((8, wdev), 0)
    hits = jnp.zeros((8, wdev), F32)
    for i in range(len(offsets)):
        hits = jnp.where((row == i) & (meta[i, 0, 0:1, :] == me), 1.0, hits)
    rank = ranks(hits)
    rank_out[0] = rank
    t, idx = [], []
    for i, offset in enumerate(offsets):
        pick = (slots == rank[i : i + 1]).astype(F32)
        target = meta[i, 0, 1:2, :].astype(F32)
        place = iota((cap, wdev), 1) + (jnp.bitwise_xor(me, offset) * wdev + 1)
        t.append(jnp.sum(pick * target, axis=1, keepdims=True))
        idx.append(jnp.sum(pick * place.astype(F32), axis=1, keepdims=True))
    t = jnp.concatenate(t, axis=0).astype(jnp.int32)
    idx = jnp.concatenate(idx, axis=0).astype(jnp.int32) - 1
    word_block = (jnp.maximum(idx, 0) // MARGIN_BLOCK_SIZE == iota((n_rows, nblk), 1)).astype(BF16)
    margin = dot(word_block, flags[0].astype(BF16)).astype(BF16)
    first = me * (pps // MARGIN_BLOCK_SIZE)
    block = iota((all_blk, pps), 1) // MARGIN_BLOCK_SIZE
    hit = dot(margin, (iota((all_blk, pps), 0) == first + block).astype(BF16))
    own = iota((n_rows, pps), 1) // MARGIN_BLOCK_SIZE == t // MARGIN_BLOCK_SIZE
    bias[0] = jnp.where((hit > 0.5) | own, 0.0, -jnp.inf).astype(BF16)
    count = info[COUNTS + page]
    valid = (idx >= 0) & (idx < count)
    coef = jnp.where(valid, 64.0 / count.astype(F32), 0.0)
    lane = iota((n_rows, 128), 1)
    table[0] = jnp.where(lane == TARGET, t.astype(F32), jnp.where(lane == COEF, coef, 0.0))


def tables(info, meta, flags, offsets, cap, pps):
    n_homes, pages, _, wdev = meta.shape
    out = [
        jax.ShapeDtypeStruct((pages, n_homes * cap, pps), BF16),
        jax.ShapeDtypeStruct((pages, n_homes * cap, 128), F32),
        jax.ShapeDtypeStruct((pages, 8, wdev), F32),
    ]
    return call(
        functools.partial(table_kernel, offsets, cap),
        pages,
        [
            pl.BlockSpec((n_homes, 1, 2, wdev), lambda p, info: (0, p, 0, 0)),
            page_of(flags),
        ],
        [page_of(o) for o in out],
        out,
        (info, meta, flags),
    )


def weights_kernel(offsets, info, patches, *refs):
    *gathered, out, proj, sems = refs
    half = proj.shape[2]

    def copies():
        for g, ref in enumerate(gathered):
            rows = ref.shape[1]
            core = g // len(offsets)
            for i, offset in enumerate(offsets[g % len(offsets)]):
                shard = jnp.bitwise_xor(info[DP], offset)
                to = proj.at[
                    jnp.bitwise_xor(info[CORE], core),
                    pl.ds(pl.multiple_of(shard * rows, rows), rows),
                ]
                yield ref.at[i], to

    @pl.when(pl.program_id(0) == 0)
    def _():
        started = [
            pltpu.make_async_copy(a, b, sems.at[i]) for i, (a, b) in enumerate(copies())
        ]
        for copy in started:
            copy.start()
        for copy in started:
            copy.wait()

    pat = patches[0]
    out[0] = sum(
        dot(proj[h], pat[:, h * half : (h + 1) * half], ((1,), (1,))) for h in range(2)
    ).astype(BF16)


def weights(info, patches, gathered, offsets):
    pages, pps, width = patches.shape
    out = jax.ShapeDtypeStruct((pages, width, pps), BF16)
    return call(
        functools.partial(weights_kernel, offsets),
        pages,
        [page_of(patches)] + [pl.BlockSpec(memory_space=pl.ANY)] * len(gathered),
        page_of(out),
        out,
        (info, patches, *gathered),
        [
            pltpu.VMEM((2, width, width // 2), BF16),
            pltpu.SemaphoreType.DMA((sum(g.shape[0] for g in gathered),)),
        ],
    )


def page_kernel(n_homes, n_pages, has_acc, last, info, bias, table, rank, weight, patches, *refs):
    refs = list(refs)
    words, rest = refs[:n_homes], refs[n_homes:]
    acc_in = rest.pop(0) if has_acc else None
    n_outs = 4 if last else 1
    outs, (loss, x_t, dqs, *rest) = rest[:n_outs], rest[n_outs:]
    page = pl.program_id(0)
    pps, width = patches.shape[1:]
    cap = words[0].shape[2]
    n_rows = n_homes * cap
    wcol = outs[0].shape[-1]
    n_cols = width // wcol
    scale = 2.0 / math.sqrt(width)
    if has_acc:
        acc, sem = rest
        acc_copy = pltpu.make_async_copy(acc_in, acc, sem)

        @pl.when(page == 0)
        def _():
            acc_copy.start()

    x = jnp.concatenate([w[0, 0] for w in words], axis=0)
    if x_t.shape[0] == n_pages:
        x_t[page] = x.T
    else:
        x_t[0, :, pl.ds(pl.multiple_of(page * n_rows, n_rows), n_rows)] = x.T
    pat = patches[0]
    scores = dot(x, weight[0]) * scale
    is_target = iota((n_rows, pps), 1) == table[0, :, TARGET : TARGET + 1].astype(jnp.int32)
    coef = table[0, :, COEF : COEF + 1]
    masked = scores + bias[0].astype(F32)
    top = jnp.max(masked, axis=1, keepdims=True)
    expo = jnp.exp(masked - top)
    total = jnp.sum(expo, axis=1, keepdims=True)
    target_score = jnp.sum(jnp.where(is_target, scores, 0.0), axis=1, keepdims=True)
    row_loss = jnp.where(coef > 0, top + jnp.log(total) - target_score, 0.0)
    share = expo * (1.0 / total)
    dscore = (coef * jnp.where(is_target, share - 1.0, share)).astype(BF16)
    dqs[pl.ds(pl.multiple_of(page * n_rows, n_rows), n_rows), :] = (
        dot(dscore, pat) * scale
    ).astype(BF16)
    slots = iota((cap, rank.shape[2]), 0).astype(F32)
    for r in range(n_homes):
        picked = jnp.where(slots == rank[0, r : r + 1, :], row_loss[r * cap : (r + 1) * cap], 0.0)
        loss[0, r : r + 1, :] = jnp.sum(picked, axis=0, keepdims=True)

    @pl.when(page == n_pages - 1)
    def _():
        if has_acc:
            acc_copy.wait()

        def gradient(j):
            got = acc[j] if has_acc else 0.0
            depth = x_t.shape[2]
            for g in range(x_t.shape[0]):
                some = pl.ds(pl.multiple_of(j * wcol, wcol), wcol)
                got += dot(x_t[g], dqs[g * depth : (g + 1) * depth, some])
            return got

        def store(halves, y, got):
            _, lows, highs, cut, _ = halves[0].shape
            for part in range(2 * lows * highs):
                rows = got[part * cut : (part + 1) * cut]
                out = halves[part % 2]
                out[y, part // 2 % lows, part // (2 * lows)] = rows.astype(out.dtype)

        if last:
            for y in range(n_cols // 2):
                store(outs[2:], y, gradient(2 * y + 1 - info[CORE]))
            for y in range(n_cols // 2):
                store(outs[:2], y, gradient(2 * y + info[CORE]))
        else:
            for j in range(n_cols):
                outs[0][j] = gradient(j)


def run_pages(n_seq, n_high, info, weight, patches, table, words, acc, first_page, last):
    _, n_pages, cap, width = words[0].shape
    n_homes = len(words)
    n_rows = n_homes * cap
    wdev = table[2].shape[2]
    wcol = width // n_seq
    has_acc = acc is not None
    if last:
        form = (n_seq // 2, 2, n_high, width // (4 * n_high), wcol)
        out = [jax.ShapeDtypeStruct(form, t) for t in (F32, F32, BF16, BF16)]
    else:
        out = [jax.ShapeDtypeStruct((n_seq, width, wcol), F32)]
    loss = jax.ShapeDtypeStruct((n_pages, n_homes, wdev), F32)
    groups = 1 if n_rows % 128 == 0 else n_pages
    scratch = [
        pltpu.VMEM((groups, width, n_pages * n_rows // groups), BF16),
        pltpu.VMEM((n_pages * n_rows, width), BF16),
    ]
    if has_acc:
        scratch += [pltpu.VMEM((n_seq, width, wcol), F32), pltpu.SemaphoreType.DMA(())]
    return call(
        functools.partial(page_kernel, n_homes, n_pages, has_acc, last),
        n_pages,
        [page_of(a, first_page) for a in (*table, weight, patches)]
        + [pl.BlockSpec((1, 1, cap, width), lambda p, info: (0, p, 0, 0))] * n_homes
        + [pl.BlockSpec(memory_space=pl.ANY)] * has_acc,
        [all_of(o) for o in out] + [page_of(loss)],
        out + [loss],
        (info, *table, weight, patches, *words) + ((acc,) if has_acc else ()),
        scratch,
    )


def exchange(x, axis, offset):
    n = lax.axis_size(axis)
    return lax.ppermute(x, axis, [(i, i ^ offset) for i in range(n)])


def pick(x, i, axis=0):
    return lax.dynamic_index_in_dim(x, i, axis, keepdims=False)


def pick_sum(terms, i, axis=0):
    return sum(pick(t, i, axis).astype(F32) for t in terms)


def local(words, patches, proj, routes, targets, counts, flags):
    pages, wdev, width = words.shape
    pps = patches.shape[1]
    n_seq = lax.axis_size("seq")
    n_dp = lax.axis_size("dp")
    me = lax.axis_index("seq")
    my_dp = lax.axis_index("dp")
    core, y, low, high = me % 2, me // 2, my_dp % 2, my_dp // 2
    n_y, n_high = n_seq // 2, n_dp // 2
    cap = 2 * wdev // n_seq
    half = width // 2
    near, far = (0, 1), tuple(range(2, n_seq))

    info = jnp.concatenate([jnp.stack([me, core, my_dp]).astype(jnp.int32), counts])
    routes = routes.reshape(pages, 1, wdev)

    cut = pages - 1
    both = dispatch(info, routes, words, far, cap, 0, cut, 2)
    held, proj, both = lax.optimization_barrier((info, proj, both))
    rest = dispatch(held, routes, words, far, cap, cut, pages - cut)
    stay, across = dispatch(held, routes, words, near, cap, 0, pages)
    both = [exchange(rows, "seq", 2 * (k + 1)) for k, rows in enumerate(both)]

    pair = jnp.concatenate([routes, targets.reshape(pages, 1, wdev)], axis=1)
    meta_near = jnp.stack([pair, exchange(pair, "seq", 1)])
    table_near = tables(info, meta_near, flags, near, cap, pps)
    meta_far = jnp.concatenate([exchange(meta_near, "seq", 2 * k) for k in range(1, n_y)], axis=0)

    piece, bit = lax.dynamic_slice_in_dim(proj, core * half, half, 1)[None], 1
    pieces = [(piece, 0)]
    while bit < n_high:
        other = exchange(piece, "dp", 2 * bit)
        pieces = [(piece, 0), (other, bit)]
        bit *= 2
        if bit < n_high:
            piece = jnp.concatenate([piece, other], axis=0)
    gathered, offsets = [], []
    for piece, start in pieces:
        gathered += [piece, exchange(piece, "dp", 1)]
        offsets += [[2 * (start + i) + low for i in range(piece.shape[0])] for low in range(2)]
    gathered, rest, across, table_near = lax.optimization_barrier(
        (gathered, rest, across, table_near)
    )
    gathered += [exchange(piece, "seq", 1) for piece in gathered]
    rest = [exchange(rows, "seq", r) for rows, r in zip(rest, far)]
    across = exchange(across, "seq", 1)

    weight = weights(info, patches, gathered, offsets)
    both, weight, meta_far = lax.optimization_barrier((both, weight, meta_far))
    table_far = tables(info, meta_far, flags, far, cap, pps)
    first = [x for rows in both for x in (rows, exchange(rows[1:], "seq", 1))]
    run = functools.partial(run_pages, n_seq, n_high, info, weight, patches)
    acc, loss = run(table_near, [stay, across], None, 0, False)
    word_loss = [loss[:, 0], exchange(loss[:, 1], "seq", 1)]
    acc, loss_a = run(table_far, first, acc, 0, False)
    *out, loss_b = run(table_far, rest, acc, cut, True)
    losses = jnp.concatenate([loss_a, loss_b], axis=0)

    terms = [[out[h], exchange(out[2 + h], "seq", 1)] for h in range(2)]

    def over_y(terms):
        total = pick_sum(terms, y)
        for k in range(1, n_y):
            other = pick_sum(terms, jnp.bitwise_xor(y, k)).astype(BF16)
            total = total + exchange(other, "seq", 2 * k)
        return total

    def over_low(terms, axis):
        other = pick_sum(terms, 1 - low, axis).astype(BF16)
        return pick_sum(terms, low, axis) + exchange(other, "dp", 1)

    one = over_low([over_y(terms[0])], 0)
    two = over_y([over_low(terms[1], 1)])
    grad = jnp.concatenate([pick(one, high), pick(two, high)], axis=0)
    for k in range(1, n_high):
        to = jnp.bitwise_xor(high, k)
        other = jnp.concatenate([pick(one, to), pick(two, to)], axis=0).astype(BF16)
        grad = grad + exchange(other, "dp", 2 * k)

    for i, r in enumerate(far):
        word_loss.append(exchange(losses[:, i], "seq", r))
    return (sum(word_loss), grad)


def solution(mesh):
    in_specs = (
        P("dp", "seq", None),
        P("dp", "seq", None),
        P("dp", None),
        P("dp", "seq", None),
        P("dp", "seq"),
        P("dp"),
        P("dp", None, None),
    )
    out_specs = (P("dp", "seq"), P("dp", "seq"))
    return jax.shard_map(local, mesh=mesh, in_specs=in_specs, out_specs=out_specs, check_vma=False)
```

```python
import functools
import math

import jax
import jax.numpy as jnp
from jax import lax
from jax.experimental import pallas as pl
from jax.experimental.pallas import tpu as pltpu
from jax.sharding import PartitionSpec as P

MARGIN_BLOCK_SIZE = 64
VMEM_LIMIT = 16 * 1024 * 1024
ME, CORE, DP, COUNTS = 0, 1, 2, 3
TARGET, COEF = 0, 1
F32, BF16 = jnp.float32, jnp.bfloat16


def dot(a, b, contract=((1,), (0,))):
    return lax.dot_general(a, b, (contract, ((), ())), preferred_element_type=F32)


def iota(shape, axis):
    return lax.broadcasted_iota(jnp.int32, shape, axis)


def ranks(hits):
    n = hits.shape[1]
    before = (iota((n, n), 0) < iota((n, n), 1)).astype(BF16)
    return jnp.where(hits > 0, dot(hits.astype(BF16), before), -1.0)


def call(kernel, n_pages, in_specs, out_specs, out_shape, operands, scratch=(), aliases={}, flops=0):
    return pl.pallas_call(
        kernel,
        grid_spec=pltpu.PrefetchScalarGridSpec(
            num_scalar_prefetch=1,
            grid=(n_pages,),
            in_specs=in_specs,
            out_specs=out_specs,
            scratch_shapes=scratch,
        ),
        out_shape=out_shape,
        compiler_params=pltpu.CompilerParams(vmem_limit_bytes=VMEM_LIMIT),
        cost_estimate=pl.CostEstimate(flops=flops, bytes_accessed=0, transcendentals=0),
        input_output_aliases=aliases,
    )(*operands)


def page_of(array, first_page=0):
    rest = array.shape[1:]
    return pl.BlockSpec((1,) + rest, lambda p, info: (p + first_page,) + (0,) * len(rest))


def all_of(array):
    return pl.BlockSpec(array.shape, lambda p, info: (0,) * len(array.shape))


def dispatch_kernel(offsets, cap, info, routes, words, *outs):
    wdev = words.shape[1]
    route = jnp.broadcast_to(routes[0], (8, wdev))
    slots = iota((cap, wdev), 0).astype(F32)
    row = iota((8, wdev), 0)
    to = jnp.full((8, wdev), -1, jnp.int32)
    for i, offset in enumerate(offsets):
        to = jnp.where(row == i, jnp.bitwise_xor(info[ME], offset), to)
    rank = ranks((route == to).astype(F32))
    picks = [(slots == rank[i : i + 1]).astype(BF16) for i in range(len(offsets))]
    rows = dot(jnp.concatenate(picks, axis=0), words[0]).astype(BF16)
    n = len(offsets) // len(outs)
    for i in range(len(offsets)):
        outs[i // n][i % n, 0] = rows[i * cap : (i + 1) * cap]


def dispatch(info, routes, words, offsets, cap, first_page, n_pages, together=1):
    width = words.shape[2]
    n = len(offsets) // together
    out = jax.ShapeDtypeStruct((together, n_pages, cap, width), BF16)
    spec = pl.BlockSpec((together, 1, cap, width), lambda p, info: (0, p, 0, 0))
    return call(
        functools.partial(dispatch_kernel, offsets, cap),
        n_pages,
        [page_of(routes, first_page), page_of(words, first_page)],
        [spec] * n,
        [out] * n,
        (info, routes, words),
    )


def table_kernel(offsets, cap, info, meta, flags, bias, table, rank_out):
    page = pl.program_id(0)
    me = info[ME]
    wdev = meta.shape[-1]
    nblk, all_blk = flags.shape[1:]
    n_rows, pps = bias.shape[1:]
    slots = iota((cap, wdev), 0).astype(F32)
    row = iota((8, wdev), 0)
    hits = jnp.zeros((8, wdev), F32)
    for i in range(len(offsets)):
        hits = jnp.where((row == i) & (meta[i, 0, 0:1, :] == me), 1.0, hits)
    rank = ranks(hits)
    rank_out[0] = rank
    t, idx = [], []
    for i, offset in enumerate(offsets):
        pick = (slots == rank[i : i + 1]).astype(F32)
        target = meta[i, 0, 1:2, :].astype(F32)
        place = iota((cap, wdev), 1) + (jnp.bitwise_xor(me, offset) * wdev + 1)
        t.append(jnp.sum(pick * target, axis=1, keepdims=True))
        idx.append(jnp.sum(pick * place.astype(F32), axis=1, keepdims=True))
    t = jnp.concatenate(t, axis=0).astype(jnp.int32)
    idx = jnp.concatenate(idx, axis=0).astype(jnp.int32) - 1
    word_block = (jnp.maximum(idx, 0) // MARGIN_BLOCK_SIZE == iota((n_rows, nblk), 1)).astype(BF16)
    margin = dot(word_block, flags[0].astype(BF16)).astype(BF16)
    first = me * (pps // MARGIN_BLOCK_SIZE)
    block = iota((all_blk, pps), 1) // MARGIN_BLOCK_SIZE
    hit = dot(margin, (iota((all_blk, pps), 0) == first + block).astype(BF16))
    own = iota((n_rows, pps), 1) // MARGIN_BLOCK_SIZE == t // MARGIN_BLOCK_SIZE
    bias[0] = jnp.where((hit > 0.5) | own, 0.0, -jnp.inf).astype(BF16)
    count = info[COUNTS + page]
    valid = (idx >= 0) & (idx < count)
    coef = jnp.where(valid, 64.0 / count.astype(F32), 0.0)
    lane = iota((n_rows, 128), 1)
    table[0] = jnp.where(lane == TARGET, t.astype(F32), jnp.where(lane == COEF, coef, 0.0))


def tables(info, meta, flags, offsets, cap, pps):
    n_homes, pages, _, wdev = meta.shape
    out = [
        jax.ShapeDtypeStruct((pages, n_homes * cap, pps), BF16),
        jax.ShapeDtypeStruct((pages, n_homes * cap, 128), F32),
        jax.ShapeDtypeStruct((pages, 8, wdev), F32),
    ]
    return call(
        functools.partial(table_kernel, offsets, cap),
        pages,
        [
            pl.BlockSpec((n_homes, 1, 2, wdev), lambda p, info: (0, p, 0, 0)),
            page_of(flags),
        ],
        [page_of(o) for o in out],
        out,
        (info, meta, flags),
    )


def weights_kernel(offsets, info, patches, *refs):
    *gathered, out, proj, sems = refs
    half = proj.shape[1] // 2

    def copies():
        for g, ref in enumerate(gathered):
            rows = ref.shape[1]
            core = g // len(offsets)
            for i, offset in enumerate(offsets[g % len(offsets)]):
                shard = jnp.bitwise_xor(info[DP], offset)
                first = jnp.bitwise_xor(info[CORE], core) * half
                to = proj.at[
                    pl.ds(pl.multiple_of(shard * rows, rows), rows),
                    pl.ds(pl.multiple_of(first, half), half),
                ]
                yield ref.at[i], to

    @pl.when(pl.program_id(0) == 0)
    def _():
        started = [
            pltpu.make_async_copy(a, b, sems.at[i]) for i, (a, b) in enumerate(copies())
        ]
        for copy in started:
            copy.start()
        for copy in started:
            copy.wait()

    out[0] = dot(proj[...], patches[0], ((1,), (1,))).astype(BF16)


def weights(info, patches, gathered, offsets):
    pages, pps, width = patches.shape
    out = jax.ShapeDtypeStruct((pages, width, pps), BF16)
    return call(
        functools.partial(weights_kernel, offsets),
        pages,
        [page_of(patches)] + [pl.BlockSpec(memory_space=pl.ANY)] * len(gathered),
        page_of(out),
        out,
        (info, patches, *gathered),
        [
            pltpu.VMEM((width, width), BF16),
            pltpu.SemaphoreType.DMA((sum(g.shape[0] for g in gathered),)),
        ],
    )


def page_kernel(n_homes, cut, info, bias, table, rank, weight, patches, *refs):
    words, (loss, x_t, dq) = refs[:n_homes], refs[-3:]
    pps, width = patches.shape[1:]
    cap = words[0].shape[2]
    n_rows = n_homes * cap
    scale = 2.0 / math.sqrt(width)
    x = jnp.concatenate([w[0, 0] for w in words], axis=0)
    scores = dot(x, weight[0]) * scale
    is_target = iota((n_rows, pps), 1) == table[0, :, TARGET : TARGET + 1].astype(jnp.int32)
    coef = table[0, :, COEF : COEF + 1]
    masked = scores + bias[0].astype(F32)
    top = jnp.max(masked, axis=1, keepdims=True)
    expo = jnp.exp(masked - top)
    total = jnp.sum(expo, axis=1, keepdims=True)
    target_score = jnp.sum(jnp.where(is_target, scores, 0.0), axis=1, keepdims=True)
    row_loss = jnp.where(coef > 0, top + jnp.log(total) - target_score, 0.0)
    share = expo * (1.0 / total)
    dscore = (coef * jnp.where(is_target, share - 1.0, share)).astype(BF16)
    dq[0] = (dot(dscore, patches[0]) * scale).astype(BF16)
    slots = iota((cap, rank.shape[2]), 0).astype(F32)
    for r in range(n_homes):
        picked = jnp.where(slots == rank[0, r : r + 1, :], row_loss[r * cap : (r + 1) * cap], 0.0)
        loss[0, r : r + 1, :] = jnp.sum(picked, axis=0, keepdims=True)
    t = x.T
    for part in range(width // cut):
        x_t[0, part % 2, part // 2 * cut : (part // 2 + 1) * cut] = t[part * cut : (part + 1) * cut]


def run_pages(cut, info, weight, patches, table, words, first_page, kept=None):
    _, n_pages, cap, width = words[0][0].shape
    pages, wdev = patches.shape[0], table[2].shape[2]
    n_homes = len(words)
    n_rows = n_homes * cap
    out = [
        jax.ShapeDtypeStruct((n_pages, n_homes, wdev), F32),
        jax.ShapeDtypeStruct((pages, 2, width // 2, n_rows), BF16),
        jax.ShapeDtypeStruct((pages, n_rows, width), BF16),
    ]
    inputs = (*table, weight, patches)
    n = 1 + len(inputs) + n_homes
    return call(
        functools.partial(page_kernel, n_homes, cut),
        n_pages,
        [page_of(a, first_page) for a in inputs]
        + [pl.BlockSpec((1, 1, cap, width), lambda p, info, i=i: (i, p, 0, 0)) for _, i in words]
        + [pl.BlockSpec(memory_space=pl.ANY)] * (2 if kept else 0),
        [page_of(out[0])] + [page_of(o, first_page) for o in out[1:]],
        out,
        (info, *inputs, *(w for w, _ in words), *(kept or ())),
        aliases={n: 1, n + 1: 2} if kept else {},
    )


def gradient_kernel(info, *refs):
    *pairs, keep, send, acc = refs
    n_y, lows, highs, cut, wcol = keep.shape
    page = pl.program_id(0)
    got = sum(dot(pairs[i][0, 0], pairs[i + 1][0]) for i in range(0, len(pairs), 2))

    @pl.when(page == 0)
    def _():
        acc[...] = got

    @pl.when(page > 0)
    def _():
        acc[...] += got

    @pl.when(page == pl.num_programs(0) - 1)
    def _():
        for out, core in ((send, 1 - info[CORE]), (keep, info[CORE])):
            for y in range(n_y):
                column = pl.multiple_of((2 * y + core) * wcol, wcol)
                for part in range(lows * highs):
                    rows = acc[part * cut : (part + 1) * cut, pl.ds(column, wcol)]
                    out[y, part % lows, part // lows] = rows.astype(out.dtype)


def gradient(info, half, n_y, n_high, pairs):
    width = pairs[0][1].shape[-1]
    form = (n_y, 2, n_high, width // (4 * n_high), width // (2 * n_y))
    out = [jax.ShapeDtypeStruct(form, t) for t in (F32, BF16)]
    specs = []
    for x_t, dq in pairs:
        specs.append(
            pl.BlockSpec((1, 1) + x_t.shape[2:], lambda p, info: (p, half, 0, 0))
        )
        specs.append(page_of(dq))
    return call(
        gradient_kernel,
        pairs[0][1].shape[0],
        specs,
        [all_of(o) for o in out],
        out,
        (info, *(x for pair in pairs for x in pair)),
        [pltpu.VMEM((width // 2, width), F32)],
        flops=2 * width * width * sum(dq.shape[0] * dq.shape[1] for _, dq in pairs),
    )


def exchange(x, axis, offset):
    n = lax.axis_size(axis)
    return lax.ppermute(x, axis, [(i, i ^ offset) for i in range(n)])


def pick(x, i, axis=0):
    return lax.dynamic_index_in_dim(x, i, axis, keepdims=False)


def pick_sum(terms, i, axis=0):
    return sum(pick(t, i, axis).astype(F32) for t in terms)


def local(words, patches, proj, routes, targets, counts, flags):
    pages, wdev, width = words.shape
    pps = patches.shape[1]
    n_seq = lax.axis_size("seq")
    n_dp = lax.axis_size("dp")
    me = lax.axis_index("seq")
    my_dp = lax.axis_index("dp")
    core, y, low, high = me % 2, me // 2, my_dp % 2, my_dp // 2
    n_y, n_high = n_seq // 2, n_dp // 2
    cap = 2 * wdev // n_seq
    half = width // 2
    shard_rows = proj.shape[0]
    near, far = (0, 1), tuple(range(2, n_seq))

    info = jnp.concatenate([jnp.stack([me, core, my_dp]).astype(jnp.int32), counts])
    routes = routes.reshape(pages, 1, wdev)

    piece, bit = lax.dynamic_slice_in_dim(proj, core * half, half, 1)[None], 1
    other = exchange(piece, "dp", 2)
    routes, other = lax.optimization_barrier((routes, other))
    pieces = [(piece, 0), (other, bit)]
    while 2 * bit < n_high:
        piece, bit = jnp.concatenate([piece, other], axis=0), 2 * bit
        other = exchange(piece, "dp", 2 * bit)
        pieces = [(piece, 0), (other, bit)]

    split = pages - 1
    both = dispatch(info, routes, words, far, cap, 0, split, 2)
    held, both = lax.optimization_barrier((info, both))
    both = [exchange(rows, "seq", 2 * (k + 1)) for k, rows in enumerate(both)]
    rest = dispatch(held, routes, words, far, cap, split, pages - split)
    stay, across = dispatch(held, routes, words, near, cap, 0, pages)

    pair = jnp.concatenate([routes, targets.reshape(pages, 1, wdev)], axis=1)
    meta_near = jnp.stack([pair, exchange(pair, "seq", 1)])
    table_near = tables(info, meta_near, flags, near, cap, pps)
    meta_far = jnp.concatenate([exchange(meta_near, "seq", 2 * k) for k in range(1, n_y)], axis=0)

    last, rest, stay, across, table_near = lax.optimization_barrier(
        (pieces[-1][0], rest, stay, across, table_near)
    )
    pieces[-1] = (last, pieces[-1][1])
    gathered, offsets = [], []
    for piece, start in pieces:
        gathered += [piece, exchange(piece, "dp", 1)]
        offsets += [[2 * (start + i) + low for i in range(piece.shape[0])] for low in range(2)]
    gathered += [exchange(piece, "seq", 1) for piece in gathered]
    across = exchange(across, "seq", 1)
    rest = [exchange(rows, "seq", r) for rows, r in zip(rest, far)]
    weight = weights(info, patches, gathered, offsets)

    both, weight, meta_far = lax.optimization_barrier((both, weight, meta_far))
    first = [pair for rows in both for pair in ((rows, 0), (exchange(rows, "seq", 1), 1))]
    table_far = tables(info, meta_far, flags, far, cap, pps)
    run = functools.partial(run_pages, shard_rows // 2, info, weight, patches)
    loss, *pair_near = run(table_near, [(stay, 0), (across, 0)], 0)
    word_loss = [loss[:, 0], exchange(loss[:, 1], "seq", 1)]
    loss_a, *pair_far = run(table_far, first, 0)
    loss_b, *pair_far = run(table_far, [(rows, 0) for rows in rest], split, pair_far)
    losses = jnp.concatenate([loss_a, loss_b], axis=0)

    terms = []
    for h in range(2):
        keep, send = gradient(info, h, n_y, n_high, [pair_near, pair_far])
        info, keep, send = lax.optimization_barrier((info, keep, send))
        terms.append([keep, exchange(send, "seq", 1)])

    def over_y(terms):
        total = pick_sum(terms, y)
        for k in range(1, n_y):
            other = pick_sum(terms, jnp.bitwise_xor(y, k)).astype(BF16)
            total = total + exchange(other, "seq", 2 * k)
        return total

    def over_low(terms, axis):
        other = pick_sum(terms, 1 - low, axis).astype(BF16)
        return pick_sum(terms, low, axis) + exchange(other, "dp", 1)

    one = over_low([over_y(terms[0])], 0)
    two = over_y([over_low(terms[1], 1)])
    grad = jnp.concatenate([pick(one, high), pick(two, high)], axis=0)
    for k in range(1, n_high):
        to = jnp.bitwise_xor(high, k)
        other = jnp.concatenate([pick(one, to), pick(two, to)], axis=0).astype(BF16)
        grad = grad + exchange(other, "dp", 2 * k)

    for i, r in enumerate(far):
        word_loss.append(exchange(losses[:, i], "seq", r))
    return (sum(word_loss), grad)


def solution(mesh):
    in_specs = (
        P("dp", "seq", None),
        P("dp", "seq", None),
        P("dp", None),
        P("dp", "seq", None),
        P("dp", "seq"),
        P("dp"),
        P("dp", None, None),
    )
    out_specs = (P("dp", "seq"), P("dp", "seq"))
    return jax.shard_map(local, mesh=mesh, in_specs=in_specs, out_specs=out_specs, check_vma=False)
```

```python
import functools
import math

import jax
import jax.numpy as jnp
from jax import lax
from jax.experimental import pallas as pl
from jax.experimental.pallas import tpu as pltpu
from jax.sharding import PartitionSpec as P

MARGIN_BLOCK_SIZE = 64
VMEM_LIMIT = 20 * 1024 * 1024
ME, CORE, DP, COUNTS = 0, 1, 2, 3
TARGET, COEF = 0, 1
F32, BF16 = jnp.float32, jnp.bfloat16


def dot(a, b, contract=((1,), (0,))):
    return lax.dot_general(a, b, (contract, ((), ())), preferred_element_type=F32)


def iota(shape, axis):
    return lax.broadcasted_iota(jnp.int32, shape, axis)


def ranks(hits):
    n = hits.shape[1]
    before = (iota((n, n), 0) < iota((n, n), 1)).astype(BF16)
    return jnp.where(hits > 0, dot(hits.astype(BF16), before), -1.0)


def call(kernel, n_pages, in_specs, out_specs, out_shape, operands, scratch=(), aliases={}, flops=0):
    return pl.pallas_call(
        kernel,
        grid_spec=pltpu.PrefetchScalarGridSpec(
            num_scalar_prefetch=1,
            grid=(n_pages,),
            in_specs=in_specs,
            out_specs=out_specs,
            scratch_shapes=scratch,
        ),
        out_shape=out_shape,
        compiler_params=pltpu.CompilerParams(vmem_limit_bytes=VMEM_LIMIT),
        cost_estimate=pl.CostEstimate(flops=flops, bytes_accessed=0, transcendentals=0),
        input_output_aliases=aliases,
    )(*operands)


def page_of(array, first_page=0):
    rest = array.shape[1:]
    return pl.BlockSpec((1,) + rest, lambda p, info: (p + first_page,) + (0,) * len(rest))


def all_of(array):
    return pl.BlockSpec(array.shape, lambda p, info: (0,) * len(array.shape))


def pad_rows(n):
    return -(-n // 8) * 8


def stacked(rows):
    n, width = pad_rows(len(rows)), rows[0].shape[1]
    row = iota((n, width), 0)
    out = jnp.zeros((n, width), rows[0].dtype)
    for i, r in enumerate(rows):
        out = jnp.where(row == i, r, out)
    return out


def dispatch_kernel(plan, cap, info, routes, words, *outs):
    wdev = words.shape[1]
    slots = iota((cap, wdev), 0).astype(F32)
    by_page = {}
    for out, (offsets, first_page, n_pages) in zip(outs, plan):
        for p in range(n_pages):
            for i, offset in enumerate(offsets):
                by_page.setdefault(first_page + p, []).append((offset, out, i, p))
    tasks = [(page, *task) for page in by_page for task in by_page[page]]
    rank = ranks(
        stacked(
            [
                (routes[page] == jnp.bitwise_xor(info[ME], offset)).astype(F32)
                for page, offset, *_ in tasks
            ]
        )
    )
    n = 0
    for page, some in by_page.items():
        picks = [
            (slots == rank[n + i : n + i + 1]).astype(BF16) for i in range(len(some))
        ]
        rows = dot(jnp.concatenate(picks, axis=0), words[page]).astype(BF16)
        for i, (_, out, place, p) in enumerate(some):
            out[place, p] = rows[i * cap : (i + 1) * cap]
        n += len(some)


def dispatch(info, routes, words, plan, cap):
    width = words.shape[2]
    out = [
        jax.ShapeDtypeStruct((len(offsets), n_pages, cap, width), BF16)
        for offsets, _, n_pages in plan
    ]
    return call(
        functools.partial(dispatch_kernel, plan, cap),
        1,
        [all_of(routes), all_of(words)],
        [all_of(o) for o in out],
        out,
        (info, routes, words),
    )


def table_kernel(offsets, cap, info, meta, flags, bias, table, rank_out):
    me = info[ME]
    n_homes, pages, _, wdev = meta.shape
    nblk, all_blk = flags.shape[1:]
    n_rows, pps = bias.shape[1:]
    slots = iota((cap, wdev), 0).astype(F32)
    rank = ranks(
        stacked(
            [
                (meta[i, p, 0:1, :] == me).astype(F32)
                for p in range(pages)
                for i in range(n_homes)
            ]
        )
    )
    first = me * (pps // MARGIN_BLOCK_SIZE)
    block = iota((all_blk, pps), 1) // MARGIN_BLOCK_SIZE
    spread = (iota((all_blk, pps), 0) == first + block).astype(BF16)
    place = iota((1, wdev), 1) + 1
    for p in range(pages):
        t, idx = [], []
        for i, offset in enumerate(offsets):
            own = rank[p * n_homes + i : p * n_homes + i + 1]
            rank_out[p, i : i + 1] = own
            target = meta[i, p, 1:2, :]
            values = stacked([target // 64, target % 64, place // 64, place % 64]).astype(F32)
            got = dot((slots == own).astype(BF16), values.astype(BF16), ((1,), (1,)))
            got = got.astype(jnp.int32)
            t.append(got[:, 0:1] * 64 + got[:, 1:2])
            at = got[:, 2:3] * 64 + got[:, 3:4]
            idx.append(jnp.where(at > 0, at - 1 + jnp.bitwise_xor(me, offset) * wdev, -1))
        t, idx = jnp.concatenate(t, axis=0), jnp.concatenate(idx, axis=0)
        word_block = jnp.maximum(idx, 0) // MARGIN_BLOCK_SIZE == iota((n_rows, nblk), 1)
        margin = dot(word_block.astype(BF16), flags[p].astype(BF16)).astype(BF16)
        hit = dot(margin, spread)
        own = iota((n_rows, pps), 1) // MARGIN_BLOCK_SIZE == t // MARGIN_BLOCK_SIZE
        bias[p] = jnp.where((hit > 0.5) | own, 0.0, -jnp.inf).astype(BF16)
        count = info[COUNTS + p]
        valid = (idx >= 0) & (idx < count)
        coef = jnp.where(valid, 64.0 / count.astype(F32), 0.0)
        lane = iota((n_rows, 128), 1)
        table[p] = jnp.where(lane == TARGET, t.astype(F32), jnp.where(lane == COEF, coef, 0.0))


def tables(info, meta, flags, offsets, cap, pps):
    n_homes, pages, _, wdev = meta.shape
    out = [
        jax.ShapeDtypeStruct((pages, n_homes * cap, pps), BF16),
        jax.ShapeDtypeStruct((pages, n_homes * cap, 128), F32),
        jax.ShapeDtypeStruct((pages, pad_rows(n_homes), wdev), F32),
    ]
    return call(
        functools.partial(table_kernel, offsets, cap),
        1,
        [all_of(meta), all_of(flags)],
        [all_of(o) for o in out],
        out,
        (info, meta, flags),
    )


def weights_kernel(offsets, info, patches, *refs):
    *gathered, out, proj, sems = refs
    half = proj.shape[1] // 2

    def copies():
        for g, ref in enumerate(gathered):
            rows = ref.shape[1]
            core = g // len(offsets)
            for i, offset in enumerate(offsets[g % len(offsets)]):
                shard = jnp.bitwise_xor(info[DP], offset)
                first = jnp.bitwise_xor(info[CORE], core) * half
                to = proj.at[
                    pl.ds(pl.multiple_of(shard * rows, rows), rows),
                    pl.ds(pl.multiple_of(first, half), half),
                ]
                yield ref.at[i], to

    @pl.when(pl.program_id(0) == 0)
    def _():
        started = [
            pltpu.make_async_copy(a, b, sems.at[i]) for i, (a, b) in enumerate(copies())
        ]
        for copy in started:
            copy.start()
        for copy in started:
            copy.wait()

    out[0] = dot(proj[...], patches[0], ((1,), (1,))).astype(BF16)


def weights(info, patches, gathered, offsets):
    pages, pps, width = patches.shape
    out = jax.ShapeDtypeStruct((pages, width, pps), BF16)
    return call(
        functools.partial(weights_kernel, offsets),
        pages,
        [page_of(patches)] + [pl.BlockSpec(memory_space=pl.ANY)] * len(gathered),
        page_of(out),
        out,
        (info, patches, *gathered),
        [
            pltpu.VMEM((width, width), BF16),
            pltpu.SemaphoreType.DMA((sum(g.shape[0] for g in gathered),)),
        ],
    )


def page_kernel(n_homes, cut, info, bias, table, rank, weight, patches, *refs):
    words, (loss, x_t, dq) = refs[:n_homes], refs[-3:]
    pps, width = patches.shape[1:]
    cap = words[0].shape[2]
    n_rows = n_homes * cap
    scale = 2.0 / math.sqrt(width)
    x = jnp.concatenate([w[0, 0] for w in words], axis=0)
    scores = dot(x, weight[0]) * scale
    is_target = iota((n_rows, pps), 1) == table[0, :, TARGET : TARGET + 1].astype(jnp.int32)
    coef = table[0, :, COEF : COEF + 1]
    masked = scores + bias[0].astype(F32)
    top = jnp.max(masked, axis=1, keepdims=True)
    expo = jnp.exp(masked - top)
    total = jnp.sum(expo, axis=1, keepdims=True)
    target_score = jnp.sum(jnp.where(is_target, scores, 0.0), axis=1, keepdims=True)
    row_loss = jnp.where(coef > 0, top + jnp.log(total) - target_score, 0.0)
    share = expo * (1.0 / total)
    dscore = (coef * jnp.where(is_target, share - 1.0, share)).astype(BF16)
    back = (dot(dscore, patches[0]) * scale).astype(BF16)
    more = dq.shape[0] - n_rows
    if more:
        back = jnp.concatenate([back, jnp.zeros((more, width), BF16)], axis=0)
        x = jnp.concatenate([x, jnp.zeros((more, width), BF16)], axis=0)
    dq[...] = back
    slots = iota((cap, rank.shape[2]), 0).astype(F32)
    for r in range(n_homes):
        picked = jnp.where(slots == rank[0, r : r + 1, :], row_loss[r * cap : (r + 1) * cap], 0.0)
        loss[0, r : r + 1, :] = jnp.sum(picked, axis=0, keepdims=True)
    t = x.T
    for part in range(width // cut):
        to = part % 2 * (width // 2) + part // 2 * cut
        x_t[to : to + cut] = t[part * cut : (part + 1) * cut]


def run_pages(cut, info, weight, patches, table, words, first_page, kept=None):
    _, n_pages, cap, width = words[0][0].shape
    pages, wdev = patches.shape[0], table[2].shape[2]
    n_homes = len(words)
    n_rows = -(-n_homes * cap // 128) * 128
    out = [
        jax.ShapeDtypeStruct((n_pages, n_homes, wdev), F32),
        jax.ShapeDtypeStruct((width, pages * n_rows), BF16),
        jax.ShapeDtypeStruct((pages * n_rows, width), BF16),
    ]
    inputs = (*table, weight, patches)
    n = 1 + len(inputs) + n_homes
    return call(
        functools.partial(page_kernel, n_homes, cut),
        n_pages,
        [page_of(a, first_page) for a in inputs]
        + [pl.BlockSpec((1, 1, cap, width), lambda p, info, i=i: (i, p, 0, 0)) for _, i in words]
        + [pl.BlockSpec(memory_space=pl.ANY)] * (2 if kept else 0),
        [
            page_of(out[0]),
            pl.BlockSpec((width, n_rows), lambda p, info: (0, p + first_page)),
            pl.BlockSpec((n_rows, width), lambda p, info: (p + first_page, 0)),
        ],
        out,
        (info, *inputs, *(w for w, _ in words), *(kept or ())),
        aliases={n: 1, n + 1: 2} if kept else {},
    )


def gradient_kernel(info, *refs):
    *pairs, one, two = refs
    _, lows, highs, cut, _ = one.shape
    got = sum(dot(pairs[i][...], pairs[i + 1][...]) for i in range(0, len(pairs), 2))
    for part in range(2 * lows * highs):
        out, shard = (one, two)[part // (lows * highs)], part % (lows * highs)
        rows = got[part * cut : (part + 1) * cut]
        out[0, shard % lows, shard // lows] = rows.astype(out.dtype)


def gradient(info, other, dtype, n_y, n_high, pairs):
    width = pairs[0][0].shape[0]
    wcol = width // (2 * n_y)
    form = (n_y, 2, n_high, width // (4 * n_high), wcol)
    out = [jax.ShapeDtypeStruct(form, dtype)] * 2
    column = lambda y, info: (0, 2 * y + jnp.bitwise_xor(info[CORE], other))
    specs = []
    for x_t, dq in pairs:
        specs += [all_of(x_t), pl.BlockSpec((dq.shape[0], wcol), column)]
    return call(
        gradient_kernel,
        n_y,
        specs,
        [page_of(o) for o in out],
        out,
        (info, *(x for pair in pairs for x in pair)),
        flops=64 * width * width * sum(dq.shape[0] for _, dq in pairs),
    )


def exchange(x, axis, offset):
    n = lax.axis_size(axis)
    return lax.ppermute(x, axis, [(i, i ^ offset) for i in range(n)])


def pick(x, i, axis=0):
    start = [i if a == axis else 0 for a in range(x.ndim)]
    size = [1 if a == axis else n for a, n in enumerate(x.shape)]
    got = lax.dynamic_slice(x, start, size, allow_negative_indices=False)
    return got.reshape(x.shape[:axis] + x.shape[axis + 1 :])


def pick_sum(terms, i, axis=0):
    return sum(pick(t, i, axis).astype(F32) for t in terms)


def local(words, patches, proj, routes, targets, counts, flags):
    pages, wdev, width = words.shape
    pps = patches.shape[1]
    n_seq = lax.axis_size("seq")
    n_dp = lax.axis_size("dp")
    n_y, n_high = n_seq // 2, n_dp // 2
    cap = 2 * wdev // n_seq
    half = width // 2
    shard_rows = proj.shape[0]
    near, far = (0, 1), tuple(range(2, n_seq))

    me, my_dp = lax.axis_index("seq"), lax.axis_index("dp")
    core, y, low, high = me & 1, me >> 1, my_dp & 1, my_dp >> 1
    own = {
        "column": core * half,
        "low": low,
        "not_low": 1 - low,
        "y": [y ^ k for k in range(n_y)],
        "high": [high ^ k for k in range(n_high)],
    }
    info = jnp.concatenate([jnp.stack([me, core, my_dp]).astype(jnp.int32), counts])
    info, own, proj = lax.optimization_barrier((info, own, proj))
    routes = routes.reshape(pages, 1, wdev)

    piece = lax.dynamic_slice(
        proj, (0, own["column"]), (shard_rows, half), allow_negative_indices=False
    )
    piece, bit = piece[None], 1
    other = exchange(piece, "dp", 2)
    info, other = lax.optimization_barrier((info, other))
    pieces = [(piece, 0), (other, bit)]
    while 2 * bit < n_high:
        piece, bit = jnp.concatenate([piece, other], axis=0), 2 * bit
        other = exchange(piece, "dp", 2 * bit)
        pieces = [(piece, 0), (other, bit)]

    split = pages - 1
    both = dispatch(
        info, routes, words, [((2 * k, 2 * k + 1), 0, split) for k in range(1, n_y)], cap
    )
    held, both = lax.optimization_barrier((info, both))
    both = [exchange(rows, "seq", 2 * (k + 1)) for k, rows in enumerate(both)]
    stay, across, *rest = dispatch(
        held,
        routes,
        words,
        [((r,), 0, pages) for r in near] + [((r,), split, pages - split) for r in far],
        cap,
    )

    pair = jnp.concatenate([routes, targets.reshape(pages, 1, wdev)], axis=1)
    meta_near = jnp.stack([pair, exchange(pair, "seq", 1)])
    table_near = tables(info, meta_near, flags, near, cap, pps)
    meta_far = jnp.concatenate([exchange(meta_near, "seq", 2 * k) for k in range(1, n_y)], axis=0)

    gathered, offsets = [], []
    for piece, start in pieces:
        gathered += [piece, exchange(piece, "dp", 1)]
        offsets += [[2 * (start + i) + low for i in range(piece.shape[0])] for low in range(2)]
    gathered, rest, stay, across, table_near = lax.optimization_barrier(
        (gathered, rest, stay, across, table_near)
    )
    gathered += [exchange(piece, "seq", 1) for piece in gathered]
    across = exchange(across, "seq", 1)
    rest = [exchange(rows, "seq", r) for rows, r in zip(rest, far)]
    weight = weights(info, patches, gathered, offsets)

    both, weight, meta_far = lax.optimization_barrier((both, weight, meta_far))
    first = [pair for rows in both for pair in ((rows, 0), (exchange(rows, "seq", 1), 1))]
    table_far = tables(info, meta_far, flags, far, cap, pps)
    run = functools.partial(run_pages, shard_rows // 2, info, weight, patches)
    loss, *pair_near = run(table_near, [(stay, 0), (across, 0)], 0)
    word_loss = [loss[:, 0], exchange(loss[:, 1], "seq", 1)]
    loss_a, *pair_far = run(table_far, first, 0)
    loss_b, *pair_far = run(table_far, [(rows, 0) for rows in rest], split, pair_far)
    losses = jnp.concatenate([loss_a, loss_b], axis=0)
    for i, r in enumerate(far):
        word_loss.append(exchange(losses[:, i], "seq", r))
    word_loss = sum(word_loss)

    sent = gradient(info, 1, BF16, n_y, n_high, [pair_near, pair_far])
    held, word_loss, sent = lax.optimization_barrier((info, word_loss, sent))
    kept = gradient(held, 0, F32, n_y, n_high, [pair_near, pair_far])
    terms = [[keep, exchange(send, "seq", 1)] for keep, send in zip(kept, sent)]

    def over_y(terms):
        total = pick_sum(terms, own["y"][0])
        for k in range(1, n_y):
            total = total + exchange(pick_sum(terms, own["y"][k]).astype(BF16), "seq", 2 * k)
        return total

    def over_low(terms, axis):
        other = pick_sum(terms, own["not_low"], axis).astype(BF16)
        return pick_sum(terms, own["low"], axis) + exchange(other, "dp", 1)

    one = over_low([over_y(terms[0])], 0)
    two = over_y([over_low(terms[1], 1)])
    part = lambda k: jnp.concatenate([pick(x, own["high"][k]) for x in (one, two)], axis=0)
    grad = part(0)
    for k in range(1, n_high):
        grad = grad + exchange(part(k).astype(BF16), "dp", 2 * k)
    return (word_loss, grad)


def solution(mesh):
    in_specs = (
        P("dp", "seq", None),
        P("dp", "seq", None),
        P("dp", None),
        P("dp", "seq", None),
        P("dp", "seq"),
        P("dp"),
        P("dp", None, None),
    )
    out_specs = (P("dp", "seq"), P("dp", "seq"))
    return jax.shard_map(local, mesh=mesh, in_specs=in_specs, out_specs=out_specs, check_vma=False)
```

```python
import functools
import math

import jax
import jax.numpy as jnp
from jax import lax
from jax.experimental import pallas as pl
from jax.experimental.pallas import tpu as pltpu
from jax.sharding import PartitionSpec as P

MARGIN_BLOCK_SIZE = 64
SHIFT = 6
VMEM_LIMIT = 16 * 1024 * 1024
ME, CORE, DP, COUNTS = 0, 1, 2, 3
TARGET, COEF = 0, 1
F32, BF16 = jnp.float32, jnp.bfloat16


def dot(a, b, contract=((1,), (0,))):
    return lax.dot_general(a, b, (contract, ((), ())), preferred_element_type=F32)


def iota(shape, axis):
    return lax.broadcasted_iota(jnp.int32, shape, axis)


def ranks(hits):
    n = hits.shape[1]
    before = (iota((n, n), 0) < iota((n, n), 1)).astype(BF16)
    return jnp.where(hits > 0, dot(hits.astype(BF16), before), -1.0)


def call(kernel, n_pages, in_specs, out_specs, out_shape, operands, scratch=(), aliases={}, flops=0):
    return pl.pallas_call(
        kernel,
        grid_spec=pltpu.PrefetchScalarGridSpec(
            num_scalar_prefetch=1,
            grid=(n_pages,),
            in_specs=in_specs,
            out_specs=out_specs,
            scratch_shapes=scratch,
        ),
        out_shape=out_shape,
        compiler_params=pltpu.CompilerParams(vmem_limit_bytes=VMEM_LIMIT),
        cost_estimate=pl.CostEstimate(flops=flops, bytes_accessed=0, transcendentals=0),
        input_output_aliases=aliases,
    )(*operands)


def page_of(array, first_page=0):
    rest = array.shape[1:]
    return pl.BlockSpec((1,) + rest, lambda p, info: (p + first_page,) + (0,) * len(rest))


def all_of(array):
    return pl.BlockSpec(array.shape, lambda p, info: (0,) * len(array.shape))


def pad_rows(n):
    return -(-n // 8) * 8


def stacked(rows):
    n, width = pad_rows(len(rows)), rows[0].shape[1]
    row = iota((n, width), 0)
    out = jnp.zeros((n, width), rows[0].dtype)
    for i, r in enumerate(rows):
        out = jnp.where(row == i, r, out)
    return out


def dispatch_kernel(plan, cap, info, routes, words, *outs):
    wdev = words.shape[1]
    slots = iota((cap, wdev), 0).astype(F32)
    by_page = {}
    for out, (offsets, first_page, n_pages) in zip(outs, plan):
        for p in range(n_pages):
            for i, offset in enumerate(offsets):
                by_page.setdefault(first_page + p, []).append((offset, out, i, p))
    tasks = [(page, *task) for page in by_page for task in by_page[page]]
    rank = ranks(
        stacked(
            [
                (routes[page] == jnp.bitwise_xor(info[ME], offset)).astype(F32)
                for page, offset, *_ in tasks
            ]
        )
    )
    n = 0
    for page, some in by_page.items():
        picks = [
            (slots == rank[n + i : n + i + 1]).astype(BF16) for i in range(len(some))
        ]
        rows = dot(jnp.concatenate(picks, axis=0), words[page]).astype(BF16)
        for i, (_, out, place, p) in enumerate(some):
            out[place, p] = rows[i * cap : (i + 1) * cap]
        n += len(some)


def dispatch(info, routes, words, plan, cap):
    width = words.shape[2]
    out = [
        jax.ShapeDtypeStruct((len(offsets), n_pages, cap, width), BF16)
        for offsets, _, n_pages in plan
    ]
    return call(
        functools.partial(dispatch_kernel, plan, cap),
        1,
        [all_of(routes), all_of(words)],
        [all_of(o) for o in out],
        out,
        (info, routes, words),
    )


def table_kernel(offsets, cap, info, meta, flags, bias, table, rank_out):
    me = info[ME]
    n_homes, pages, _, wdev = meta.shape
    nblk, all_blk = flags.shape[1:]
    n_rows, pps = bias.shape[1:]
    slots = iota((cap, wdev), 0).astype(F32)
    rank = ranks(
        stacked(
            [
                (meta[i, p, 0:1, :] == me).astype(F32)
                for p in range(pages)
                for i in range(n_homes)
            ]
        )
    )
    first = me * (pps // MARGIN_BLOCK_SIZE)
    block = iota((all_blk, pps), 1) >> SHIFT
    spread = (iota((all_blk, pps), 0) == first + block).astype(BF16)
    place = iota((1, wdev), 1) + 1
    for p in range(pages):
        t, idx = [], []
        for i, offset in enumerate(offsets):
            own = rank[p * n_homes + i : p * n_homes + i + 1]
            rank_out[p, i : i + 1] = own
            target = meta[i, p, 1:2, :]
            values = stacked([target >> 6, target & 63, place >> 6, place & 63]).astype(F32)
            got = dot((slots == own).astype(BF16), values.astype(BF16), ((1,), (1,)))
            got = got.astype(jnp.int32)
            t.append(got[:, 0:1] * 64 + got[:, 1:2])
            at = got[:, 2:3] * 64 + got[:, 3:4]
            idx.append(jnp.where(at > 0, at - 1 + jnp.bitwise_xor(me, offset) * wdev, -1))
        t, idx = jnp.concatenate(t, axis=0), jnp.concatenate(idx, axis=0)
        word_block = jnp.maximum(idx, 0) >> SHIFT == iota((n_rows, nblk), 1)
        margin = dot(word_block.astype(BF16), flags[p].astype(BF16)).astype(BF16)
        hit = dot(margin, spread)
        own = iota((n_rows, pps), 1) >> SHIFT == t >> SHIFT
        bias[p] = jnp.where((hit > 0.5) | own, 0.0, -jnp.inf).astype(BF16)
        count = info[COUNTS + p]
        valid = (idx >= 0) & (idx < count)
        coef = jnp.where(valid, 64.0 / count.astype(F32), 0.0)
        lane = iota((n_rows, 128), 1)
        table[p] = jnp.where(lane == TARGET, t.astype(F32), jnp.where(lane == COEF, coef, 0.0))


def tables(info, meta, flags, offsets, cap, pps):
    n_homes, pages, _, wdev = meta.shape
    out = [
        jax.ShapeDtypeStruct((pages, n_homes * cap, pps), BF16),
        jax.ShapeDtypeStruct((pages, n_homes * cap, 128), F32),
        jax.ShapeDtypeStruct((pages, pad_rows(n_homes), wdev), F32),
    ]
    return call(
        functools.partial(table_kernel, offsets, cap),
        1,
        [all_of(meta), all_of(flags)],
        [all_of(o) for o in out],
        out,
        (info, meta, flags),
    )


def weights_kernel(offsets, info, patches, *refs):
    *gathered, out, proj, sems = refs
    half = proj.shape[1] // 2

    def copies():
        for g, ref in enumerate(gathered):
            rows = ref.shape[1]
            core = g // len(offsets)
            for i, offset in enumerate(offsets[g % len(offsets)]):
                shard = jnp.bitwise_xor(info[DP], offset)
                first = jnp.bitwise_xor(info[CORE], core) * half
                to = proj.at[
                    pl.ds(pl.multiple_of(shard * rows, rows), rows),
                    pl.ds(pl.multiple_of(first, half), half),
                ]
                yield ref.at[i], to

    @pl.when(pl.program_id(0) == 0)
    def _():
        started = [
            pltpu.make_async_copy(a, b, sems.at[i]) for i, (a, b) in enumerate(copies())
        ]
        for copy in started:
            copy.start()
        for copy in started:
            copy.wait()

    out[0] = dot(proj[...], patches[0], ((1,), (1,))).astype(BF16)


def weights(info, patches, gathered, offsets):
    pages, pps, width = patches.shape
    out = jax.ShapeDtypeStruct((pages, width, pps), BF16)
    return call(
        functools.partial(weights_kernel, offsets),
        pages,
        [page_of(patches)] + [pl.BlockSpec(memory_space=pl.ANY)] * len(gathered),
        page_of(out),
        out,
        (info, patches, *gathered),
        [
            pltpu.VMEM((width, width), BF16),
            pltpu.SemaphoreType.DMA((sum(g.shape[0] for g in gathered),)),
        ],
    )


def page_kernel(n_homes, info, bias, table, rank, weight, patches, *refs):
    *words, loss, x_t, dq = refs
    pps, width = patches.shape[1:]
    cap = words[0].shape[2]
    n_rows = n_homes * cap
    scale = 2.0 / math.sqrt(width)
    x = jnp.concatenate([w[0, 0] for w in words], axis=0)
    scores = dot(x, weight[0]) * scale
    is_target = iota((n_rows, pps), 1) == table[0, :, TARGET : TARGET + 1].astype(jnp.int32)
    coef = table[0, :, COEF : COEF + 1]
    masked = scores + bias[0].astype(F32)
    top = jnp.max(masked, axis=1, keepdims=True)
    expo = jnp.exp(masked - top)
    total = jnp.sum(expo, axis=1, keepdims=True)
    target_score = jnp.sum(jnp.where(is_target, scores, 0.0), axis=1, keepdims=True)
    row_loss = jnp.where(coef > 0, top + jnp.log(total) - target_score, 0.0)
    share = expo * (1.0 / total)
    dscore = (coef * jnp.where(is_target, share - 1.0, share)).astype(BF16)
    back = (dot(dscore, patches[0]) * scale).astype(BF16)
    more = dq.shape[0] - n_rows
    if more:
        back = jnp.concatenate([back, jnp.zeros((more, width), BF16)], axis=0)
        x = jnp.concatenate([x, jnp.zeros((more, width), BF16)], axis=0)
    dq[...] = back
    slots = iota((cap, rank.shape[2]), 0).astype(F32)
    for r in range(n_homes):
        picked = jnp.where(slots == rank[0, r : r + 1, :], row_loss[r * cap : (r + 1) * cap], 0.0)
        loss[0, r : r + 1, :] = jnp.sum(picked, axis=0, keepdims=True)
    x_t[...] = x.T


def run_pages(info, weight, patches, table, words, first_page):
    _, n_pages, cap, width = words[0][0].shape
    wdev = table[2].shape[2]
    n_homes = len(words)
    n_rows = -(-n_homes * cap // 128) * 128
    out = [
        jax.ShapeDtypeStruct((n_pages, n_homes, wdev), F32),
        jax.ShapeDtypeStruct((width, n_pages * n_rows), BF16),
        jax.ShapeDtypeStruct((n_pages * n_rows, width), BF16),
    ]
    inputs = (*table, weight, patches)
    return call(
        functools.partial(page_kernel, n_homes),
        n_pages,
        [page_of(a, first_page) for a in inputs]
        + [pl.BlockSpec((1, 1, cap, width), lambda p, info, i=i: (i, p, 0, 0)) for _, i in words],
        [
            page_of(out[0]),
            pl.BlockSpec((width, n_rows), lambda p, info: (0, p)),
            pl.BlockSpec((n_rows, width), lambda p, info: (p, 0)),
        ],
        out,
        (info, *inputs, *(w for w, _ in words)),
    )


def gradient_kernel(n_pairs, info, *refs):
    pairs, (*before, out) = refs[: 2 * n_pairs], refs[2 * n_pairs :]
    got = sum(dot(pairs[i][...], pairs[i + 1][...]) for i in range(0, len(pairs), 2))
    for part in before:
        got = got + part[0]
    out[0] = got.astype(out.dtype)


def gradient(info, other, dtype, n_y, pairs, before=()):
    width = pairs[0][0].shape[0]
    wcol = width // (2 * n_y)
    out = jax.ShapeDtypeStruct((n_y, width, wcol), dtype)
    column = lambda y, info: (0, 2 * y + jnp.bitwise_xor(info[CORE], other))
    specs = []
    for x_t, dq in pairs:
        specs += [all_of(x_t), pl.BlockSpec((dq.shape[0], wcol), column)]
    return call(
        functools.partial(gradient_kernel, len(pairs)),
        n_y,
        specs + [page_of(b) for b in before],
        page_of(out),
        out,
        (info, *(x for pair in pairs for x in pair), *before),
        flops=64 * width * width * sum(dq.shape[0] for _, dq in pairs),
    )


def exchange(x, axis, offset):
    n = lax.axis_size(axis)
    return lax.ppermute(x, axis, [(i, i ^ offset) for i in range(n)])


def exchange_both(x, dp, seq):
    n_seq = lax.axis_size("seq")
    n = lax.axis_size("dp") * n_seq
    return lax.ppermute(x, ("dp", "seq"), [(i, i ^ (dp * n_seq + seq)) for i in range(n)])


def pick(x, places):
    places = list(places) + [None] * (x.ndim - len(places))
    start = [0 if i is None else i for i in places]
    size = [n if i is None else 1 for i, n in zip(places, x.shape)]
    got = lax.dynamic_slice(x, start, size, allow_negative_indices=False)
    return got.reshape([n for i, n in zip(places, x.shape) if i is None])


def local(words, patches, proj, routes, targets, counts, flags):
    pages, wdev, width = words.shape
    pps = patches.shape[1]
    n_seq = lax.axis_size("seq")
    n_dp = lax.axis_size("dp")
    n_y, n_high = n_seq // 2, n_dp // 2
    cap = 2 * wdev // n_seq
    half = width // 2
    shard_rows = proj.shape[0]
    near, far = (0, 1), tuple(range(2, n_seq))

    me, my_dp = lax.axis_index("seq"), lax.axis_index("dp")
    core, y, low, high = me & 1, me >> 1, my_dp & 1, my_dp >> 1
    own = {
        "column": core * half,
        "low": [low ^ k for k in range(2)],
        "y": [y ^ k for k in range(n_y)],
        "high": [high ^ k for k in range(n_high)],
    }
    info = jnp.concatenate([jnp.stack([me, core, my_dp]).astype(jnp.int32), counts])
    info, own, proj = lax.optimization_barrier((info, own, proj))
    routes = routes.reshape(pages, 1, wdev)

    split = pages - 1
    both = dispatch(
        info, routes, words, [((2 * k, 2 * k + 1), 0, split) for k in range(1, n_y)], cap
    )
    info, proj, both = lax.optimization_barrier((info, proj, both))
    both = [exchange(rows, "seq", 2 * (k + 1)) for k, rows in enumerate(both)]
    stay, across, *rest = dispatch(
        info,
        routes,
        words,
        [((r,), 0, pages) for r in near] + [((r,), split, pages - split) for r in far],
        cap,
    )

    piece = lax.dynamic_slice(
        proj, (0, own["column"]), (shard_rows, half), allow_negative_indices=False
    )
    pieces = [piece] + [exchange(piece, "dp", 2 * k) for k in range(1, n_high)]
    group = n_high // 2
    groups = [jnp.stack(pieces[i : i + group]) for i in range(0, n_high, group)]

    pair = jnp.concatenate([routes, targets.reshape(pages, 1, wdev)], axis=1)
    meta_near = jnp.stack([pair, exchange(pair, "seq", 1)])
    table_near = tables(info, meta_near, flags, near, cap, pps)
    meta_far = jnp.concatenate([exchange(meta_near, "seq", 2 * k) for k in range(1, n_y)], axis=0)

    crossed = exchange(groups[0], "dp", 1)
    crossed, groups[1], rest, stay, across, table_near = lax.optimization_barrier(
        (crossed, groups[1], rest, stay, across, table_near)
    )
    gathered = [groups[0], crossed, groups[1], exchange(groups[1], "dp", 1)]
    offsets = [[2 * (i + k) + bit for k in range(group)] for i in (0, group) for bit in range(2)]
    gathered += [exchange(some, "seq", 1) for some in gathered]
    across = exchange(across, "seq", 1)
    rest = [exchange(rows, "seq", r) for rows, r in zip(rest, far)]
    weight = weights(info, patches, gathered, offsets)
    run = functools.partial(run_pages, info, weight, patches)
    loss, *pair_near = run(table_near, [(stay, 0), (across, 0)], 0)
    word_loss = [loss[:, 0], exchange(loss[:, 1], "seq", 1)]

    both, meta_far, pair_near = lax.optimization_barrier((both, meta_far, pair_near))
    first = [pair for rows in both for pair in ((rows, 0), (exchange(rows, "seq", 1), 1))]
    table_far = tables(info, meta_far, flags, far, cap, pps)
    loss_a, *pair_a = run(table_far, first, 0)
    before = [gradient(info, other, F32, n_y, [pair_near, pair_a]) for other in range(2)]
    before, rest = lax.optimization_barrier((before, rest))
    loss_b, *pair_b = run(table_far, [(rows, 0) for rows in rest], split)
    losses = jnp.concatenate([loss_a, loss_b], axis=0)
    for i, r in enumerate(far):
        word_loss.append(exchange(losses[:, i], "seq", r))

    sent = gradient(info, 1, BF16, n_y, [pair_b], [before[1]])
    kept = gradient(info, 0, F32, n_y, [pair_b], [before[0]])
    form = (n_y, n_high, 2, shard_rows, width // n_seq)
    terms = [kept.reshape(form), exchange(sent, "seq", 1).reshape(form)]
    part = lambda i, j: sum(
        pick(t, (own["y"][i], None, own["low"][j])).astype(F32) for t in terms
    )
    total = part(0, 0)
    for i in range(n_y):
        for j in range(2):
            if i or j:
                total = total + exchange_both(part(i, j).astype(BF16), j, 2 * i)
    grad = pick(total, (own["high"][0],))
    for k in range(1, n_high):
        grad = grad + exchange(pick(total, (own["high"][k],)).astype(BF16), "dp", 2 * k)
    return (sum(word_loss), grad)


def solution(mesh):
    in_specs = (
        P("dp", "seq", None),
        P("dp", "seq", None),
        P("dp", None),
        P("dp", "seq", None),
        P("dp", "seq"),
        P("dp"),
        P("dp", None, None),
    )
    out_specs = (P("dp", "seq"), P("dp", "seq"))
    return jax.shard_map(local, mesh=mesh, in_specs=in_specs, out_specs=out_specs, check_vma=False)
```

```python
import functools
import math

import jax
import jax.numpy as jnp
from jax import lax
from jax.experimental import pallas as pl
from jax.experimental.pallas import tpu as pltpu
from jax.sharding import PartitionSpec as P

MARGIN_BLOCK_SIZE = 64
SHIFT = 6
VMEM_LIMIT = 16 * 1024 * 1024
WORK = 1<<31
ME, CORE, DP, COUNTS = 0, 1, 2, 3
TARGET, COEF = 0, 1
F32, BF16 = jnp.float32, jnp.bfloat16


def dot(a, b, contract=((1,), (0,))):
    return lax.dot_general(a, b, (contract, ((), ())), preferred_element_type=F32)


def iota(shape, axis):
    return lax.broadcasted_iota(jnp.int32, shape, axis)


def ranks(hits):
    n = hits.shape[1]
    before = (iota((n, n), 0) < iota((n, n), 1)).astype(BF16)
    return jnp.where(hits > 0, dot(hits.astype(BF16), before), -1.0)


def call(kernel, n_pages, in_specs, out_specs, out_shape, operands, scratch=(), aliases={}, flops=0):
    return pl.pallas_call(
        kernel,
        grid_spec=pltpu.PrefetchScalarGridSpec(
            num_scalar_prefetch=1,
            grid=(n_pages,),
            in_specs=in_specs,
            out_specs=out_specs,
            scratch_shapes=scratch,
        ),
        out_shape=out_shape,
        compiler_params=pltpu.CompilerParams(vmem_limit_bytes=VMEM_LIMIT),
        cost_estimate=pl.CostEstimate(flops=flops, bytes_accessed=0, transcendentals=0),
        input_output_aliases=aliases,
    )(*operands)


def page_of(array, first_page=0):
    rest = array.shape[1:]
    return pl.BlockSpec((1,) + rest, lambda p, info: (p + first_page,) + (0,) * len(rest))


def all_of(array):
    return pl.BlockSpec(array.shape, lambda p, info: (0,) * len(array.shape))


def pad_rows(n):
    return -(-n // 8) * 8


def stacked(rows):
    n, width = pad_rows(len(rows)), rows[0].shape[1]
    row = iota((n, width), 0)
    out = jnp.zeros((n, width), rows[0].dtype)
    for i, r in enumerate(rows):
        out = jnp.where(row == i, r, out)
    return out


def dispatch_kernel(plan, cap, info, routes, words, *outs):
    wdev = words.shape[1]
    slots = iota((cap, wdev), 0).astype(F32)
    by_page = {}
    for out, (offsets, first_page, n_pages) in zip(outs, plan):
        for p in range(n_pages):
            for i, offset in enumerate(offsets):
                by_page.setdefault(first_page + p, []).append((offset, out, i, p))
    tasks = [(page, *task) for page in by_page for task in by_page[page]]
    rank = ranks(
        stacked(
            [
                (routes[page] == jnp.bitwise_xor(info[ME], offset)).astype(F32)
                for page, offset, *_ in tasks
            ]
        )
    )
    n = 0
    for page, some in by_page.items():
        picks = [
            (slots == rank[n + i : n + i + 1]).astype(BF16) for i in range(len(some))
        ]
        rows = dot(jnp.concatenate(picks, axis=0), words[page]).astype(BF16)
        for i, (_, out, place, p) in enumerate(some):
            out[place, p] = rows[i * cap : (i + 1) * cap]
        n += len(some)


def dispatch(info, routes, words, plan, cap, flops=0):
    width = words.shape[2]
    out = [
        jax.ShapeDtypeStruct((len(offsets), n_pages, cap, width), BF16)
        for offsets, _, n_pages in plan
    ]
    return call(
        functools.partial(dispatch_kernel, plan, cap),
        1,
        [all_of(routes), all_of(words)],
        [all_of(o) for o in out],
        out,
        (info, routes, words),
        flops=flops,
    )


def table_kernel(offsets, cap, info, meta, flags, bias, table, rank_out):
    me = info[ME]
    n_homes, pages, _, wdev = meta.shape
    nblk, all_blk = flags.shape[1:]
    n_rows, pps = bias.shape[1:]
    slots = iota((cap, wdev), 0).astype(F32)
    rank = ranks(
        stacked(
            [
                (meta[i, p, 0:1, :] == me).astype(F32)
                for p in range(pages)
                for i in range(n_homes)
            ]
        )
    )
    first = me * (pps // MARGIN_BLOCK_SIZE)
    block = iota((all_blk, pps), 1) >> SHIFT
    spread = (iota((all_blk, pps), 0) == first + block).astype(BF16)
    place = iota((1, wdev), 1) + 1
    for p in range(pages):
        t, idx = [], []
        for i, offset in enumerate(offsets):
            own = rank[p * n_homes + i : p * n_homes + i + 1]
            rank_out[p, i : i + 1] = own
            target = meta[i, p, 1:2, :]
            values = stacked([target >> 6, target & 63, place >> 6, place & 63]).astype(F32)
            got = dot((slots == own).astype(BF16), values.astype(BF16), ((1,), (1,)))
            got = got.astype(jnp.int32)
            t.append(got[:, 0:1] * 64 + got[:, 1:2])
            at = got[:, 2:3] * 64 + got[:, 3:4]
            idx.append(jnp.where(at > 0, at - 1 + jnp.bitwise_xor(me, offset) * wdev, -1))
        t, idx = jnp.concatenate(t, axis=0), jnp.concatenate(idx, axis=0)
        word_block = jnp.maximum(idx, 0) >> SHIFT == iota((n_rows, nblk), 1)
        margin = dot(word_block.astype(BF16), flags[p].astype(BF16)).astype(BF16)
        hit = dot(margin, spread)
        own = iota((n_rows, pps), 1) >> SHIFT == t >> SHIFT
        bias[p] = jnp.where((hit > 0.5) | own, 0.0, -jnp.inf).astype(BF16)
        count = info[COUNTS + p]
        valid = (idx >= 0) & (idx < count)
        coef = jnp.where(valid, 64.0 / count.astype(F32), 0.0)
        lane = iota((n_rows, 128), 1)
        table[p] = jnp.where(lane == TARGET, t.astype(F32), jnp.where(lane == COEF, coef, 0.0))


def tables(info, meta, flags, offsets, cap, pps, flops=0):
    n_homes, pages, _, wdev = meta.shape
    out = [
        jax.ShapeDtypeStruct((pages, n_homes * cap, pps), BF16),
        jax.ShapeDtypeStruct((pages, n_homes * cap, 128), F32),
        jax.ShapeDtypeStruct((pages, pad_rows(n_homes), wdev), F32),
    ]
    return call(
        functools.partial(table_kernel, offsets, cap),
        1,
        [all_of(meta), all_of(flags)],
        [all_of(o) for o in out],
        out,
        (info, meta, flags),
        flops=flops,
    )


def half_kernel(info, proj, out):
    out[...] = proj[...]


def half_of(info, proj):
    rows, width = proj.shape
    out = jax.ShapeDtypeStruct((rows, width // 2), BF16)
    return call(
        half_kernel,
        1,
        [pl.BlockSpec((rows, width // 2), lambda p, info: (0, info[CORE]))],
        all_of(out),
        out,
        (info, proj),
        flops=1 << 35,
    )


def weights_kernel(offsets, info, patches, *refs):
    gathered, (*before, out, proj, sems) = refs[: 2 * len(offsets)], refs[2 * len(offsets) :]
    half = proj.shape[1] // 2
    rows = gathered[0].shape[1]
    shards = [offset for some in offsets for offset in some]

    def copies():
        n = 0
        for core in range(2):
            at = 0
            for some, ref in zip(offsets, gathered[core * len(offsets) :]):
                for i in range(len(some)):
                    first = jnp.bitwise_xor(info[CORE], core) * half
                    to = proj.at[pl.ds(at * rows, rows), pl.ds(pl.multiple_of(first, half), half)]
                    yield pltpu.make_async_copy(ref.at[i], to, sems.at[n])
                    at, n = at + 1, n + 1

    @pl.when(pl.program_id(0) == 0)
    def _():
        started = list(copies())
        for copy in started:
            copy.start()
        for copy in started:
            copy.wait()

    for other in before:
        out[...] = other[...]
    got = dot(proj[...], patches[0], ((1,), (1,))).astype(BF16)
    for i, offset in enumerate(shards):
        to = pl.multiple_of(jnp.bitwise_xor(info[DP], offset) * rows, rows)
        out[0, pl.ds(to, rows)] = got[i * rows : (i + 1) * rows]


def weights(info, patches, gathered, offsets, before=(), flops=0):
    pages, pps, width = patches.shape
    n_shards = sum(len(some) for some in offsets)
    out = jax.ShapeDtypeStruct((pages, width, pps), BF16)
    return call(
        functools.partial(weights_kernel, offsets),
        pages,
        [page_of(patches)]
        + [pl.BlockSpec(memory_space=pl.ANY)] * len(gathered)
        + [page_of(b) for b in before],
        page_of(out),
        out,
        (info, patches, *gathered, *before),
        [
            pltpu.VMEM((n_shards * gathered[0].shape[1], width), BF16),
            pltpu.SemaphoreType.DMA((2 * n_shards,)),
        ],
        flops=flops,
    )


def page_kernel(n_homes, info, bias, table, rank, weight, patches, *refs):
    *words, loss, x_t, dq = refs
    pps, width = patches.shape[1:]
    cap = words[0].shape[2]
    n_rows = n_homes * cap
    scale = 2.0 / math.sqrt(width)
    x = jnp.concatenate([w[0, 0] for w in words], axis=0)
    scores = dot(x, weight[0]) * scale
    is_target = iota((n_rows, pps), 1) == table[0, :, TARGET : TARGET + 1].astype(jnp.int32)
    coef = table[0, :, COEF : COEF + 1]
    masked = scores + bias[0].astype(F32)
    top = jnp.max(masked, axis=1, keepdims=True)
    expo = jnp.exp(masked - top)
    total = jnp.sum(expo, axis=1, keepdims=True)
    target_score = jnp.sum(jnp.where(is_target, scores, 0.0), axis=1, keepdims=True)
    row_loss = jnp.where(coef > 0, top + jnp.log(total) - target_score, 0.0)
    share = expo * (1.0 / total)
    dscore = (coef * jnp.where(is_target, share - 1.0, share)).astype(BF16)
    back = (dot(dscore, patches[0]) * scale).astype(BF16)
    more = dq.shape[0] - n_rows
    if more:
        back = jnp.concatenate([back, jnp.zeros((more, width), BF16)], axis=0)
        x = jnp.concatenate([x, jnp.zeros((more, width), BF16)], axis=0)
    dq[...] = back
    slots = iota((cap, rank.shape[2]), 0).astype(F32)
    for r in range(n_homes):
        picked = jnp.where(slots == rank[0, r : r + 1, :], row_loss[r * cap : (r + 1) * cap], 0.0)
        loss[0, r : r + 1, :] = jnp.sum(picked, axis=0, keepdims=True)
    x_t[...] = x.T


def run_pages(info, weight, patches, table, words, first_page):
    _, n_pages, cap, width = words[0][0].shape
    wdev = table[2].shape[2]
    n_homes = len(words)
    n_rows = -(-n_homes * cap // 128) * 128
    out = [
        jax.ShapeDtypeStruct((n_pages, n_homes, wdev), F32),
        jax.ShapeDtypeStruct((width, n_pages * n_rows), BF16),
        jax.ShapeDtypeStruct((n_pages * n_rows, width), BF16),
    ]
    inputs = (*table, weight, patches)
    return call(
        functools.partial(page_kernel, n_homes),
        n_pages,
        [page_of(a, first_page) for a in inputs]
        + [pl.BlockSpec((1, 1, cap, width), lambda p, info, i=i: (i, p, 0, 0)) for _, i in words],
        [
            page_of(out[0]),
            pl.BlockSpec((width, n_rows), lambda p, info: (0, p)),
            pl.BlockSpec((n_rows, width), lambda p, info: (p, 0)),
        ],
        out,
        (info, *inputs, *(w for w, _ in words)),
    )


def gradient_kernel(n_pairs, info, *refs):
    pairs, (*before, out) = refs[: 2 * n_pairs], refs[2 * n_pairs :]
    got = sum(dot(pairs[i][...], pairs[i + 1][...]) for i in range(0, len(pairs), 2))
    for part in before:
        got = got + part[0]
    out[0] = got.astype(out.dtype)


def gradient(info, other, dtype, n_y, pairs, before=()):
    width = pairs[0][0].shape[0]
    wcol = width // (2 * n_y)
    out = jax.ShapeDtypeStruct((n_y, width, wcol), dtype)
    column = lambda y, info: (0, 2 * y + jnp.bitwise_xor(info[CORE], other))
    specs = []
    for x_t, dq in pairs:
        specs += [all_of(x_t), pl.BlockSpec((dq.shape[0], wcol), column)]
    return call(
        functools.partial(gradient_kernel, len(pairs)),
        n_y,
        specs + [page_of(b) for b in before],
        page_of(out),
        out,
        (info, *(x for pair in pairs for x in pair), *before),
        flops=64 * width * width * sum(dq.shape[0] for _, dq in pairs) if before else 0,
    )


def exchange(x, axis, offset):
    n = lax.axis_size(axis)
    return lax.ppermute(x, axis, [(i, i ^ offset) for i in range(n)])


def exchange_both(x, dp, seq):
    n_seq = lax.axis_size("seq")
    n = lax.axis_size("dp") * n_seq
    return lax.ppermute(x, ("dp", "seq"), [(i, i ^ (dp * n_seq + seq)) for i in range(n)])


def pick(x, places):
    places = list(places) + [None] * (x.ndim - len(places))
    start = [0 if i is None else i for i in places]
    size = [n if i is None else 1 for i, n in zip(places, x.shape)]
    got = lax.dynamic_slice(x, start, size, allow_negative_indices=False)
    return got.reshape([n for i, n in zip(places, x.shape) if i is None])


def local(words, patches, proj, routes, targets, counts, flags):
    pages, wdev, width = words.shape
    pps = patches.shape[1]
    n_seq = lax.axis_size("seq")
    n_dp = lax.axis_size("dp")
    n_y, n_high = n_seq // 2, n_dp // 2
    cap = 2 * wdev // n_seq
    shard_rows = proj.shape[0]
    near, far = (0, 1), tuple(range(2, n_seq))

    me, my_dp = lax.axis_index("seq"), lax.axis_index("dp")
    core, y, low, high = me & 1, me >> 1, my_dp & 1, my_dp >> 1
    own = {
        "low": [low ^ k for k in range(2)],
        "y": [y ^ k for k in range(n_y)],
        "high": [high ^ k for k in range(n_high)],
    }
    info = jnp.concatenate([jnp.stack([me, core, my_dp]).astype(jnp.int32), counts])
    info, own, proj = lax.optimization_barrier((info, own, proj))
    routes = routes.reshape(pages, 1, wdev)

    split = pages - 1
    both = dispatch(
        info, routes, words, [((2 * k, 2 * k + 1), 0, split) for k in range(1, n_y)], cap
    )
    info, proj, both = lax.optimization_barrier((info, proj, both))
    both = [exchange(rows, "seq", 2 * (k + 1)) for k, rows in enumerate(both)]
    piece = half_of(info, proj)
    pieces = [piece] + [exchange(piece, "dp", 2 * k) for k in range(1, n_high)]
    group = n_high // 2
    stay, across, *rest = dispatch(
        info,
        routes,
        words,
        [((r,), 0, pages) for r in near] + [((r,), split, pages - split) for r in far],
        cap,
        WORK,
    )
    pieces[1:group], rest, stay, across = lax.optimization_barrier(
        (pieces[1:group], rest, stay, across)
    )
    early = jnp.stack(pieces[:group])
    early = [early, exchange(early, "dp", 1)]
    late_offsets = [[2 * k + bit] for k in range(group, n_high) for bit in range(2)]

    pair = jnp.concatenate([routes, targets.reshape(pages, 1, wdev)], axis=1)
    meta_near = jnp.stack([pair, exchange(pair, "seq", 1)])
    table_near = tables(info, meta_near, flags, near, cap, pps, WORK)
    meta_far = jnp.concatenate([exchange(meta_near, "seq", 2 * k) for k in range(1, n_y)], axis=0)

    early, pieces[group:], table_near = lax.optimization_barrier(
        (early, pieces[group:], table_near)
    )
    late = [jnp.stack([piece]) for piece in pieces[group:]]

    early += [exchange(some, "seq", 1) for some in early]
    early, late[-1] = lax.optimization_barrier((early, late[-1]))
    weight = weights(
        info, patches, early, [[2 * k + bit for k in range(group)] for bit in range(2)], (), WORK
    )
    late = [x for piece in late for x in (piece, exchange(piece, "dp", 1))]
    late, weight = lax.optimization_barrier((late, weight))
    across = exchange(across, "seq", 1)
    late += [exchange(piece, "seq", 1) for piece in late]
    rest = [exchange(rows, "seq", r) for rows, r in zip(rest, far)]
    weight = weights(info, patches, late, late_offsets, [weight])
    run = functools.partial(run_pages, info, weight, patches)
    loss, *pair_near = run(table_near, [(stay, 0), (across, 0)], 0)
    word_loss = [loss[:, 0], exchange(loss[:, 1], "seq", 1)]

    both, meta_far, pair_near = lax.optimization_barrier((both, meta_far, pair_near))
    first = [pair for rows in both for pair in ((rows, 0), (exchange(rows, "seq", 1), 1))]
    before = [gradient(info, other, F32, n_y, [pair_near]) for other in range(2)]
    info, before = lax.optimization_barrier((info, before))
    table_far = tables(info, meta_far, flags, far, cap, pps)
    loss_a, *pair_a = run(table_far, first, 0)
    rest, pair_a = lax.optimization_barrier((rest, pair_a))
    loss_b, *pair_b = run(table_far, [(rows, 0) for rows in rest], split)
    losses = jnp.concatenate([loss_a, loss_b], axis=0)
    for i, r in enumerate(far):
        word_loss.append(exchange(losses[:, i], "seq", r))

    sent = gradient(info, 1, BF16, n_y, [pair_a, pair_b], [before[1]])
    kept = gradient(info, 0, F32, n_y, [pair_a, pair_b], [before[0]])
    form = (n_y, n_high, 2, shard_rows, width // n_seq)
    terms = [kept.reshape(form), exchange(sent, "seq", 1).reshape(form)]
    part = lambda i, j: sum(
        pick(t, (own["y"][i], None, own["low"][j])).astype(F32) for t in terms
    )
    total = part(0, 0)
    for i in range(n_y):
        for j in range(2):
            if i or j:
                total = total + exchange_both(part(i, j).astype(BF16), j, 2 * i)
    grad = pick(total, (own["high"][0],))
    for k in range(1, n_high):
        grad = grad + exchange(pick(total, (own["high"][k],)).astype(BF16), "dp", 2 * k)
    return (sum(word_loss), grad)


def solution(mesh):
    in_specs = (
        P("dp", "seq", None),
        P("dp", "seq", None),
        P("dp", None),
        P("dp", "seq", None),
        P("dp", "seq"),
        P("dp"),
        P("dp", None, None),
    )
    out_specs = (P("dp", "seq"), P("dp", "seq"))
    return jax.shard_map(local, mesh=mesh, in_specs=in_specs, out_specs=out_specs, check_vma=False)
```

```python
import functools
import math

import jax
import jax.numpy as jnp
from jax import lax
from jax.experimental import pallas as pl
from jax.experimental.pallas import tpu as pltpu
from jax.sharding import PartitionSpec as P

MARGIN_BLOCK_SIZE = 64
SHIFT = 6
VMEM_LIMIT = 16 * 1024 * 1024
WORK = 1<<31
MUCH = 1 << 35
ME, CORE, DP, COUNTS = 0, 1, 2, 3
TARGET, COEF = 0, 1
F32, BF16 = jnp.float32, jnp.bfloat16


def dot(a, b, contract=((1,), (0,))):
    return lax.dot_general(a, b, (contract, ((), ())), preferred_element_type=F32)


def iota(shape, axis):
    return lax.broadcasted_iota(jnp.int32, shape, axis)


def ranks(hits):
    n = hits.shape[1]
    before = (iota((n, n), 0) < iota((n, n), 1)).astype(BF16)
    return jnp.where(hits > 0, dot(hits.astype(BF16), before), -1.0)


def call(kernel, n_pages, in_specs, out_specs, out_shape, operands, scratch=(), aliases={}, flops=0):
    return pl.pallas_call(
        kernel,
        grid_spec=pltpu.PrefetchScalarGridSpec(
            num_scalar_prefetch=1,
            grid=(n_pages,),
            in_specs=in_specs,
            out_specs=out_specs,
            scratch_shapes=scratch,
        ),
        out_shape=out_shape,
        compiler_params=pltpu.CompilerParams(vmem_limit_bytes=VMEM_LIMIT),
        cost_estimate=pl.CostEstimate(flops=flops, bytes_accessed=0, transcendentals=0),
        input_output_aliases=aliases,
    )(*operands)


def page_of(array, first_page=0):
    rest = array.shape[1:]
    return pl.BlockSpec((1,) + rest, lambda p, info: (p + first_page,) + (0,) * len(rest))


def all_of(array):
    return pl.BlockSpec(array.shape, lambda p, info: (0,) * len(array.shape))


def pad_rows(n):
    return -(-n // 8) * 8


def stacked(rows):
    n, width = pad_rows(len(rows)), rows[0].shape[1]
    row = iota((n, width), 0)
    out = jnp.zeros((n, width), rows[0].dtype)
    for i, r in enumerate(rows):
        out = jnp.where(row == i, r, out)
    return out


def dispatch_kernel(plan, cap, info, routes, words, *outs):
    wdev = words.shape[1]
    slots = iota((cap, wdev), 0).astype(F32)
    by_page = {}
    for out, (offsets, first_page, n_pages) in zip(outs, plan):
        for p in range(n_pages):
            for i, offset in enumerate(offsets):
                by_page.setdefault(first_page + p, []).append((offset, out, i, p))
    tasks = [(page, *task) for page in by_page for task in by_page[page]]
    rank = ranks(
        stacked(
            [
                (routes[page] == jnp.bitwise_xor(info[ME], offset)).astype(F32)
                for page, offset, *_ in tasks
            ]
        )
    )
    n = 0
    for page, some in by_page.items():
        picks = [
            (slots == rank[n + i : n + i + 1]).astype(BF16) for i in range(len(some))
        ]
        rows = dot(jnp.concatenate(picks, axis=0), words[page]).astype(BF16)
        for i, (_, out, place, p) in enumerate(some):
            out[place, p] = rows[i * cap : (i + 1) * cap]
        n += len(some)


def dispatch(info, routes, words, plan, cap, flops=0):
    width = words.shape[2]
    out = [
        jax.ShapeDtypeStruct((len(offsets), n_pages, cap, width), BF16)
        for offsets, _, n_pages in plan
    ]
    return call(
        functools.partial(dispatch_kernel, plan, cap),
        1,
        [all_of(routes), all_of(words)],
        [all_of(o) for o in out],
        out,
        (info, routes, words),
        flops=flops,
    )


def table_kernel(offsets, cap, info, meta, flags, bias, table, rank_out):
    me = info[ME]
    n_homes, pages, _, wdev = meta.shape
    nblk, all_blk = flags.shape[1:]
    n_rows, pps = bias.shape[1:]
    slots = iota((cap, wdev), 0).astype(F32)
    rank = ranks(
        stacked(
            [
                (meta[i, p, 0:1, :] == me).astype(F32)
                for p in range(pages)
                for i in range(n_homes)
            ]
        )
    )
    first = me * (pps // MARGIN_BLOCK_SIZE)
    block = iota((all_blk, pps), 1) >> SHIFT
    spread = (iota((all_blk, pps), 0) == first + block).astype(BF16)
    place = iota((1, wdev), 1) + 1
    for p in range(pages):
        t, idx = [], []
        for i, offset in enumerate(offsets):
            own = rank[p * n_homes + i : p * n_homes + i + 1]
            rank_out[p, i : i + 1] = own
            target = meta[i, p, 1:2, :]
            values = stacked([target >> 6, target & 63, place >> 6, place & 63]).astype(F32)
            got = dot((slots == own).astype(BF16), values.astype(BF16), ((1,), (1,)))
            got = got.astype(jnp.int32)
            t.append(got[:, 0:1] * 64 + got[:, 1:2])
            at = got[:, 2:3] * 64 + got[:, 3:4]
            idx.append(jnp.where(at > 0, at - 1 + jnp.bitwise_xor(me, offset) * wdev, -1))
        t, idx = jnp.concatenate(t, axis=0), jnp.concatenate(idx, axis=0)
        word_block = jnp.maximum(idx, 0) >> SHIFT == iota((n_rows, nblk), 1)
        margin = dot(word_block.astype(BF16), flags[p].astype(BF16)).astype(BF16)
        hit = dot(margin, spread)
        own = iota((n_rows, pps), 1) >> SHIFT == t >> SHIFT
        bias[p] = jnp.where((hit > 0.5) | own, 0.0, -jnp.inf).astype(BF16)
        count = info[COUNTS + p]
        valid = (idx >= 0) & (idx < count)
        coef = jnp.where(valid, 64.0 / count.astype(F32), 0.0)
        lane = iota((n_rows, 128), 1)
        table[p] = jnp.where(lane == TARGET, t.astype(F32), jnp.where(lane == COEF, coef, 0.0))


def tables(info, meta, flags, offsets, cap, pps, flops=0):
    n_homes, pages, _, wdev = meta.shape
    out = [
        jax.ShapeDtypeStruct((pages, n_homes * cap, pps), BF16),
        jax.ShapeDtypeStruct((pages, n_homes * cap, 128), F32),
        jax.ShapeDtypeStruct((pages, pad_rows(n_homes), wdev), F32),
    ]
    return call(
        functools.partial(table_kernel, offsets, cap),
        1,
        [all_of(meta), all_of(flags)],
        [all_of(o) for o in out],
        out,
        (info, meta, flags),
        flops=flops,
    )


def half_kernel(info, proj, out):
    out[...] = proj[...]


def half_of(info, proj):
    rows, width = proj.shape
    out = jax.ShapeDtypeStruct((rows, width // 2), BF16)
    return call(
        half_kernel,
        1,
        [pl.BlockSpec((rows, width // 2), lambda p, info: (0, info[CORE]))],
        all_of(out),
        out,
        (info, proj),
        flops=MUCH,
    )


def weights_kernel(offsets, info, patches, *refs):
    gathered, (*before, out, proj, sems) = refs[: 2 * len(offsets)], refs[2 * len(offsets) :]
    half = proj.shape[1] // 2
    rows = gathered[0].shape[1]
    shards = [offset for some in offsets for offset in some]

    def copies():
        n = 0
        for core in range(2):
            at = 0
            for some, ref in zip(offsets, gathered[core * len(offsets) :]):
                for i in range(len(some)):
                    first = jnp.bitwise_xor(info[CORE], core) * half
                    to = proj.at[pl.ds(at * rows, rows), pl.ds(pl.multiple_of(first, half), half)]
                    yield pltpu.make_async_copy(ref.at[i], to, sems.at[n])
                    at, n = at + 1, n + 1

    @pl.when(pl.program_id(0) == 0)
    def _():
        started = list(copies())
        for copy in started:
            copy.start()
        for copy in started:
            copy.wait()

    for other in before:
        out[...] = other[...]
    got = dot(proj[...], patches[0], ((1,), (1,))).astype(BF16)
    for i, offset in enumerate(shards):
        to = pl.multiple_of(jnp.bitwise_xor(info[DP], offset) * rows, rows)
        out[0, pl.ds(to, rows)] = got[i * rows : (i + 1) * rows]


def weights(info, patches, gathered, offsets, before=(), flops=0):
    pages, pps, width = patches.shape
    n_shards = sum(len(some) for some in offsets)
    out = jax.ShapeDtypeStruct((pages, width, pps), BF16)
    return call(
        functools.partial(weights_kernel, offsets),
        pages,
        [page_of(patches)]
        + [pl.BlockSpec(memory_space=pl.ANY)] * len(gathered)
        + [page_of(b) for b in before],
        page_of(out),
        out,
        (info, patches, *gathered, *before),
        [
            pltpu.VMEM((n_shards * gathered[0].shape[1], width), BF16),
            pltpu.SemaphoreType.DMA((2 * n_shards,)),
        ],
        flops=flops,
    )


def page_kernel(n_homes, cut, info, bias, table, rank, weight, patches, *refs):
    *words, loss, x_t, dq = refs
    pps, width = patches.shape[1:]
    cap = words[0].shape[2]
    n_rows = n_homes * cap
    scale = 2.0 / math.sqrt(width)
    x = jnp.concatenate([w[0, 0] for w in words], axis=0)
    scores = dot(x, weight[0]) * scale
    is_target = iota((n_rows, pps), 1) == table[0, :, TARGET : TARGET + 1].astype(jnp.int32)
    coef = table[0, :, COEF : COEF + 1]
    masked = scores + bias[0].astype(F32)
    top = jnp.max(masked, axis=1, keepdims=True)
    expo = jnp.exp(masked - top)
    total = jnp.sum(expo, axis=1, keepdims=True)
    target_score = jnp.sum(jnp.where(is_target, scores, 0.0), axis=1, keepdims=True)
    row_loss = jnp.where(coef > 0, top + jnp.log(total) - target_score, 0.0)
    share = expo * (1.0 / total)
    dscore = (coef * jnp.where(is_target, share - 1.0, share)).astype(BF16)
    back = (dot(dscore, patches[0]) * scale).astype(BF16)
    more = dq.shape[0] - n_rows
    if more:
        back = jnp.concatenate([back, jnp.zeros((more, width), BF16)], axis=0)
        x = jnp.concatenate([x, jnp.zeros((more, width), BF16)], axis=0)
    dq[...] = back
    slots = iota((cap, rank.shape[2]), 0).astype(F32)
    for r in range(n_homes):
        picked = jnp.where(slots == rank[0, r : r + 1, :], row_loss[r * cap : (r + 1) * cap], 0.0)
        loss[0, r : r + 1, :] = jnp.sum(picked, axis=0, keepdims=True)
    t = x.T
    for part in range(width // cut):
        to = part % 2 * (width // 2) + part // 2 * cut
        x_t[to : to + cut] = t[part * cut : (part + 1) * cut]


def run_pages(cut, info, weight, patches, table, words, first_page):
    _, n_pages, cap, width = words[0][0].shape
    wdev = table[2].shape[2]
    n_homes = len(words)
    n_rows = -(-n_homes * cap // 128) * 128
    out = [
        jax.ShapeDtypeStruct((n_pages, n_homes, wdev), F32),
        jax.ShapeDtypeStruct((width, n_pages * n_rows), BF16),
        jax.ShapeDtypeStruct((n_pages * n_rows, width), BF16),
    ]
    inputs = (*table, weight, patches)
    return call(
        functools.partial(page_kernel, n_homes, cut),
        n_pages,
        [page_of(a, first_page) for a in inputs]
        + [pl.BlockSpec((1, 1, cap, width), lambda p, info, i=i: (i, p, 0, 0)) for _, i in words],
        [
            page_of(out[0]),
            pl.BlockSpec((width, n_rows), lambda p, info: (0, p)),
            pl.BlockSpec((n_rows, width), lambda p, info: (p, 0)),
        ],
        out,
        (info, *inputs, *(w for w, _ in words)),
    )


def gradient_kernel(n_pairs, info, *refs):
    pairs, (*before, out) = refs[: 2 * n_pairs], refs[2 * n_pairs :]
    got = sum(dot(pairs[i][...], pairs[i + 1][...]) for i in range(0, len(pairs), 2))
    for part in before:
        got = got + part[0]
    out[0] = got.astype(out.dtype)


def gradient(info, dtype, n_y, pairs, cores, half=None, before=(), flops=0):
    width = pairs[0][0].shape[0]
    wcol = width // (2 * n_y)
    rows, at = (width, 0) if half is None else (width // 2, half)
    out = jax.ShapeDtypeStruct((len(cores) * n_y, rows, wcol), dtype)

    def column(i, info):
        core = cores[0] if len(cores) == 1 else jnp.where(i < n_y, cores[0], cores[1])
        return 0, 2 * (i % n_y) + jnp.bitwise_xor(info[CORE], core)

    specs = []
    for x_t, dq in pairs:
        specs.append(pl.BlockSpec((rows, x_t.shape[1]), lambda i, info: (at, 0)))
        specs.append(pl.BlockSpec((dq.shape[0], wcol), column))
    if before:
        total, first = before
        specs.append(pl.BlockSpec((1, rows, wcol), lambda i, info: (first + i, at, 0)))
    return call(
        functools.partial(gradient_kernel, len(pairs)),
        len(cores) * n_y,
        specs,
        page_of(out),
        out,
        (info, *(x for pair in pairs for x in pair), *before[:1]),
        flops=flops,
    )


def exchange(x, axis, offset):
    n = lax.axis_size(axis)
    return lax.ppermute(x, axis, [(i, i ^ offset) for i in range(n)])


def exchange_both(x, dp, seq):
    n_seq = lax.axis_size("seq")
    n = lax.axis_size("dp") * n_seq
    return lax.ppermute(x, ("dp", "seq"), [(i, i ^ (dp * n_seq + seq)) for i in range(n)])


def pick(x, places):
    places = list(places) + [None] * (x.ndim - len(places))
    start = [0 if i is None else i for i in places]
    size = [n if i is None else 1 for i, n in zip(places, x.shape)]
    got = lax.dynamic_slice(x, start, size, allow_negative_indices=False)
    return got.reshape([n for i, n in zip(places, x.shape) if i is None])


def local(words, patches, proj, routes, targets, counts, flags):
    pages, wdev, width = words.shape
    pps = patches.shape[1]
    n_seq = lax.axis_size("seq")
    n_dp = lax.axis_size("dp")
    n_y, n_high = n_seq // 2, n_dp // 2
    cap = 2 * wdev // n_seq
    shard_rows = proj.shape[0]
    near, far = (0, 1), tuple(range(2, n_seq))

    me, my_dp = lax.axis_index("seq"), lax.axis_index("dp")
    core, y, low, high = me & 1, me >> 1, my_dp & 1, my_dp >> 1
    own = {
        "low": [low ^ k for k in range(2)],
        "y": [y ^ k for k in range(n_y)],
        "high": [high ^ k for k in range(n_high)],
    }
    info = jnp.concatenate([jnp.stack([me, core, my_dp]).astype(jnp.int32), counts])
    info, own, proj = lax.optimization_barrier((info, own, proj))
    routes = routes.reshape(pages, 1, wdev)

    split = pages - 1
    both = dispatch(
        info, routes, words, [((2 * k, 2 * k + 1), 0, split) for k in range(1, n_y)], cap
    )
    info, proj, both = lax.optimization_barrier((info, proj, both))
    both = [exchange(rows, "seq", 2 * (k + 1)) for k, rows in enumerate(both)]
    piece = half_of(info, proj)
    pieces = [piece] + [exchange(piece, "dp", 2 * k) for k in range(1, n_high)]
    group = n_high // 2
    stay, across, *rest = dispatch(
        info,
        routes,
        words,
        [((r,), 0, pages) for r in near] + [((r,), split, pages - split) for r in far],
        cap,
        WORK,
    )
    pieces[1:group], rest, stay, across = lax.optimization_barrier(
        (pieces[1:group], rest, stay, across)
    )
    early = jnp.stack(pieces[:group])
    early = [early, exchange(early, "dp", 1)]
    late_offsets = [[2 * k + bit] for k in range(group, n_high) for bit in range(2)]

    pair = jnp.concatenate([routes, targets.reshape(pages, 1, wdev)], axis=1)
    meta_near = jnp.stack([pair, exchange(pair, "seq", 1)])
    table_near = tables(info, meta_near, flags, near, cap, pps, WORK)
    meta_far = jnp.concatenate([exchange(meta_near, "seq", 2 * k) for k in range(1, n_y)], axis=0)

    early, pieces[group:], table_near = lax.optimization_barrier(
        (early, pieces[group:], table_near)
    )
    late = [jnp.stack([piece]) for piece in pieces[group:]]

    early += [exchange(some, "seq", 1) for some in early]
    early, late[-1] = lax.optimization_barrier((early, late[-1]))
    weight = weights(
        info, patches, early, [[2 * k + bit for k in range(group)] for bit in range(2)], (), WORK
    )
    late = [x for piece in late for x in (piece, exchange(piece, "dp", 1))]
    late, weight = lax.optimization_barrier((late, weight))
    across = exchange(across, "seq", 1)
    late += [exchange(piece, "seq", 1) for piece in late]
    rest = [exchange(rows, "seq", r) for rows, r in zip(rest, far)]
    weight = weights(info, patches, late, late_offsets, [weight])
    run = functools.partial(run_pages, shard_rows // 2, info, weight, patches)
    loss, *pair_near = run(table_near, [(stay, 0), (across, 0)], 0)
    near_loss = loss[:, 0] + exchange(loss[:, 1], "seq", 1)

    both, meta_far, pair_near = lax.optimization_barrier((both, meta_far, pair_near))
    first = [pair for rows in both for pair in ((rows, 0), (exchange(rows, "seq", 1), 1))]
    before = gradient(info, F32, n_y, [pair_near], (1, 0))
    info, before = lax.optimization_barrier((info, before))
    table_far = tables(info, meta_far, flags, far, cap, pps)
    loss_a, *pair_a = run(table_far, first, 0)
    rest, pair_a, near_loss = lax.optimization_barrier((rest, pair_a, near_loss))
    loss_b, *pair_b = run(table_far, [(rows, 0) for rows in rest], split)
    losses = jnp.concatenate([loss_a, loss_b], axis=0)
    far_loss = [exchange(losses[:, i], "seq", r) for i, r in enumerate(far)]

    form = (n_y, n_high, 2, shard_rows // 2, width // n_seq)
    pairs = [pair_a, pair_b]
    grads = []
    for half in range(2):
        sent = gradient(info, BF16, n_y, pairs, (1,), half, (before, 0), half * MUCH)
        info, sent = lax.optimization_barrier((info, sent))
        if half:
            far_loss, sent = lax.optimization_barrier((far_loss, sent))
        kept = gradient(info, F32, n_y, pairs, (0,), half, (before, n_y), MUCH)
        terms = [kept.reshape(form), exchange(sent, "seq", 1).reshape(form)]
        parts = {
            (i, j): sum(pick(t, (own["y"][i], None, own["low"][j])).astype(F32) for t in terms)
            for i in range(n_y)
            for j in range(2)
        }
        leaving = {key: part.astype(BF16) for key, part in parts.items() if key != (0, 0)}
        info, leaving = lax.optimization_barrier((info, leaving))
        total = parts[0, 0]
        for (i, j), part in leaving.items():
            total = total + exchange_both(part, j, 2 * i)
        grad = pick(total, (own["high"][0],))
        for k in range(1, n_high):
            grad = grad + exchange(pick(total, (own["high"][k],)).astype(BF16), "dp", 2 * k)
        grads.append(grad)
    return (near_loss + sum(far_loss), jnp.concatenate(grads, axis=0))


def solution(mesh):
    in_specs = (
        P("dp", "seq", None),
        P("dp", "seq", None),
        P("dp", None),
        P("dp", "seq", None),
        P("dp", "seq"),
        P("dp"),
        P("dp", None, None),
    )
    out_specs = (P("dp", "seq"), P("dp", "seq"))
    return jax.shard_map(local, mesh=mesh, in_specs=in_specs, out_specs=out_specs, check_vma=False)
```

```python
import functools
import math

import jax
import jax.numpy as jnp
from jax import lax
from jax.experimental import pallas as pl
from jax.experimental.pallas import tpu as pltpu
from jax.sharding import PartitionSpec as P

MARGIN_BLOCK_SIZE = 64
SHIFT = 6
VMEM_LIMIT = 16 * 1024 * 1024
WORK = 1 << 28
MUCH = 1 << 35
ME, CORE, DP, COUNTS = 0, 1, 2, 3
TARGET, COEF = 0, 1
F32, BF16 = jnp.float32, jnp.bfloat16


def dot(a, b, contract=((1,), (0,))):
    return lax.dot_general(a, b, (contract, ((), ())), preferred_element_type=F32)


def iota(shape, axis):
    return lax.broadcasted_iota(jnp.int32, shape, axis)


def ranks(hits):
    n = hits.shape[1]
    before = (iota((n, n), 0) < iota((n, n), 1)).astype(BF16)
    return jnp.where(hits > 0, dot(hits.astype(BF16), before), -1.0)


def call(kernel, n_pages, in_specs, out_specs, out_shape, operands, scratch=(), aliases={}, flops=0):
    return pl.pallas_call(
        kernel,
        grid_spec=pltpu.PrefetchScalarGridSpec(
            num_scalar_prefetch=1,
            grid=(n_pages,),
            in_specs=in_specs,
            out_specs=out_specs,
            scratch_shapes=scratch,
        ),
        out_shape=out_shape,
        compiler_params=pltpu.CompilerParams(vmem_limit_bytes=VMEM_LIMIT),
        cost_estimate=pl.CostEstimate(flops=flops, bytes_accessed=0, transcendentals=0),
        input_output_aliases=aliases,
    )(*operands)


def page_of(array, first_page=0):
    rest = array.shape[1:]
    return pl.BlockSpec((1,) + rest, lambda p, info: (p + first_page,) + (0,) * len(rest))


def all_of(array):
    return pl.BlockSpec(array.shape, lambda p, info: (0,) * len(array.shape))


def pad_rows(n):
    return -(-n // 8) * 8


def stacked(rows):
    n, width = pad_rows(len(rows)), rows[0].shape[1]
    row = iota((n, width), 0)
    out = jnp.zeros((n, width), rows[0].dtype)
    for i, r in enumerate(rows):
        out = jnp.where(row == i, r, out)
    return out


def dispatch_kernel(plan, cap, info, routes, words, *outs):
    wdev = words.shape[1]
    slots = iota((cap, wdev), 0).astype(F32)
    by_page = {}
    for out, (offsets, first_page, n_pages) in zip(outs, plan):
        for p in range(n_pages):
            for i, offset in enumerate(offsets):
                by_page.setdefault(first_page + p, []).append((offset, out, i, p))
    tasks = [(page, *task) for page in by_page for task in by_page[page]]
    rank = ranks(
        stacked(
            [
                (routes[page] == jnp.bitwise_xor(info[ME], offset)).astype(F32)
                for page, offset, *_ in tasks
            ]
        )
    )
    n = 0
    for page, some in by_page.items():
        picks = [
            (slots == rank[n + i : n + i + 1]).astype(BF16) for i in range(len(some))
        ]
        rows = dot(jnp.concatenate(picks, axis=0), words[page]).astype(BF16)
        for i, (_, out, place, p) in enumerate(some):
            out[place, p] = rows[i * cap : (i + 1) * cap]
        n += len(some)


def dispatch(info, routes, words, plan, cap, flops=0):
    width = words.shape[2]
    out = [
        jax.ShapeDtypeStruct((len(offsets), n_pages, cap, width), BF16)
        for offsets, _, n_pages in plan
    ]
    return call(
        functools.partial(dispatch_kernel, plan, cap),
        1,
        [all_of(routes), all_of(words)],
        [all_of(o) for o in out],
        out,
        (info, routes, words),
        flops=flops,
    )


def table_kernel(offsets, cap, info, meta, flags, bias, table, rank_out):
    me = info[ME]
    n_homes, pages, _, wdev = meta.shape
    nblk, all_blk = flags.shape[1:]
    n_rows, pps = bias.shape[1:]
    slots = iota((cap, wdev), 0).astype(F32)
    rank = ranks(
        stacked(
            [
                (meta[i, p, 0:1, :] == me).astype(F32)
                for p in range(pages)
                for i in range(n_homes)
            ]
        )
    )
    first = me * (pps // MARGIN_BLOCK_SIZE)
    block = iota((all_blk, pps), 1) >> SHIFT
    spread = (iota((all_blk, pps), 0) == first + block).astype(BF16)
    place = iota((1, wdev), 1) + 1
    for p in range(pages):
        t, idx = [], []
        for i, offset in enumerate(offsets):
            own = rank[p * n_homes + i : p * n_homes + i + 1]
            rank_out[p, i : i + 1] = own
            target = meta[i, p, 1:2, :]
            values = stacked([target >> 6, target & 63, place >> 6, place & 63]).astype(F32)
            got = dot((slots == own).astype(BF16), values.astype(BF16), ((1,), (1,)))
            got = got.astype(jnp.int32)
            t.append(got[:, 0:1] * 64 + got[:, 1:2])
            at = got[:, 2:3] * 64 + got[:, 3:4]
            idx.append(jnp.where(at > 0, at - 1 + jnp.bitwise_xor(me, offset) * wdev, -1))
        t, idx = jnp.concatenate(t, axis=0), jnp.concatenate(idx, axis=0)
        word_block = jnp.maximum(idx, 0) >> SHIFT == iota((n_rows, nblk), 1)
        margin = dot(word_block.astype(BF16), flags[p].astype(BF16)).astype(BF16)
        hit = dot(margin, spread)
        own = iota((n_rows, pps), 1) >> SHIFT == t >> SHIFT
        bias[p] = jnp.where((hit > 0.5) | own, 0.0, -jnp.inf).astype(BF16)
        count = info[COUNTS + p]
        valid = (idx >= 0) & (idx < count)
        coef = jnp.where(valid, 64.0 / count.astype(F32), 0.0)
        lane = iota((n_rows, 128), 1)
        table[p] = jnp.where(lane == TARGET, t.astype(F32), jnp.where(lane == COEF, coef, 0.0))


def tables(info, meta, flags, offsets, cap, pps, flops=0):
    n_homes, pages, _, wdev = meta.shape
    out = [
        jax.ShapeDtypeStruct((pages, n_homes * cap, pps), BF16),
        jax.ShapeDtypeStruct((pages, n_homes * cap, 128), F32),
        jax.ShapeDtypeStruct((pages, pad_rows(n_homes), wdev), F32),
    ]
    return call(
        functools.partial(table_kernel, offsets, cap),
        1,
        [all_of(meta), all_of(flags)],
        [all_of(o) for o in out],
        out,
        (info, meta, flags),
        flops=flops,
    )


def half_kernel(info, proj, out):
    out[...] = proj[...]


def half_of(info, proj, half):
    rows, width = proj.shape
    out = jax.ShapeDtypeStruct((rows, half), BF16)
    return call(
        half_kernel,
        1,
        [pl.BlockSpec((rows, half), lambda p, info: (0, info[CORE] if width > half else 0))],
        all_of(out),
        out,
        (info, proj),
        flops=MUCH,
    )


def weights_kernel(offsets, info, patches, *refs):
    gathered, (*before, out, proj, sems) = refs[: 2 * len(offsets)], refs[2 * len(offsets) :]
    half = proj.shape[1] // 2
    rows = gathered[0].shape[1]
    shards = [offset for some in offsets for offset in some]

    def copies():
        n = 0
        for core in range(2):
            at = 0
            for some, ref in zip(offsets, gathered[core * len(offsets) :]):
                for i in range(len(some)):
                    first = jnp.bitwise_xor(info[CORE], core) * half
                    to = proj.at[pl.ds(at * rows, rows), pl.ds(pl.multiple_of(first, half), half)]
                    yield pltpu.make_async_copy(ref.at[i], to, sems.at[n])
                    at, n = at + 1, n + 1

    @pl.when(pl.program_id(0) == 0)
    def _():
        started = list(copies())
        for copy in started:
            copy.start()
        for copy in started:
            copy.wait()

    for other in before:
        out[...] = other[...]
    got = dot(proj[...], patches[0], ((1,), (1,))).astype(BF16)
    for i, offset in enumerate(shards):
        to = pl.multiple_of(jnp.bitwise_xor(info[DP], offset) * rows, rows)
        out[0, pl.ds(to, rows)] = got[i * rows : (i + 1) * rows]


def weights(info, patches, gathered, offsets, before=(), flops=0):
    pages, pps, width = patches.shape
    n_shards = sum(len(some) for some in offsets)
    out = jax.ShapeDtypeStruct((pages, width, pps), BF16)
    return call(
        functools.partial(weights_kernel, offsets),
        pages,
        [page_of(patches)]
        + [pl.BlockSpec(memory_space=pl.ANY)] * len(gathered)
        + [page_of(b) for b in before],
        page_of(out),
        out,
        (info, patches, *gathered, *before),
        [
            pltpu.VMEM((n_shards * gathered[0].shape[1], width), BF16),
            pltpu.SemaphoreType.DMA((2 * n_shards,)),
        ],
        flops=flops,
    )


def page_kernel(n_homes, info, bias, table, rank, weight, patches, *refs):
    *words, loss, x_t, dq = refs
    pps, width = patches.shape[1:]
    cap = words[0].shape[2]
    n_rows = n_homes * cap
    scale = 2.0 / math.sqrt(width)
    x = jnp.concatenate([w[0, 0] for w in words], axis=0)
    scores = dot(x, weight[0]) * scale
    is_target = iota((n_rows, pps), 1) == table[0, :, TARGET : TARGET + 1].astype(jnp.int32)
    coef = table[0, :, COEF : COEF + 1]
    masked = scores + bias[0].astype(F32)
    top = jnp.max(masked, axis=1, keepdims=True)
    expo = jnp.exp(masked - top)
    total = jnp.sum(expo, axis=1, keepdims=True)
    target_score = jnp.sum(jnp.where(is_target, scores, 0.0), axis=1, keepdims=True)
    row_loss = jnp.where(coef > 0, top + jnp.log(total) - target_score, 0.0)
    share = expo * (1.0 / total)
    dscore = (coef * jnp.where(is_target, share - 1.0, share)).astype(BF16)
    back = (dot(dscore, patches[0]) * scale).astype(BF16)
    more = dq.shape[0] - n_rows
    if more:
        back = jnp.concatenate([back, jnp.zeros((more, width), BF16)], axis=0)
        x = jnp.concatenate([x, jnp.zeros((more, width), BF16)], axis=0)
    dq[...] = back
    slots = iota((cap, rank.shape[2]), 0).astype(F32)
    for r in range(n_homes):
        picked = jnp.where(slots == rank[0, r : r + 1, :], row_loss[r * cap : (r + 1) * cap], 0.0)
        loss[0, r : r + 1, :] = jnp.sum(picked, axis=0, keepdims=True)
    x_t[...] = x.T


def run_pages(info, weight, patches, table, words, first_page):
    _, n_pages, cap, width = words[0][0].shape
    wdev = table[2].shape[2]
    n_homes = len(words)
    n_rows = -(-n_homes * cap // 128) * 128
    out = [
        jax.ShapeDtypeStruct((n_pages, n_homes, wdev), F32),
        jax.ShapeDtypeStruct((width, n_pages * n_rows), BF16),
        jax.ShapeDtypeStruct((n_pages * n_rows, width), BF16),
    ]
    inputs = (*table, weight, patches)
    return call(
        functools.partial(page_kernel, n_homes),
        n_pages,
        [page_of(a, first_page) for a in inputs]
        + [pl.BlockSpec((1, 1, cap, width), lambda p, info, i=i: (i, p, 0, 0)) for _, i in words],
        [
            page_of(out[0]),
            pl.BlockSpec((width, n_rows), lambda p, info: (0, p)),
            pl.BlockSpec((n_rows, width), lambda p, info: (p, 0)),
        ],
        out,
        (info, *inputs, *(w for w, _ in words)),
    )


def gradient_kernel(n_pairs, info, *refs):
    *pairs, out = refs
    got = sum(dot(pairs[i][...], pairs[i + 1][...]) for i in range(0, 2 * n_pairs, 2))
    out[0] = got.astype(out.dtype)


def gradient(info, other, dtype, n_y, pairs, flops=0):
    width = pairs[0][0].shape[0]
    wcol = width // (2 * n_y)
    out = jax.ShapeDtypeStruct((n_y, width, wcol), dtype)
    column = lambda y, info: (0, 2 * y + jnp.bitwise_xor(info[CORE], other))
    specs = []
    for x_t, dq in pairs:
        specs += [all_of(x_t), pl.BlockSpec((dq.shape[0], wcol), column)]
    return call(
        functools.partial(gradient_kernel, len(pairs)),
        n_y,
        specs,
        page_of(out),
        out,
        (info, *(x for pair in pairs for x in pair)),
        flops=flops,
    )


def exchange(x, axis, offset):
    n = lax.axis_size(axis)
    return lax.ppermute(x, axis, [(i, i ^ offset) for i in range(n)])


def exchange_both(x, dp, seq):
    n_seq = lax.axis_size("seq")
    n = lax.axis_size("dp") * n_seq
    return lax.ppermute(x, ("dp", "seq"), [(i, i ^ (dp * n_seq + seq)) for i in range(n)])


def pick(x, places):
    places = list(places) + [None] * (x.ndim - len(places))
    start = [0 if i is None else i for i in places]
    size = [n if i is None else 1 for i, n in zip(places, x.shape)]
    got = lax.dynamic_slice(x, start, size, allow_negative_indices=False)
    return got.reshape([n for i, n in zip(places, x.shape) if i is None])


def local(words, patches, proj, routes, targets, counts, flags):
    pages, wdev, width = words.shape
    pps = patches.shape[1]
    n_seq = lax.axis_size("seq")
    n_dp = lax.axis_size("dp")
    n_y, n_high = n_seq // 2, n_dp // 2
    cap = 2 * wdev // n_seq
    shard_rows = proj.shape[0]
    near, far = (0, 1), tuple(range(2, n_seq))

    me, my_dp = lax.axis_index("seq"), lax.axis_index("dp")
    core, y, low, high = me & 1, me >> 1, my_dp & 1, my_dp >> 1
    own = {
        "low": [low ^ k for k in range(2)],
        "y": [y ^ k for k in range(n_y)],
        "high": [high ^ k for k in range(n_high)],
    }
    info = jnp.concatenate([jnp.stack([me, core, my_dp]).astype(jnp.int32), counts])
    info, own, proj = lax.optimization_barrier((info, own, proj))
    routes = routes.reshape(pages, 1, wdev)

    pair = jnp.concatenate([routes, targets.reshape(pages, 1, wdev)], axis=1)
    metas = [pair] + [exchange(pair, "seq", r) for r in range(1, n_seq)]
    info, metas = lax.optimization_barrier((info, metas))
    meta_near, meta_far = jnp.stack(metas[:2]), jnp.stack(metas[2:])

    split = pages - 1
    first = dispatch(info, routes, words, [((r,), 0, split) for r in far], cap)
    info, proj, first = lax.optimization_barrier((info, proj, first))
    first = [exchange(rows, "seq", r) for rows, r in zip(first, far)]

    piece = half_of(info, proj, width // 2)
    again = half_of(info, piece, width // 2)
    pieces = [piece] + [exchange(piece if k == 1 else again, "dp", 2 * k) for k in range(1, n_high)]
    group = n_high // 2

    stay, across, *rest = dispatch(
        info,
        routes,
        words,
        [((r,), 0, pages) for r in near] + [((r,), split, pages - split) for r in far],
        cap,
        WORK,
    )
    pieces[1:group], rest, stay, across = lax.optimization_barrier(
        (pieces[1:group], rest, stay, across)
    )
    early = jnp.stack(pieces[:group])
    early = [early, exchange(early, "dp", 1)]
    late_offsets = [[2 * k + bit] for k in range(group, n_high) for bit in range(2)]
    table_near = tables(info, meta_near, flags, near, cap, pps, WORK)
    table_far = tables(info, meta_far, flags, far, cap, pps, WORK)
    early, pieces[group:], table_near, table_far = lax.optimization_barrier(
        (early, pieces[group:], table_near, table_far)
    )
    late = [jnp.stack([piece]) for piece in pieces[group:]]

    early += [exchange(some, "seq", 1) for some in early]
    early, late[-1], first[0] = lax.optimization_barrier((early, late[-1], first[0]))
    weight = weights(
        info, patches, early, [[2 * k + bit for k in range(group)] for bit in range(2)], (), WORK
    )
    late = [x for piece in late for x in (piece, exchange(piece, "dp", 1))]
    late, weight = lax.optimization_barrier((late, weight))
    across = exchange(across, "seq", 1)
    late += [exchange(piece, "seq", 1) for piece in late]
    rest = [exchange(rows, "seq", r) for rows, r in zip(rest, far)]
    weight = weights(info, patches, late, late_offsets, [weight])

    run = functools.partial(run_pages, info, weight, patches)
    loss, *pair_near = run(table_near, [(stay, 0), (across, 0)], 0)
    near_loss = loss[:, 0] + exchange(loss[:, 1], "seq", 1)
    first, pair_near = lax.optimization_barrier((first, pair_near))
    loss_a, *pair_a = run(table_far, [(rows, 0) for rows in first], 0)
    rest, pair_a, near_loss = lax.optimization_barrier((rest, pair_a, near_loss))
    loss_b, *pair_b = run(table_far, [(rows, 0) for rows in rest], split)
    losses = jnp.concatenate([loss_a, loss_b], axis=0)
    far_loss = [exchange(losses[:, i], "seq", r) for i, r in enumerate(far)]

    pairs = [pair_near, pair_a, pair_b]
    sent = gradient(info, 1, BF16, n_y, pairs)
    kept = gradient(info, 0, F32, n_y, pairs, MUCH)
    form = (n_y, n_high, 2, shard_rows, width // n_seq)
    terms = [kept.reshape(form), exchange(sent, "seq", 1).reshape(form)]
    part = lambda i, j: sum(
        pick(t, (own["y"][i], None, own["low"][j])).astype(F32) for t in terms
    )
    total = part(0, 0)
    for i in range(n_y):
        for j in range(2):
            if i or j:
                total = total + exchange_both(part(i, j).astype(BF16), j, 2 * i)
    grad = pick(total, (own["high"][0],))
    for k in range(1, n_high):
        grad = grad + exchange(pick(total, (own["high"][k],)).astype(BF16), "dp", 2 * k)
    return (near_loss + sum(far_loss), grad)


def solution(mesh):
    in_specs = (
        P("dp", "seq", None),
        P("dp", "seq", None),
        P("dp", None),
        P("dp", "seq", None),
        P("dp", "seq"),
        P("dp"),
        P("dp", None, None),
    )
    out_specs = (P("dp", "seq"), P("dp", "seq"))
    return jax.shard_map(local, mesh=mesh, in_specs=in_specs, out_specs=out_specs, check_vma=False)
```

```python
import functools
import math

import jax
import jax.numpy as jnp
from jax import lax
from jax.experimental import pallas as pl
from jax.experimental.pallas import tpu as pltpu
from jax.sharding import PartitionSpec as P

MARGIN_BLOCK_SIZE = 64
SHIFT = 6
VMEM_LIMIT = 16 * 1024 * 1024
WORK = 1 << 30
MUCH = 1 << 35
ME, CORE, DP, COUNTS = 0, 1, 2, 3
TARGET, COEF, BLOCKS = 0, 1, 2
F32, BF16 = jnp.float32, jnp.bfloat16


def dot(a, b, contract=((1,), (0,))):
    return lax.dot_general(a, b, (contract, ((), ())), preferred_element_type=F32)


def iota(shape, axis):
    return lax.broadcasted_iota(jnp.int32, shape, axis)


def ranks(hits):
    n = hits.shape[1]
    before = (iota((n, n), 0) < iota((n, n), 1)).astype(BF16)
    return jnp.where(hits > 0, dot(hits.astype(BF16), before), -1.0)


def call(kernel, n_pages, in_specs, out_specs, out_shape, operands, scratch=(), aliases={}, flops=0):
    return pl.pallas_call(
        kernel,
        grid_spec=pltpu.PrefetchScalarGridSpec(
            num_scalar_prefetch=1,
            grid=(n_pages,),
            in_specs=in_specs,
            out_specs=out_specs,
            scratch_shapes=scratch,
        ),
        out_shape=out_shape,
        compiler_params=pltpu.CompilerParams(vmem_limit_bytes=VMEM_LIMIT),
        cost_estimate=pl.CostEstimate(flops=flops, bytes_accessed=0, transcendentals=0),
        input_output_aliases=aliases,
    )(*operands)


def page_of(array, first_page=0):
    rest = array.shape[1:]
    return pl.BlockSpec((1,) + rest, lambda p, info: (p + first_page,) + (0,) * len(rest))


def all_of(array):
    return pl.BlockSpec(array.shape, lambda p, info: (0,) * len(array.shape))


def pad_rows(n):
    return -(-n // 8) * 8


def stacked(rows):
    n, width = -(-len(rows) // 8) * 8, rows[0].shape[1]
    row = iota((n, width), 0)
    out = jnp.zeros((n, width), rows[0].dtype)
    for i, r in enumerate(rows):
        out = jnp.where(row == i, r, out)
    return out


def dispatch_kernel(plan, cap, labels, info, routes, words, *outs):
    if labels:
        targets, *outs = outs
    wdev = words.shape[1]
    slots = iota((cap, wdev), 0).astype(F32)
    by_page = {}
    for out, (offsets, first_page, n_pages) in zip(outs, plan):
        for p in range(n_pages):
            for i, offset in enumerate(offsets):
                by_page.setdefault(first_page + p, []).append((offset, out, i, p))
    tasks = [(page, *task) for page in by_page for task in by_page[page]]
    rank = ranks(
        stacked(
            [
                (routes[page] == jnp.bitwise_xor(info[ME], offset)).astype(F32)
                for page, offset, *_ in tasks
            ]
        )
    )
    n = 0
    for page, some in by_page.items():
        picks = [
            (slots == rank[n + i : n + i + 1]).astype(BF16) for i in range(len(some))
        ]
        rows = dot(jnp.concatenate(picks, axis=0), words[page]).astype(BF16)
        for i, (_, out, place, p) in enumerate(some):
            here = rows[i * cap : (i + 1) * cap]
            if labels:
                out[place, p * cap : (p + 1) * cap] = here
            else:
                out[place, p] = here
        n += len(some)
    if labels:
        block = stacked(
            [
                part.astype(F32)
                for page in range(words.shape[0])
                for part in (routes[page], targets[page] >> 6, targets[page] & 63)
            ]
        )
        block = jnp.concatenate(
            [block, jnp.zeros((block.shape[0], words.shape[2] - wdev), F32)], axis=1
        ).astype(BF16)
        for out in outs:
            for place in range(out.shape[0]):
                out[place, out.shape[1] - block.shape[0] :] = block


def label_rows(pages):
    return -(-3 * pages // 16) * 16


def dispatch(info, routes, words, plan, cap, targets=None, flops=0):
    pages, _, width = words.shape
    labels = targets is not None
    out = [
        jax.ShapeDtypeStruct(
            (len(offsets), n_pages * cap + label_rows(pages), width)
            if labels
            else (len(offsets), n_pages, cap, width),
            BF16,
        )
        for offsets, _, n_pages in plan
    ]
    operands = (routes, words) + ((targets,) if labels else ())
    return call(
        functools.partial(dispatch_kernel, plan, cap, labels),
        1,
        [all_of(x) for x in operands],
        [all_of(o) for o in out],
        out,
        (info, *operands),
        flops=flops,
    )


def table_kernel(offsets, cap, own_blk, info, *refs):
    *labels, flags, table, rank_out = refs
    me = info[ME]
    n_homes, pages, wdev = len(offsets), flags.shape[0], rank_out.shape[2]
    labels = [block[0].astype(F32)[:, :wdev] for block in labels]
    label = lambda i, p, part: labels[i][3 * p + part : 3 * p + part + 1]
    nblk, all_blk = flags.shape[1:]
    n_rows = table.shape[1]
    slots = iota((cap, wdev), 0).astype(F32)
    rank = ranks(
        stacked(
            [
                (label(i, p, 0) == me.astype(F32)).astype(F32)
                for p in range(pages)
                for i in range(n_homes)
            ]
        )
    )
    lane = iota((n_rows, 128), 1)
    own = iota((all_blk, 128), 1) - BLOCKS
    chosen = (own >= 0) & (own < own_blk) & (iota((all_blk, 128), 0) == me * own_blk + own)
    chosen = chosen.astype(BF16)
    place = iota((1, wdev), 1) + 1
    for p in range(pages):
        t, idx = [], []
        for i, offset in enumerate(offsets):
            own = rank[p * n_homes + i : p * n_homes + i + 1]
            rank_out[p, i : i + 1] = own
            values = [label(i, p, 1), label(i, p, 2), place >> 6, place & 63]
            values = stacked([v.astype(F32) for v in values])
            got = dot((slots == own).astype(BF16), values.astype(BF16), ((1,), (1,)))
            got = got.astype(jnp.int32)
            t.append(got[:, 0:1] * 64 + got[:, 1:2])
            at = got[:, 2:3] * 64 + got[:, 3:4]
            idx.append(jnp.where(at > 0, at - 1 + jnp.bitwise_xor(me, offset) * wdev, -1))
        t, idx = jnp.concatenate(t, axis=0), jnp.concatenate(idx, axis=0)
        word_block = jnp.maximum(idx, 0) >> SHIFT == iota((n_rows, nblk), 1)
        margin = dot(word_block.astype(BF16), flags[p].astype(BF16)).astype(BF16)
        allowed = (dot(margin, chosen) > 0.5) | (lane - BLOCKS == t >> SHIFT)
        count = info[COUNTS + p]
        valid = (idx >= 0) & (idx < count)
        coef = jnp.where(valid, 64.0 / count.astype(F32), 0.0)
        value = jnp.where(allowed, 1.0, 0.0)
        table[p] = jnp.where(lane == TARGET, t.astype(F32), jnp.where(lane == COEF, coef, value))


def tables(info, labels, flags, offsets, cap, pps, wdev, flops=0):
    pages, n_homes = flags.shape[0], len(offsets)
    rows = label_rows(pages)
    out = [
        jax.ShapeDtypeStruct((pages, n_homes * cap, 128), F32),
        jax.ShapeDtypeStruct((pages, pad_rows(n_homes), wdev), F32),
    ]
    ends = [
        pl.BlockSpec((1, rows, x.shape[2]), lambda p, info, at=x.shape[1] // rows - 1: (0, at, 0))
        for x in labels
    ]
    return call(
        functools.partial(table_kernel, offsets, cap, pps // MARGIN_BLOCK_SIZE),
        1,
        ends + [all_of(flags)],
        [all_of(o) for o in out],
        out,
        (info, *labels, flags),
        flops=flops,
    )


def half_kernel(info, proj, out):
    out[...] = proj[...]


def half_of(info, proj, half):
    rows, width = proj.shape
    out = jax.ShapeDtypeStruct((rows, half), BF16)
    return call(
        half_kernel,
        1,
        [pl.BlockSpec((rows, half), lambda p, info: (0, info[CORE] if width > half else 0))],
        all_of(out),
        out,
        (info, proj),
        flops=MUCH,
    )


def weights_kernel(offsets, info, patches, *refs):
    gathered, (*before, out, proj, sems) = refs[: 2 * len(offsets)], refs[2 * len(offsets) :]
    half = proj.shape[1] // 2
    rows = gathered[0].shape[1]
    shards = [offset for some in offsets for offset in some]

    def copies():
        n = 0
        for core in range(2):
            at = 0
            for some, ref in zip(offsets, gathered[core * len(offsets) :]):
                for i in range(len(some)):
                    first = jnp.bitwise_xor(info[CORE], core) * half
                    to = proj.at[pl.ds(at * rows, rows), pl.ds(pl.multiple_of(first, half), half)]
                    yield pltpu.make_async_copy(ref.at[i], to, sems.at[n])
                    at, n = at + 1, n + 1

    @pl.when(pl.program_id(0) == 0)
    def _():
        started = list(copies())
        for copy in started:
            copy.start()
        for copy in started:
            copy.wait()

    for other in before:
        out[...] = other[...]
    got = dot(proj[...], patches[0], ((1,), (1,))).astype(BF16)
    for i, offset in enumerate(shards):
        to = pl.multiple_of(jnp.bitwise_xor(info[DP], offset) * rows, rows)
        out[0, pl.ds(to, rows)] = got[i * rows : (i + 1) * rows]


def weights(info, patches, gathered, offsets, before=(), flops=0):
    pages, pps, width = patches.shape
    n_shards = sum(len(some) for some in offsets)
    out = jax.ShapeDtypeStruct((pages, width, pps), BF16)
    return call(
        functools.partial(weights_kernel, offsets),
        pages,
        [page_of(patches)]
        + [pl.BlockSpec(memory_space=pl.ANY)] * len(gathered)
        + [page_of(b) for b in before],
        page_of(out),
        out,
        (info, patches, *gathered, *before),
        [
            pltpu.VMEM((n_shards * gathered[0].shape[1], width), BF16),
            pltpu.SemaphoreType.DMA((2 * n_shards,)),
        ],
        flops=flops,
    )


def page_kernel(rows_of_rank, info, weight, patches, *refs):
    n_homes = len(rows_of_rank)
    tables, ranks_of, words = (refs[i * n_homes : (i + 1) * n_homes] for i in range(3))
    loss, x_t, dq = refs[3 * n_homes :]
    pps, width = patches.shape[1:]
    cap = words[0].shape[1]
    n_rows = n_homes * cap
    scale = 2.0 / math.sqrt(width)
    x = jnp.concatenate([w[0] for w in words], axis=0)
    scores = dot(x, weight[0]) * scale
    lanes = jnp.concatenate([t[0] for t in tables], axis=0)
    is_target = iota((n_rows, pps), 1) == lanes[:, TARGET : TARGET + 1].astype(jnp.int32)
    coef = lanes[:, COEF : COEF + 1]
    spread = iota((128, pps), 0) - BLOCKS == iota((128, pps), 1) >> SHIFT
    allowed = dot(jnp.where(iota(lanes.shape, 1) < BLOCKS, 0.0, lanes).astype(BF16), spread.astype(BF16))
    masked = jnp.where(allowed > 0.5, scores, -jnp.inf)
    top = jnp.max(masked, axis=1, keepdims=True)
    expo = jnp.exp(masked - top)
    total = jnp.sum(expo, axis=1, keepdims=True)
    target_score = jnp.sum(jnp.where(is_target, scores, 0.0), axis=1, keepdims=True)
    row_loss = jnp.where(coef > 0, top + jnp.log(total) - target_score, 0.0)
    share = expo * (1.0 / total)
    dscore = (coef * jnp.where(is_target, share - 1.0, share)).astype(BF16)
    back = (dot(dscore, patches[0]) * scale).astype(BF16)
    more = dq.shape[0] - n_rows
    if more:
        back = jnp.concatenate([back, jnp.zeros((more, width), BF16)], axis=0)
        x = jnp.concatenate([x, jnp.zeros((more, width), BF16)], axis=0)
    dq[...] = back
    slots = iota((cap, loss.shape[2]), 0).astype(F32)
    for r, row in enumerate(rows_of_rank):
        rank = ranks_of[r][0, row : row + 1, :]
        picked = jnp.where(slots == rank, row_loss[r * cap : (r + 1) * cap], 0.0)
        loss[0, r : r + 1, :] = jnp.sum(picked, axis=0, keepdims=True)
    x_t[...] = x.T


def run_pages(info, weight, patches, homes):
    pages, _, width = patches.shape
    wdev = homes[0][1][1].shape[2]
    n_homes = len(homes)
    cap = homes[0][2][1]
    n_rows = -(-n_homes * cap // 128) * 128
    out = [
        jax.ShapeDtypeStruct((pages, n_homes, wdev), F32),
        jax.ShapeDtypeStruct((width, pages * n_rows), BF16),
        jax.ShapeDtypeStruct((pages * n_rows, width), BF16),
    ]
    return call(
        functools.partial(page_kernel, [at for *_, (at, _) in homes]),
        pages,
        [page_of(weight), page_of(patches)]
        + [pl.BlockSpec((1, cap, 128), lambda p, info, at=at: (p, at, 0)) for *_, (at, _) in homes]
        + [page_of(table[1]) for _, table, _ in homes]
        + [pl.BlockSpec((1, cap, width), lambda p, info: (0, p, 0))] * n_homes,
        [
            page_of(out[0]),
            pl.BlockSpec((width, n_rows), lambda p, info: (0, p)),
            pl.BlockSpec((n_rows, width), lambda p, info: (p, 0)),
        ],
        out,
        (
            info,
            weight,
            patches,
            *(table[0] for _, table, _ in homes),
            *(table[1] for _, table, _ in homes),
            *(rows for rows, _, _ in homes),
        ),
    )


def gradient_kernel(n_pairs, info, *refs):
    pairs, (*before, out) = refs[: 2 * n_pairs], refs[2 * n_pairs :]
    got = sum(dot(pairs[i][...], pairs[i + 1][...]) for i in range(0, 2 * n_pairs, 2))
    for part in before:
        got = got + part[0]
    out[0] = got.astype(out.dtype)


def gradient(info, dtype, n_y, pairs, cores, before=(), flops=0):
    width = pairs[0][0].shape[0]
    wcol = width // (2 * n_y)
    out = jax.ShapeDtypeStruct((len(cores) * n_y, width, wcol), dtype)

    def column(i, info):
        core = cores[0] if len(cores) == 1 else jnp.where(i < n_y, cores[0], cores[1])
        return 0, 2 * (i % n_y) + jnp.bitwise_xor(info[CORE], core)

    specs = []
    for x_t, dq in pairs:
        specs += [all_of(x_t), pl.BlockSpec((dq.shape[0], wcol), column)]
    if before:
        first = before[1]
        specs.append(pl.BlockSpec((1, width, wcol), lambda i, info: (first + i, 0, 0)))
    return call(
        functools.partial(gradient_kernel, len(pairs)),
        len(cores) * n_y,
        specs,
        page_of(out),
        out,
        (info, *(x for pair in pairs for x in pair), *before[:1]),
        flops=flops,
    )


def exchange(x, axis, offset):
    n = lax.axis_size(axis)
    return lax.ppermute(x, axis, [(i, i ^ offset) for i in range(n)])


def exchange_both(x, dp, seq):
    n_seq = lax.axis_size("seq")
    n = lax.axis_size("dp") * n_seq
    return lax.ppermute(x, ("dp", "seq"), [(i, i ^ (dp * n_seq + seq)) for i in range(n)])


def pick(x, places):
    places = list(places) + [None] * (x.ndim - len(places))
    start = [0 if i is None else i for i in places]
    size = [n if i is None else 1 for i, n in zip(places, x.shape)]
    got = lax.dynamic_slice(x, start, size, allow_negative_indices=False)
    return got.reshape([n for i, n in zip(places, x.shape) if i is None])


def local(words, patches, proj, routes, targets, counts, flags):
    pages, wdev, width = words.shape
    pps = patches.shape[1]
    n_seq = lax.axis_size("seq")
    n_dp = lax.axis_size("dp")
    n_y, n_high = n_seq // 2, n_dp // 2
    cap = 2 * wdev // n_seq
    shard_rows = proj.shape[0]
    near, far = (0, 1), tuple(range(2, n_seq))

    me, my_dp = lax.axis_index("seq"), lax.axis_index("dp")
    core, y, low, high = me & 1, me >> 1, my_dp & 1, my_dp >> 1
    own = {
        "low": [low ^ k for k in range(2)],
        "y": [y ^ k for k in range(n_y)],
        "high": [high ^ k for k in range(n_high)],
    }
    info = jnp.concatenate([jnp.stack([me, core, my_dp]).astype(jnp.int32), counts])
    info, own, proj = lax.optimization_barrier((info, own, proj))
    routes, targets = (x.reshape(pages, 1, wdev) for x in (routes, targets))

    even, odd = far[0::2], far[1::2]
    to_even = dispatch(info, routes, words, [((r,), 0, pages) for r in even], cap, targets)
    info, proj, to_even = lax.optimization_barrier((info, proj, to_even))
    from_even = [exchange(rows, "seq", r) for rows, r in zip(to_even, even)]
    label_of = lambda rows: rows[:, pages * cap :]
    labels = [label_of(to_even[0]), exchange(label_of(to_even[0]), "seq", 1)]

    piece = half_of(info, proj, width // 2)
    again = half_of(info, piece, width // 2)
    info, again = lax.optimization_barrier((info, again))
    pieces = [piece] + [exchange(piece if k == 1 else again, "dp", 2 * k) for k in range(1, n_high)]
    group = n_high // 2

    stay, across, *to_odd = dispatch(
        info, routes, words, [((r,), 0, pages) for r in near + odd], cap, flops=WORK
    )
    rows_of = lambda x: x.reshape(1, -1, width)
    pieces[1:group], to_odd, stay, across = lax.optimization_barrier(
        (pieces[1:group], to_odd, stay, across)
    )
    from_odd = [exchange(rows_of(rows), "seq", r) for rows, r in zip(to_odd, odd)]
    early = jnp.stack(pieces[:group])
    early = [early, exchange(early, "dp", 1)]
    late_offsets = [[2 * k + bit] for k in range(group, n_high) for bit in range(2)]
    table_near = tables(info, labels, flags, near, cap, pps, wdev, 4 * WORK)
    early, pieces[group:], table_near = lax.optimization_barrier(
        (early, pieces[group:], table_near)
    )
    late = [jnp.stack([piece]) for piece in pieces[group:]]

    late = [x for piece in late for x in (piece, exchange(piece, "dp", 1))]
    early += [exchange(some, "seq", 1) for some in early]
    late, early, from_even, across = lax.optimization_barrier((late, early, from_even, across))
    late += [exchange(piece, "seq", 1) for piece in late]
    across = exchange(across, "seq", 1)

    labels = [
        x
        for rows in from_even
        for x in (label_of(rows), exchange(label_of(rows), "seq", 1))
    ]
    table_far = tables(info, labels, flags, far, cap, pps, wdev)
    late, table_far = lax.optimization_barrier((late, table_far))
    n, m = len(early) // 2, len(late) // 2
    offsets = [[2 * k + bit for k in range(group)] for bit in range(2)] + late_offsets
    weight = weights(info, patches, early[:n] + late[:m] + early[n:] + late[m:], offsets)

    run = functools.partial(run_pages, info, weight, patches)
    loss, *pair_first = run(
        [(rows_of(stay), table_near, (0, cap)), (rows_of(across), table_near, (1, cap))]
        + [(rows, table_far, (2 * i, cap)) for i, rows in enumerate(from_even)]
    )
    word_loss = loss[:, 0] + exchange(loss[:, 1], "seq", 1)
    for i, r in enumerate(even):
        word_loss = word_loss + exchange(loss[:, 2 + i], "seq", r)
    before = gradient(info, F32, n_y, [pair_first], (1, 0))
    from_odd, before, word_loss = lax.optimization_barrier((from_odd, before, word_loss))
    loss, *pair_last = run([(rows, table_far, (2 * i + 1, cap)) for i, rows in enumerate(from_odd)])
    for i, r in enumerate(odd):
        word_loss = word_loss + exchange(loss[:, i], "seq", r)

    sent = gradient(info, BF16, n_y, [pair_last], (1,), (before, 0))
    kept = gradient(info, F32, n_y, [pair_last], (0,), (before, n_y), MUCH)
    form = (n_y, n_high, 2, shard_rows, width // n_seq)
    terms = [kept.reshape(form), exchange(sent, "seq", 1).reshape(form)]
    part = lambda i, j: sum(
        pick(t, (own["y"][i], None, own["low"][j])).astype(F32) for t in terms
    )
    total = part(0, 0)
    for i in range(n_y):
        for j in range(2):
            if i or j:
                total = total + exchange_both(part(i, j).astype(BF16), j, 2 * i)
    grad = pick(total, (own["high"][0],))
    for k in range(1, n_high):
        grad = grad + exchange(pick(total, (own["high"][k],)).astype(BF16), "dp", 2 * k)
    return (word_loss, grad)


def solution(mesh):
    in_specs = (
        P("dp", "seq", None),
        P("dp", "seq", None),
        P("dp", None),
        P("dp", "seq", None),
        P("dp", "seq"),
        P("dp"),
        P("dp", None, None),
    )
    out_specs = (P("dp", "seq"), P("dp", "seq"))
    return jax.shard_map(local, mesh=mesh, in_specs=in_specs, out_specs=out_specs, check_vma=False)
```

```python
import functools
import math

import jax
import jax.numpy as jnp
from jax import lax
from jax.experimental import pallas as pl
from jax.experimental.pallas import tpu as pltpu
from jax.sharding import PartitionSpec as P

MARGIN_BLOCK_SIZE = 64
SHIFT = 6
VMEM_LIMIT = 16 * 1024 * 1024
WORK = 1<<31
MUCH = 1 << 35
ME, CORE, DP, COUNTS = 0, 1, 2, 3
TARGET, COEF, BLOCKS = 0, 1, 2
F32, BF16 = jnp.float32, jnp.bfloat16


def dot(a, b, contract=((1,), (0,))):
    return lax.dot_general(a, b, (contract, ((), ())), preferred_element_type=F32)


def iota(shape, axis):
    return lax.broadcasted_iota(jnp.int32, shape, axis)


def ranks(hits):
    n = hits.shape[1]
    before = (iota((n, n), 0) < iota((n, n), 1)).astype(BF16)
    return jnp.where(hits > 0, dot(hits.astype(BF16), before), -1.0)


def call(kernel, n_pages, in_specs, out_specs, out_shape, operands, scratch=(), aliases={}, flops=0):
    return pl.pallas_call(
        kernel,
        grid_spec=pltpu.PrefetchScalarGridSpec(
            num_scalar_prefetch=1,
            grid=(n_pages,),
            in_specs=in_specs,
            out_specs=out_specs,
            scratch_shapes=scratch,
        ),
        out_shape=out_shape,
        compiler_params=pltpu.CompilerParams(vmem_limit_bytes=VMEM_LIMIT),
        cost_estimate=pl.CostEstimate(flops=flops, bytes_accessed=0, transcendentals=0),
        input_output_aliases=aliases,
    )(*operands)


def page_of(array, first_page=0):
    rest = array.shape[1:]
    return pl.BlockSpec((1,) + rest, lambda p, info: (p + first_page,) + (0,) * len(rest))


def all_of(array):
    return pl.BlockSpec(array.shape, lambda p, info: (0,) * len(array.shape))


def pad_rows(n):
    return -(-n // 8) * 8


def stacked(rows):
    n, width = pad_rows(len(rows)), rows[0].shape[1]
    row = iota((n, width), 0)
    out = jnp.zeros((n, width), rows[0].dtype)
    for i, r in enumerate(rows):
        out = jnp.where(row == i, r, out)
    return out


def dispatch_kernel(plan, cap, info, routes, words, *outs):
    wdev = words.shape[1]
    slots = iota((cap, wdev), 0).astype(F32)
    by_page = {}
    for out, (offsets, first_page, n_pages) in zip(outs, plan):
        for p in range(n_pages):
            for i, offset in enumerate(offsets):
                by_page.setdefault(first_page + p, []).append((offset, out, i, p))
    tasks = [(page, *task) for page in by_page for task in by_page[page]]
    rank = ranks(
        stacked(
            [
                (routes[page] == jnp.bitwise_xor(info[ME], offset)).astype(F32)
                for page, offset, *_ in tasks
            ]
        )
    )
    n = 0
    for page, some in by_page.items():
        picks = [
            (slots == rank[n + i : n + i + 1]).astype(BF16) for i in range(len(some))
        ]
        rows = dot(jnp.concatenate(picks, axis=0), words[page]).astype(BF16)
        for i, (_, out, place, p) in enumerate(some):
            out[place, p] = rows[i * cap : (i + 1) * cap]
        n += len(some)


def dispatch(info, routes, words, plan, cap, flops=0):
    width = words.shape[2]
    out = [
        jax.ShapeDtypeStruct((len(offsets), n_pages, cap, width), BF16)
        for offsets, _, n_pages in plan
    ]
    return call(
        functools.partial(dispatch_kernel, plan, cap),
        1,
        [all_of(routes), all_of(words)],
        [all_of(o) for o in out],
        out,
        (info, routes, words),
        flops=flops,
    )


def table_kernel(offsets, cap, own_blk, info, meta, flags, table, rank_out):
    me = info[ME]
    n_homes, pages, _, wdev = meta.shape
    nblk, all_blk = flags.shape[1:]
    n_rows = table.shape[1]
    slots = iota((cap, wdev), 0).astype(F32)
    rank = ranks(
        stacked(
            [
                (meta[i, p, 0:1, :] == me).astype(F32)
                for p in range(pages)
                for i in range(n_homes)
            ]
        )
    )
    lane = iota((n_rows, 128), 1)
    own = iota((all_blk, 128), 1) - BLOCKS
    chosen = (own >= 0) & (own < own_blk) & (iota((all_blk, 128), 0) == me * own_blk + own)
    chosen = chosen.astype(BF16)
    place = iota((1, wdev), 1) + 1
    for p in range(pages):
        t, idx = [], []
        for i, offset in enumerate(offsets):
            own = rank[p * n_homes + i : p * n_homes + i + 1]
            rank_out[p, i : i + 1] = own
            target = meta[i, p, 1:2, :]
            values = stacked([target >> 6, target & 63, place >> 6, place & 63]).astype(F32)
            got = dot((slots == own).astype(BF16), values.astype(BF16), ((1,), (1,)))
            got = got.astype(jnp.int32)
            t.append(got[:, 0:1] * 64 + got[:, 1:2])
            at = got[:, 2:3] * 64 + got[:, 3:4]
            idx.append(jnp.where(at > 0, at - 1 + jnp.bitwise_xor(me, offset) * wdev, -1))
        t, idx = jnp.concatenate(t, axis=0), jnp.concatenate(idx, axis=0)
        word_block = jnp.maximum(idx, 0) >> SHIFT == iota((n_rows, nblk), 1)
        margin = dot(word_block.astype(BF16), flags[p].astype(BF16)).astype(BF16)
        allowed = (dot(margin, chosen) > 0.5) | (lane - BLOCKS == t >> SHIFT)
        count = info[COUNTS + p]
        valid = (idx >= 0) & (idx < count)
        coef = jnp.where(valid, 64.0 / count.astype(F32), 0.0)
        value = jnp.where(allowed, 1.0, 0.0)
        table[p] = jnp.where(lane == TARGET, t.astype(F32), jnp.where(lane == COEF, coef, value))


def tables(info, meta, flags, offsets, cap, pps, flops=0):
    n_homes, pages, _, wdev = meta.shape
    out = [
        jax.ShapeDtypeStruct((pages, n_homes * cap, 128), F32),
        jax.ShapeDtypeStruct((pages, pad_rows(n_homes), wdev), F32),
    ]
    return call(
        functools.partial(table_kernel, offsets, cap, pps // MARGIN_BLOCK_SIZE),
        1,
        [all_of(meta), all_of(flags)],
        [all_of(o) for o in out],
        out,
        (info, meta, flags),
        flops=flops,
    )


def half_kernel(info, proj, out):
    out[...] = proj[...]


def half_of(info, proj, half):
    rows, width = proj.shape
    out = jax.ShapeDtypeStruct((rows, half), BF16)
    return call(
        half_kernel,
        1,
        [pl.BlockSpec((rows, half), lambda p, info: (0, info[CORE] if width > half else 0))],
        all_of(out),
        out,
        (info, proj),
        flops=MUCH,
    )


def weights_kernel(offsets, info, patches, *refs):
    gathered, (*before, out, proj, sems) = refs[: 2 * len(offsets)], refs[2 * len(offsets) :]
    half = proj.shape[1] // 2
    rows = gathered[0].shape[1]
    shards = [offset for some in offsets for offset in some]

    def copies():
        n = 0
        for core in range(2):
            at = 0
            for some, ref in zip(offsets, gathered[core * len(offsets) :]):
                for i in range(len(some)):
                    first = jnp.bitwise_xor(info[CORE], core) * half
                    to = proj.at[pl.ds(at * rows, rows), pl.ds(pl.multiple_of(first, half), half)]
                    yield pltpu.make_async_copy(ref.at[i], to, sems.at[n])
                    at, n = at + 1, n + 1

    @pl.when(pl.program_id(0) == 0)
    def _():
        started = list(copies())
        for copy in started:
            copy.start()
        for copy in started:
            copy.wait()

    for other in before:
        out[...] = other[...]
    got = dot(proj[...], patches[0], ((1,), (1,))).astype(BF16)
    for i, offset in enumerate(shards):
        to = pl.multiple_of(jnp.bitwise_xor(info[DP], offset) * rows, rows)
        out[0, pl.ds(to, rows)] = got[i * rows : (i + 1) * rows]


def weights(info, patches, gathered, offsets, before=(), flops=0):
    pages, pps, width = patches.shape
    n_shards = sum(len(some) for some in offsets)
    out = jax.ShapeDtypeStruct((pages, width, pps), BF16)
    return call(
        functools.partial(weights_kernel, offsets),
        pages,
        [page_of(patches)]
        + [pl.BlockSpec(memory_space=pl.ANY)] * len(gathered)
        + [page_of(b) for b in before],
        page_of(out),
        out,
        (info, patches, *gathered, *before),
        [
            pltpu.VMEM((n_shards * gathered[0].shape[1], width), BF16),
            pltpu.SemaphoreType.DMA((2 * n_shards,)),
        ],
        flops=flops,
    )


def page_kernel(n_homes, info, table, rank, weight, patches, *refs):
    *words, loss, x_t, dq = refs
    pps, width = patches.shape[1:]
    cap = words[0].shape[2]
    n_rows = n_homes * cap
    scale = 2.0 / math.sqrt(width)
    x = jnp.concatenate([w[0, 0] for w in words], axis=0)
    scores = dot(x, weight[0]) * scale
    is_target = iota((n_rows, pps), 1) == table[0, :, TARGET : TARGET + 1].astype(jnp.int32)
    coef = table[0, :, COEF : COEF + 1]
    lanes = table[0]
    spread = iota((128, pps), 0) - BLOCKS == iota((128, pps), 1) >> SHIFT
    marks = jnp.where(iota(lanes.shape, 1) < BLOCKS, 0.0, lanes).astype(BF16)
    masked = jnp.where(dot(marks, spread.astype(BF16)) > 0.5, scores, -jnp.inf)
    top = jnp.max(masked, axis=1, keepdims=True)
    expo = jnp.exp(masked - top)
    total = jnp.sum(expo, axis=1, keepdims=True)
    target_score = jnp.sum(jnp.where(is_target, scores, 0.0), axis=1, keepdims=True)
    row_loss = jnp.where(coef > 0, top + jnp.log(total) - target_score, 0.0)
    share = expo * (1.0 / total)
    dscore = (coef * jnp.where(is_target, share - 1.0, share)).astype(BF16)
    back = (dot(dscore, patches[0]) * scale).astype(BF16)
    more = dq.shape[0] - n_rows
    if more:
        back = jnp.concatenate([back, jnp.zeros((more, width), BF16)], axis=0)
        x = jnp.concatenate([x, jnp.zeros((more, width), BF16)], axis=0)
    dq[...] = back
    slots = iota((cap, rank.shape[2]), 0).astype(F32)
    for r in range(n_homes):
        picked = jnp.where(slots == rank[0, r : r + 1, :], row_loss[r * cap : (r + 1) * cap], 0.0)
        loss[0, r : r + 1, :] = jnp.sum(picked, axis=0, keepdims=True)
    x_t[...] = x.T


def run_pages(info, weight, patches, table, words, first_page, n_pages, at=0):
    _, _, cap, width = words[0][0].shape
    wdev = table[1].shape[2]
    n_homes = len(words)
    n_rows = -(-n_homes * cap // 128) * 128
    out = [
        jax.ShapeDtypeStruct((n_pages, n_homes, wdev), F32),
        jax.ShapeDtypeStruct((width, n_pages * n_rows), BF16),
        jax.ShapeDtypeStruct((n_pages * n_rows, width), BF16),
    ]
    inputs = (*table, weight, patches)
    return call(
        functools.partial(page_kernel, n_homes),
        n_pages,
        [page_of(a, first_page) for a in inputs]
        + [pl.BlockSpec((1, 1, cap, width), lambda p, info, i=i: (i, p + at, 0, 0)) for _, i in words],
        [
            page_of(out[0]),
            pl.BlockSpec((width, n_rows), lambda p, info: (0, p)),
            pl.BlockSpec((n_rows, width), lambda p, info: (p, 0)),
        ],
        out,
        (info, *inputs, *(w for w, _ in words)),
    )


def gradient_kernel(n_pairs, info, *refs):
    pairs, (*before, out) = refs[: 2 * n_pairs], refs[2 * n_pairs :]
    got = sum(dot(pairs[i][...], pairs[i + 1][...]) for i in range(0, len(pairs), 2))
    for part in before:
        got = got + part[0]
    out[0] = got.astype(out.dtype)


def gradient(info, dtype, n_y, pairs, cores, before=(), flops=0):
    width = pairs[0][0].shape[0]
    wcol = width // (2 * n_y)
    out = jax.ShapeDtypeStruct((len(cores) * n_y, width, wcol), dtype)

    def column(i, info):
        core = cores[0] if len(cores) == 1 else jnp.where(i < n_y, cores[0], cores[1])
        return 0, 2 * (i % n_y) + jnp.bitwise_xor(info[CORE], core)

    specs = []
    for x_t, dq in pairs:
        specs += [all_of(x_t), pl.BlockSpec((dq.shape[0], wcol), column)]
    if before:
        first = before[1]
        specs.append(pl.BlockSpec((1, width, wcol), lambda i, info: (first + i, 0, 0)))
    return call(
        functools.partial(gradient_kernel, len(pairs)),
        len(cores) * n_y,
        specs,
        page_of(out),
        out,
        (info, *(x for pair in pairs for x in pair), *before[:1]),
        flops=flops,
    )


def exchange(x, axis, offset):
    n = lax.axis_size(axis)
    return lax.ppermute(x, axis, [(i, i ^ offset) for i in range(n)])


def exchange_both(x, dp, seq):
    n_seq = lax.axis_size("seq")
    n = lax.axis_size("dp") * n_seq
    return lax.ppermute(x, ("dp", "seq"), [(i, i ^ (dp * n_seq + seq)) for i in range(n)])


def pick(x, places):
    places = list(places) + [None] * (x.ndim - len(places))
    start = [0 if i is None else i for i in places]
    size = [n if i is None else 1 for i, n in zip(places, x.shape)]
    got = lax.dynamic_slice(x, start, size, allow_negative_indices=False)
    return got.reshape([n for i, n in zip(places, x.shape) if i is None])


def local(words, patches, proj, routes, targets, counts, flags):
    pages, wdev, width = words.shape
    pps = patches.shape[1]
    n_seq = lax.axis_size("seq")
    n_dp = lax.axis_size("dp")
    n_y, n_high = n_seq // 2, n_dp // 2
    cap = 2 * wdev // n_seq
    shard_rows = proj.shape[0]
    near, far = (0, 1), tuple(range(2, n_seq))

    me, my_dp = lax.axis_index("seq"), lax.axis_index("dp")
    core, y, low, high = me & 1, me >> 1, my_dp & 1, my_dp >> 1
    own = {
        "low": [low ^ k for k in range(2)],
        "y": [y ^ k for k in range(n_y)],
        "high": [high ^ k for k in range(n_high)],
    }
    info = jnp.concatenate([jnp.stack([me, core, my_dp]).astype(jnp.int32), counts])
    info, own, proj = lax.optimization_barrier((info, own, proj))
    routes = routes.reshape(pages, 1, wdev)

    split = pages - 1
    both = dispatch(
        info, routes, words, [((2 * k, 2 * k + 1), 0, split) for k in range(1, n_y)], cap
    )
    info, proj, both = lax.optimization_barrier((info, proj, both))
    both = [exchange(rows, "seq", 2 * (k + 1)) for k, rows in enumerate(both)]
    piece = half_of(info, proj, width // 2)
    pieces = [piece] + [exchange(piece, "dp", 2 * k) for k in range(1, n_high)]
    group = n_high // 2
    stay, across, *rest = dispatch(
        info,
        routes,
        words,
        [((r,), 0, pages) for r in near] + [((r,), split, pages - split) for r in far],
        cap,
        WORK,
    )
    pieces[1:group], rest, stay, across = lax.optimization_barrier(
        (pieces[1:group], rest, stay, across)
    )
    early = jnp.stack(pieces[:group])
    early = [early, exchange(early, "dp", 1)]
    late_offsets = [[2 * k + bit] for k in range(group, n_high) for bit in range(2)]

    pair = jnp.concatenate([routes, targets.reshape(pages, 1, wdev)], axis=1)
    meta_near = jnp.stack([pair, exchange(pair, "seq", 1)])
    table_near = tables(info, meta_near, flags, near, cap, pps, WORK)
    meta_far = jnp.concatenate([exchange(meta_near, "seq", 2 * k) for k in range(1, n_y)], axis=0)

    early, pieces[group:], table_near = lax.optimization_barrier(
        (early, pieces[group:], table_near)
    )
    late = [jnp.stack([piece]) for piece in pieces[group:]]

    early += [exchange(some, "seq", 1) for some in early]
    early, late[-1] = lax.optimization_barrier((early, late[-1]))
    weight = weights(
        info, patches, early, [[2 * k + bit for k in range(group)] for bit in range(2)], (), WORK
    )
    late = [x for piece in late for x in (piece, exchange(piece, "dp", 1))]
    late, weight = lax.optimization_barrier((late, weight))
    across = exchange(across, "seq", 1)
    late += [exchange(piece, "seq", 1) for piece in late]
    rest = [exchange(rows, "seq", r) for rows, r in zip(rest, far)]
    weight = weights(info, patches, late, late_offsets, [weight])
    run = functools.partial(run_pages, info, weight, patches)
    near_words = [(stay, 0), (across, 0)]
    some = pages // 2
    loss, *pair_0 = run(table_near, near_words, 0, some)
    both, meta_far, pair_0 = lax.optimization_barrier((both, meta_far, pair_0))
    first = [pair for rows in both for pair in ((rows, 0), (exchange(rows, "seq", 1), 1))]
    loss_1, *pair_1 = run(table_near, near_words, some, pages - some, some)
    loss = jnp.concatenate([loss, loss_1], axis=0)
    near_loss = [loss[:, 0], exchange(loss[:, 1], "seq", 1)]
    pair_1, meta_far = lax.optimization_barrier((pair_1, meta_far))
    table_far = tables(info, meta_far, flags, far, cap, pps)
    loss_a, *pair_a = run(table_far, first, 0, split)
    before = gradient(info, F32, n_y, [pair_0, pair_1], (1,))
    rest, pair_a, before = lax.optimization_barrier((rest, pair_a, before))
    loss_b, *pair_b = run(table_far, [(rows, 0) for rows in rest], split, pages - split)
    losses = jnp.concatenate([loss_a, loss_b], axis=0)
    word_loss = near_loss + [exchange(losses[:, i], "seq", r) for i, r in enumerate(far)]

    sent = gradient(info, BF16, n_y, [pair_a, pair_b], (1,), (before, 0))
    kept = gradient(info, F32, n_y, [pair_0, pair_1, pair_a, pair_b], (0,), flops=MUCH)
    form = (n_y, n_high, 2, shard_rows, width // n_seq)
    terms = [kept.reshape(form), exchange(sent, "seq", 1).reshape(form)]
    part = lambda i, j: sum(
        pick(t, (own["y"][i], None, own["low"][j])).astype(F32) for t in terms
    )
    total = part(0, 0)
    for i, j in [(0, 1)] + [(i, j) for i in range(1, n_y) for j in (1, 0)]:
        total = total + exchange_both(part(i, j).astype(BF16), j, 2 * i)
    grad = pick(total, (own["high"][0],))
    for k in range(1, n_high):
        grad = grad + exchange(pick(total, (own["high"][k],)).astype(BF16), "dp", 2 * k)
    return (sum(word_loss), grad)


def solution(mesh):
    in_specs = (
        P("dp", "seq", None),
        P("dp", "seq", None),
        P("dp", None),
        P("dp", "seq", None),
        P("dp", "seq"),
        P("dp"),
        P("dp", None, None),
    )
    out_specs = (P("dp", "seq"), P("dp", "seq"))
    return jax.shard_map(local, mesh=mesh, in_specs=in_specs, out_specs=out_specs, check_vma=False)
```

```python
import functools
import math

import jax
import jax.numpy as jnp
from jax import lax
from jax.experimental import pallas as pl
from jax.experimental.pallas import tpu as pltpu
from jax.sharding import PartitionSpec as P

MARGIN_BLOCK_SIZE = 64
SHIFT = 6
VMEM_LIMIT = 16 * 1024 * 1024
WORK = 1<<31
MUCH = 1 << 35
ME, CORE, DP, COUNTS = 0, 1, 2, 3
TARGET, COEF, BLOCKS = 0, 1, 2
F32, BF16 = jnp.float32, jnp.bfloat16


def dot(a, b, contract=((1,), (0,))):
    return lax.dot_general(a, b, (contract, ((), ())), preferred_element_type=F32)


def iota(shape, axis):
    return lax.broadcasted_iota(jnp.int32, shape, axis)


def ranks(hits):
    n = hits.shape[1]
    before = (iota((n, n), 0) < iota((n, n), 1)).astype(BF16)
    return jnp.where(hits > 0, dot(hits.astype(BF16), before), -1.0)


def call(kernel, n_pages, in_specs, out_specs, out_shape, operands, scratch=(), aliases={}, flops=0):
    return pl.pallas_call(
        kernel,
        grid_spec=pltpu.PrefetchScalarGridSpec(
            num_scalar_prefetch=1,
            grid=(n_pages,),
            in_specs=in_specs,
            out_specs=out_specs,
            scratch_shapes=scratch,
        ),
        out_shape=out_shape,
        compiler_params=pltpu.CompilerParams(vmem_limit_bytes=VMEM_LIMIT),
        cost_estimate=pl.CostEstimate(flops=flops, bytes_accessed=0, transcendentals=0),
        input_output_aliases=aliases,
    )(*operands)


def call_whole(kernel, out_shape, operands, flops=0):
    vmem = pl.BlockSpec(memory_space=pltpu.VMEM)
    return pl.pallas_call(
        kernel,
        in_specs=[pl.BlockSpec(memory_space=pltpu.SMEM)] + [vmem] * (len(operands) - 1),
        out_specs=[vmem] * len(out_shape),
        out_shape=out_shape,
        compiler_params=pltpu.CompilerParams(vmem_limit_bytes=VMEM_LIMIT),
        cost_estimate=pl.CostEstimate(flops=flops, bytes_accessed=0, transcendentals=0),
    )(*operands)


def page_of(array, first_page=0):
    rest = array.shape[1:]
    return pl.BlockSpec((1,) + rest, lambda p, info: (p + first_page,) + (0,) * len(rest))


def all_of(array):
    return pl.BlockSpec(array.shape, lambda p, info: (0,) * len(array.shape))


def pad_rows(n):
    return -(-n // 8) * 8


def stacked(rows):
    n, width = pad_rows(len(rows)), rows[0].shape[1]
    row = iota((n, width), 0)
    out = jnp.zeros((n, width), rows[0].dtype)
    for i, r in enumerate(rows):
        out = jnp.where(row == i, r, out)
    return out


def dispatch_kernel(plan, cap, info, routes, words, *outs):
    wdev = words.shape[1]
    slots = iota((cap, wdev), 0).astype(F32)
    by_page = {}
    for out, (offsets, first_page, n_pages) in zip(outs, plan):
        for p in range(n_pages):
            for i, offset in enumerate(offsets):
                by_page.setdefault(first_page + p, []).append((offset, out, i, p))
    tasks = [(page, *task) for page in by_page for task in by_page[page]]
    rank = ranks(
        stacked(
            [
                (routes[page] == jnp.bitwise_xor(info[ME], offset)).astype(F32)
                for page, offset, *_ in tasks
            ]
        )
    )
    n = 0
    for page, some in by_page.items():
        picks = [
            (slots == rank[n + i : n + i + 1]).astype(BF16) for i in range(len(some))
        ]
        rows = dot(jnp.concatenate(picks, axis=0), words[page]).astype(BF16)
        for i, (_, out, place, p) in enumerate(some):
            out[place, p] = rows[i * cap : (i + 1) * cap]
        n += len(some)


def dispatch(info, routes, words, plan, cap, flops=0):
    width = words.shape[2]
    out = [
        jax.ShapeDtypeStruct((len(offsets), n_pages, cap, width), BF16)
        for offsets, _, n_pages in plan
    ]
    return call_whole(
        functools.partial(dispatch_kernel, plan, cap), out, (info, routes, words), flops
    )


def table_kernel(offsets, cap, own_blk, info, meta, flags, table, rank_out):
    me = info[ME]
    n_homes, pages, _, wdev = meta.shape
    nblk, all_blk = flags.shape[1:]
    n_rows = table.shape[1]
    slots = iota((cap, wdev), 0).astype(F32)
    rank = ranks(
        stacked(
            [
                (meta[i, p, 0:1, :] == me).astype(F32)
                for p in range(pages)
                for i in range(n_homes)
            ]
        )
    )
    lane = iota((n_rows, 128), 1)
    own = iota((all_blk, 128), 1) - BLOCKS
    chosen = (own >= 0) & (own < own_blk) & (iota((all_blk, 128), 0) == me * own_blk + own)
    chosen = chosen.astype(BF16)
    place = iota((1, wdev), 1) + 1
    for p in range(pages):
        t, idx = [], []
        for i, offset in enumerate(offsets):
            own = rank[p * n_homes + i : p * n_homes + i + 1]
            rank_out[p, i : i + 1] = own
            target = meta[i, p, 1:2, :]
            values = stacked([target >> 6, target & 63, place >> 6, place & 63]).astype(F32)
            got = dot((slots == own).astype(BF16), values.astype(BF16), ((1,), (1,)))
            got = got.astype(jnp.int32)
            t.append(got[:, 0:1] * 64 + got[:, 1:2])
            at = got[:, 2:3] * 64 + got[:, 3:4]
            idx.append(jnp.where(at > 0, at - 1 + jnp.bitwise_xor(me, offset) * wdev, -1))
        t, idx = jnp.concatenate(t, axis=0), jnp.concatenate(idx, axis=0)
        word_block = jnp.maximum(idx, 0) >> SHIFT == iota((n_rows, nblk), 1)
        margin = dot(word_block.astype(BF16), flags[p].astype(BF16)).astype(BF16)
        allowed = (dot(margin, chosen) > 0.5) | (lane - BLOCKS == t >> SHIFT)
        count = info[COUNTS + p]
        valid = (idx >= 0) & (idx < count)
        coef = jnp.where(valid, 64.0 / count.astype(F32), 0.0)
        value = jnp.where(allowed, 1.0, 0.0)
        table[p] = jnp.where(lane == TARGET, t.astype(F32), jnp.where(lane == COEF, coef, value))


def tables(info, meta, flags, offsets, cap, pps, flops=0):
    n_homes, pages, _, wdev = meta.shape
    out = [
        jax.ShapeDtypeStruct((pages, n_homes * cap, 128), F32),
        jax.ShapeDtypeStruct((pages, pad_rows(n_homes), wdev), F32),
    ]
    return call_whole(
        functools.partial(table_kernel, offsets, cap, pps // MARGIN_BLOCK_SIZE),
        out,
        (info, meta, flags),
        flops,
    )


def half_kernel(info, proj, out):
    half = out.shape[1]
    out[...] = proj[:, pl.ds(pl.multiple_of(info[CORE] * half, half), half)]


def half_of(info, proj):
    rows, width = proj.shape
    out = [jax.ShapeDtypeStruct((rows, width // 2), BF16)]
    return call_whole(half_kernel, out, (info, proj), MUCH)[0]


def weights_kernel(offsets, info, patches, *refs):
    gathered, (*before, out, proj, sems) = refs[: 2 * len(offsets)], refs[2 * len(offsets) :]
    half = proj.shape[1] // 2
    rows = gathered[0].shape[1]
    shards = [offset for some in offsets for offset in some]

    def copies():
        n = 0
        for core in range(2):
            at = 0
            for some, ref in zip(offsets, gathered[core * len(offsets) :]):
                for i in range(len(some)):
                    first = jnp.bitwise_xor(info[CORE], core) * half
                    to = proj.at[pl.ds(at * rows, rows), pl.ds(pl.multiple_of(first, half), half)]
                    yield pltpu.make_async_copy(ref.at[i], to, sems.at[n])
                    at, n = at + 1, n + 1

    @pl.when(pl.program_id(0) == 0)
    def _():
        started = list(copies())
        for copy in started:
            copy.start()
        for copy in started:
            copy.wait()

    for other in before:
        out[...] = other[...]
    got = dot(proj[...], patches[0], ((1,), (1,))).astype(BF16)
    for i, offset in enumerate(shards):
        to = pl.multiple_of(jnp.bitwise_xor(info[DP], offset) * rows, rows)
        out[0, pl.ds(to, rows)] = got[i * rows : (i + 1) * rows]


def weights(info, patches, gathered, offsets, before=(), flops=0):
    pages, pps, width = patches.shape
    n_shards = sum(len(some) for some in offsets)
    out = jax.ShapeDtypeStruct((pages, width, pps), BF16)
    return call(
        functools.partial(weights_kernel, offsets),
        pages,
        [page_of(patches)]
        + [pl.BlockSpec(memory_space=pl.ANY)] * len(gathered)
        + [page_of(b) for b in before],
        page_of(out),
        out,
        (info, patches, *gathered, *before),
        [
            pltpu.VMEM((n_shards * gathered[0].shape[1], width), BF16),
            pltpu.SemaphoreType.DMA((2 * n_shards,)),
        ],
        flops=flops,
    )


def page_kernel(n_homes, info, table, rank, weight, patches, *refs):
    *words, loss, x_t, dq = refs
    pps, width = patches.shape[1:]
    cap = words[0].shape[2]
    n_rows = n_homes * cap
    scale = 2.0 / math.sqrt(width)
    x = jnp.concatenate([w[0, 0] for w in words], axis=0)
    scores = dot(x, weight[0]) * scale
    is_target = iota((n_rows, pps), 1) == table[0, :, TARGET : TARGET + 1].astype(jnp.int32)
    coef = table[0, :, COEF : COEF + 1]
    lanes = table[0]
    spread = iota((128, pps), 0) - BLOCKS == iota((128, pps), 1) >> SHIFT
    marks = jnp.where(iota(lanes.shape, 1) < BLOCKS, 0.0, lanes).astype(BF16)
    masked = jnp.where(dot(marks, spread.astype(BF16)) > 0.5, scores, -jnp.inf)
    top = jnp.max(masked, axis=1, keepdims=True)
    expo = jnp.exp(masked - top)
    total = jnp.sum(expo, axis=1, keepdims=True)
    target_score = jnp.sum(jnp.where(is_target, scores, 0.0), axis=1, keepdims=True)
    row_loss = jnp.where(coef > 0, top + jnp.log(total) - target_score, 0.0)
    share = expo * (1.0 / total)
    dscore = (coef * jnp.where(is_target, share - 1.0, share)).astype(BF16)
    back = (dot(dscore, patches[0]) * scale).astype(BF16)
    more = dq.shape[0] - n_rows
    if more:
        back = jnp.concatenate([back, jnp.zeros((more, width), BF16)], axis=0)
        x = jnp.concatenate([x, jnp.zeros((more, width), BF16)], axis=0)
    dq[...] = back
    slots = iota((cap, rank.shape[2]), 0).astype(F32)
    for r in range(n_homes):
        picked = jnp.where(slots == rank[0, r : r + 1, :], row_loss[r * cap : (r + 1) * cap], 0.0)
        loss[0, r : r + 1, :] = jnp.sum(picked, axis=0, keepdims=True)
    x_t[...] = x.T


def run_pages(info, weight, patches, table, words, first_page, n_pages, at=0):
    _, _, cap, width = words[0][0].shape
    wdev = table[1].shape[2]
    n_homes = len(words)
    n_rows = -(-n_homes * cap // 128) * 128
    out = [
        jax.ShapeDtypeStruct((n_pages, n_homes, wdev), F32),
        jax.ShapeDtypeStruct((width, n_pages * n_rows), BF16),
        jax.ShapeDtypeStruct((n_pages * n_rows, width), BF16),
    ]
    inputs = (*table, weight, patches)
    return call(
        functools.partial(page_kernel, n_homes),
        n_pages,
        [page_of(a, first_page) for a in inputs]
        + [pl.BlockSpec((1, 1, cap, width), lambda p, info, i=i: (i, p + at, 0, 0)) for _, i in words],
        [
            page_of(out[0]),
            pl.BlockSpec((width, n_rows), lambda p, info: (0, p)),
            pl.BlockSpec((n_rows, width), lambda p, info: (p, 0)),
        ],
        out,
        (info, *inputs, *(w for w, _ in words)),
    )


def gradient_kernel(core, info, *refs):
    *pairs, out = refs
    n_y, _, wcol = out.shape

    def block(y, _):
        column = pl.multiple_of((2 * y + jnp.bitwise_xor(info[CORE], core)) * wcol, wcol)
        got = sum(
            dot(pairs[i][...], pairs[i + 1][:, pl.ds(column, wcol)])
            for i in range(0, len(pairs), 2)
        )
        out[y] = got.astype(out.dtype)
        return 0

    lax.fori_loop(0, n_y, block, 0)


def gradient(info, core, dtype, n_y, pairs, flops=0):
    width = pairs[0][0].shape[0]
    out = [jax.ShapeDtypeStruct((n_y, width, width // (2 * n_y)), dtype)]
    operands = (info, *(x for pair in pairs for x in pair))
    return call_whole(functools.partial(gradient_kernel, core), out, operands, flops)[0]


def exchange(x, axis, offset):
    n = lax.axis_size(axis)
    return lax.ppermute(x, axis, [(i, i ^ offset) for i in range(n)])


def exchange_both(x, dp, seq):
    n_seq = lax.axis_size("seq")
    n = lax.axis_size("dp") * n_seq
    return lax.ppermute(x, ("dp", "seq"), [(i, i ^ (dp * n_seq + seq)) for i in range(n)])


def pick(x, places):
    places = list(places) + [None] * (x.ndim - len(places))
    start = [0 if i is None else i for i in places]
    size = [n if i is None else 1 for i, n in zip(places, x.shape)]
    got = lax.dynamic_slice(x, start, size, allow_negative_indices=False)
    return got.reshape([n for i, n in zip(places, x.shape) if i is None])


def local(words, patches, proj, routes, targets, counts, flags):
    pages, wdev, width = words.shape
    pps = patches.shape[1]
    n_seq = lax.axis_size("seq")
    n_dp = lax.axis_size("dp")
    n_y, n_high = n_seq // 2, n_dp // 2
    cap = 2 * wdev // n_seq
    shard_rows = proj.shape[0]
    near, far = (0, 1), tuple(range(2, n_seq))

    me, my_dp = lax.axis_index("seq"), lax.axis_index("dp")
    core, y, low, high = me & 1, me >> 1, my_dp & 1, my_dp >> 1
    own = {
        "low": [low ^ k for k in range(2)],
        "y": [y ^ k for k in range(n_y)],
        "high": [high ^ k for k in range(n_high)],
    }
    info = jnp.concatenate([jnp.stack([me, core, my_dp]).astype(jnp.int32), counts])
    info, own, proj = lax.optimization_barrier((info, own, proj))
    routes = routes.reshape(pages, 1, wdev)

    split = pages - 1
    both = dispatch(
        info, routes, words, [((2 * k, 2 * k + 1), 0, split) for k in range(1, n_y)], cap
    )
    info, proj, both = lax.optimization_barrier((info, proj, both))
    both = [exchange(rows, "seq", 2 * (k + 1)) for k, rows in enumerate(both)]
    piece = half_of(info, proj)
    pieces = [piece] + [exchange(piece, "dp", 2 * k) for k in range(1, n_high)]
    group = n_high // 2
    stay, across, *rest = dispatch(
        info,
        routes,
        words,
        [((r,), 0, pages) for r in near] + [((r,), split, pages - split) for r in far],
        cap,
        WORK,
    )
    pieces[1:group], rest, stay, across = lax.optimization_barrier(
        (pieces[1:group], rest, stay, across)
    )
    early = jnp.stack(pieces[:group])
    early = [early, exchange(early, "dp", 1)]
    late_offsets = [[2 * k + bit] for k in range(group, n_high) for bit in range(2)]

    pair = jnp.concatenate([routes, targets.reshape(pages, 1, wdev)], axis=1)
    meta_near = jnp.stack([pair, exchange(pair, "seq", 1)])
    table_near = tables(info, meta_near, flags, near, cap, pps, WORK)
    meta_far = jnp.concatenate([exchange(meta_near, "seq", 2 * k) for k in range(1, n_y)], axis=0)

    early, pieces[group:], table_near = lax.optimization_barrier(
        (early, pieces[group:], table_near)
    )
    late = [jnp.stack([piece]) for piece in pieces[group:]]

    early += [exchange(some, "seq", 1) for some in early]
    early, late[-1] = lax.optimization_barrier((early, late[-1]))
    weight = weights(
        info, patches, early, [[2 * k + bit for k in range(group)] for bit in range(2)], (), WORK
    )
    late = [x for piece in late for x in (piece, exchange(piece, "dp", 1))]
    late, weight = lax.optimization_barrier((late, weight))
    across = exchange(across, "seq", 1)
    late += [exchange(piece, "seq", 1) for piece in late]
    rest = [exchange(rows, "seq", r) for rows, r in zip(rest, far)]
    weight = weights(info, patches, late, late_offsets, [weight])
    run = functools.partial(run_pages, info, weight, patches)
    near_words = [(stay, 0), (across, 0)]
    some = pages // 2
    loss, *pair_0 = run(table_near, near_words, 0, some)
    both, meta_far, pair_0 = lax.optimization_barrier((both, meta_far, pair_0))
    first = [pair for rows in both for pair in ((rows, 0), (exchange(rows, "seq", 1), 1))]
    loss_1, *pair_1 = run(table_near, near_words, some, pages - some, some)
    loss = jnp.concatenate([loss, loss_1], axis=0)
    near_loss = [loss[:, 0], exchange(loss[:, 1], "seq", 1)]
    pair_1, meta_far = lax.optimization_barrier((pair_1, meta_far))
    table_far = tables(info, meta_far, flags, far, cap, pps)
    loss_a, *pair_a = run(table_far, first, 0, split)
    rest, pair_a = lax.optimization_barrier((rest, pair_a))
    loss_b, *pair_b = run(table_far, [(rows, 0) for rows in rest], split, pages - split)
    losses = jnp.concatenate([loss_a, loss_b], axis=0)
    word_loss = near_loss + [exchange(losses[:, i], "seq", r) for i, r in enumerate(far)]

    pairs = [pair_0, pair_1, pair_a, pair_b]
    sent = gradient(info, 1, BF16, n_y, pairs)
    kept = gradient(info, 0, F32, n_y, pairs, MUCH)
    form = (n_y, n_high, 2, shard_rows, width // n_seq)
    terms = [kept.reshape(form), exchange(sent, "seq", 1).reshape(form)]
    part = lambda i, j: sum(
        pick(t, (own["y"][i], None, own["low"][j])).astype(F32) for t in terms
    )
    total = part(0, 0)
    for i, j in [(i, j) for i in range(1, n_y) for j in (0, 1)] + [(0, 1)]:
        total = total + exchange_both(part(i, j).astype(BF16), j, 2 * i)
    grad = pick(total, (own["high"][0],))
    for k in range(1, n_high):
        grad = grad + exchange(pick(total, (own["high"][k],)).astype(BF16), "dp", 2 * k)
    return (sum(word_loss), grad)


def solution(mesh):
    in_specs = (
        P("dp", "seq", None),
        P("dp", "seq", None),
        P("dp", None),
        P("dp", "seq", None),
        P("dp", "seq"),
        P("dp"),
        P("dp", None, None),
    )
    out_specs = (P("dp", "seq"), P("dp", "seq"))
    return jax.shard_map(local, mesh=mesh, in_specs=in_specs, out_specs=out_specs, check_vma=False)
```

```python
import functools
import math

import jax
import jax.numpy as jnp
from jax import lax
from jax.experimental import pallas as pl
from jax.experimental.pallas import tpu as pltpu
from jax.sharding import PartitionSpec as P

MARGIN_BLOCK_SIZE = 64
SHIFT = 6
VMEM_LIMIT = 16 * 1024 * 1024
FIRST_LIMIT = 54 * 1024 * 1024
WORK = 1<<31
MUCH = 1 << 35
ME, CORE, DP, COUNTS = 0, 1, 2, 3
TARGET, COEF, BLOCKS = 0, 1, 2
F32, BF16 = jnp.float32, jnp.bfloat16


def dot(a, b, contract=((1,), (0,))):
    return lax.dot_general(a, b, (contract, ((), ())), preferred_element_type=F32)


def iota(shape, axis):
    return lax.broadcasted_iota(jnp.int32, shape, axis)


def ranks(hits):
    n = hits.shape[1]
    before = (iota((n, n), 0) < iota((n, n), 1)).astype(BF16)
    return jnp.where(hits > 0, dot(hits.astype(BF16), before), -1.0)


def call(kernel, n_pages, in_specs, out_specs, out_shape, operands, scratch=(), aliases={}, flops=0):
    return pl.pallas_call(
        kernel,
        grid_spec=pltpu.PrefetchScalarGridSpec(
            num_scalar_prefetch=1,
            grid=(n_pages,),
            in_specs=in_specs,
            out_specs=out_specs,
            scratch_shapes=scratch,
        ),
        out_shape=out_shape,
        compiler_params=pltpu.CompilerParams(vmem_limit_bytes=VMEM_LIMIT),
        cost_estimate=pl.CostEstimate(flops=flops, bytes_accessed=0, transcendentals=0),
        input_output_aliases=aliases,
    )(*operands)


def call_whole(kernel, out_shape, operands, flops=0):
    vmem = pl.BlockSpec(memory_space=pltpu.VMEM)
    return pl.pallas_call(
        kernel,
        in_specs=[pl.BlockSpec(memory_space=pltpu.SMEM)] + [vmem] * (len(operands) - 1),
        out_specs=[vmem] * len(out_shape),
        out_shape=out_shape,
        compiler_params=pltpu.CompilerParams(vmem_limit_bytes=VMEM_LIMIT),
        cost_estimate=pl.CostEstimate(flops=flops, bytes_accessed=0, transcendentals=0),
    )(*operands)


def page_of(array, first_page=0):
    rest = array.shape[1:]
    return pl.BlockSpec((1,) + rest, lambda p, info: (p + first_page,) + (0,) * len(rest))


def all_of(array):
    return pl.BlockSpec(array.shape, lambda p, info: (0,) * len(array.shape))


def pad_rows(n):
    return -(-n // 8) * 8


def stacked(rows):
    n, width = pad_rows(len(rows)), rows[0].shape[1]
    row = iota((n, width), 0)
    out = jnp.zeros((n, width), rows[0].dtype)
    for i, r in enumerate(rows):
        out = jnp.where(row == i, r, out)
    return out


def dispatch_kernel(plan, cap, info, routes, words, *outs, ready=lambda page: None):
    wdev = words.shape[1]
    slots = iota((cap, wdev), 0).astype(F32)
    by_page = {}
    for out, (offsets, first_page, n_pages) in zip(outs, plan):
        for p in range(n_pages):
            for i, offset in enumerate(offsets):
                by_page.setdefault(first_page + p, []).append((offset, out, i, p))
    tasks = [(page, *task) for page in by_page for task in by_page[page]]
    rank = ranks(
        stacked(
            [
                (routes[page] == jnp.bitwise_xor(info[ME], offset)).astype(F32)
                for page, offset, *_ in tasks
            ]
        )
    )
    n = 0
    for page, some in by_page.items():
        picks = [
            (slots == rank[n + i : n + i + 1]).astype(BF16) for i in range(len(some))
        ]
        ready(page)
        rows = dot(jnp.concatenate(picks, axis=0), words[page]).astype(BF16)
        for i, (_, out, place, p) in enumerate(some):
            out[place, p] = rows[i * cap : (i + 1) * cap]
        n += len(some)


def dispatch(info, routes, words, plan, cap, flops=0):
    width = words.shape[2]
    out = [
        jax.ShapeDtypeStruct((len(offsets), n_pages, cap, width), BF16)
        for offsets, _, n_pages in plan
    ]
    return call_whole(
        functools.partial(dispatch_kernel, plan, cap), out, (info, routes, words), flops
    )


def first_dispatch_kernel(plan, cap, info, routes, words, *refs):
    *outs, held_routes, held_words, sems = refs
    n_pages = held_words.shape[0]
    get_routes = pltpu.make_async_copy(routes, held_routes, sems.at[n_pages])
    get_words = [
        pltpu.make_async_copy(words.at[p], held_words.at[p], sems.at[p]) for p in range(n_pages)
    ]
    get_routes.start()
    for copy in get_words:
        copy.start()
    get_routes.wait()
    ready = lambda page: get_words[page].wait()
    dispatch_kernel(plan, cap, info, held_routes, held_words, *outs, ready=ready)


def first_dispatch(info, routes, words, plan, cap):
    _, wdev, width = words.shape
    n_pages = max(first_page + n for _, first_page, n in plan)
    out = [
        jax.ShapeDtypeStruct((len(offsets), n, cap, width), BF16) for offsets, _, n in plan
    ]
    anywhere, vmem = pl.BlockSpec(memory_space=pl.ANY), pl.BlockSpec(memory_space=pltpu.VMEM)
    return pl.pallas_call(
        functools.partial(first_dispatch_kernel, plan, cap),
        in_specs=[pl.BlockSpec(memory_space=pltpu.SMEM), anywhere, anywhere],
        out_specs=[vmem] * len(out),
        out_shape=out,
        scratch_shapes=[
            pltpu.VMEM(routes.shape, jnp.int32),
            pltpu.VMEM((n_pages, wdev, width), BF16),
            pltpu.SemaphoreType.DMA((n_pages + 1,)),
        ],
        compiler_params=pltpu.CompilerParams(vmem_limit_bytes=FIRST_LIMIT),
        cost_estimate=pl.CostEstimate(flops=0, bytes_accessed=0, transcendentals=0),
    )(info, routes, words)


def table_kernel(offsets, cap, own_blk, info, meta, flags, table, rank_out):
    me = info[ME]
    n_homes, pages, _, wdev = meta.shape
    nblk, all_blk = flags.shape[1:]
    n_rows = table.shape[1]
    slots = iota((cap, wdev), 0).astype(F32)
    rank = ranks(
        stacked(
            [
                (meta[i, p, 0:1, :] == me).astype(F32)
                for p in range(pages)
                for i in range(n_homes)
            ]
        )
    )
    lane = iota((n_rows, 128), 1)
    own = iota((all_blk, 128), 1) - BLOCKS
    chosen = (own >= 0) & (own < own_blk) & (iota((all_blk, 128), 0) == me * own_blk + own)
    chosen = chosen.astype(BF16)
    place = iota((1, wdev), 1) + 1
    for p in range(pages):
        t, idx = [], []
        for i, offset in enumerate(offsets):
            own = rank[p * n_homes + i : p * n_homes + i + 1]
            rank_out[p, i : i + 1] = own
            target = meta[i, p, 1:2, :]
            values = stacked([target >> 6, target & 63, place >> 6, place & 63]).astype(F32)
            got = dot((slots == own).astype(BF16), values.astype(BF16), ((1,), (1,)))
            got = got.astype(jnp.int32)
            t.append(got[:, 0:1] * 64 + got[:, 1:2])
            at = got[:, 2:3] * 64 + got[:, 3:4]
            idx.append(jnp.where(at > 0, at - 1 + jnp.bitwise_xor(me, offset) * wdev, -1))
        t, idx = jnp.concatenate(t, axis=0), jnp.concatenate(idx, axis=0)
        word_block = jnp.maximum(idx, 0) >> SHIFT == iota((n_rows, nblk), 1)
        margin = dot(word_block.astype(BF16), flags[p].astype(BF16)).astype(BF16)
        allowed = (dot(margin, chosen) > 0.5) | (lane - BLOCKS == t >> SHIFT)
        count = info[COUNTS + p]
        valid = (idx >= 0) & (idx < count)
        coef = jnp.where(valid, 64.0 / count.astype(F32), 0.0)
        value = jnp.where(allowed, 1.0, 0.0)
        table[p] = jnp.where(lane == TARGET, t.astype(F32), jnp.where(lane == COEF, coef, value))


def tables(info, meta, flags, offsets, cap, pps, flops=0):
    n_homes, pages, _, wdev = meta.shape
    out = [
        jax.ShapeDtypeStruct((pages, n_homes * cap, 128), F32),
        jax.ShapeDtypeStruct((pages, pad_rows(n_homes), wdev), F32),
    ]
    return call_whole(
        functools.partial(table_kernel, offsets, cap, pps // MARGIN_BLOCK_SIZE),
        out,
        (info, meta, flags),
        flops,
    )


def half_kernel(info, proj, out):
    half = out.shape[1]
    out[...] = proj[:, pl.ds(pl.multiple_of(info[CORE] * half, half), half)]


def half_of(info, proj):
    rows, width = proj.shape
    out = [jax.ShapeDtypeStruct((rows, width // 2), BF16)]
    return call_whole(half_kernel, out, (info, proj), MUCH)[0]


def weights_kernel(offsets, info, patches, *refs):
    gathered, (*before, out, proj, sems) = refs[: 2 * len(offsets)], refs[2 * len(offsets) :]
    half = proj.shape[1] // 2
    rows = gathered[0].shape[1]
    shards = [offset for some in offsets for offset in some]

    def copies():
        n = 0
        for core in range(2):
            at = 0
            for some, ref in zip(offsets, gathered[core * len(offsets) :]):
                for i in range(len(some)):
                    first = jnp.bitwise_xor(info[CORE], core) * half
                    to = proj.at[pl.ds(at * rows, rows), pl.ds(pl.multiple_of(first, half), half)]
                    yield pltpu.make_async_copy(ref.at[i], to, sems.at[n])
                    at, n = at + 1, n + 1

    @pl.when(pl.program_id(0) == 0)
    def _():
        started = list(copies())
        for copy in started:
            copy.start()
        for copy in started:
            copy.wait()

    for other in before:
        out[...] = other[...]
    got = dot(proj[...], patches[0], ((1,), (1,))).astype(BF16)
    for i, offset in enumerate(shards):
        to = pl.multiple_of(jnp.bitwise_xor(info[DP], offset) * rows, rows)
        out[0, pl.ds(to, rows)] = got[i * rows : (i + 1) * rows]


def weights(info, patches, gathered, offsets, before=(), flops=0):
    pages, pps, width = patches.shape
    n_shards = sum(len(some) for some in offsets)
    out = jax.ShapeDtypeStruct((pages, width, pps), BF16)
    return call(
        functools.partial(weights_kernel, offsets),
        pages,
        [page_of(patches)]
        + [pl.BlockSpec(memory_space=pl.ANY)] * len(gathered)
        + [page_of(b) for b in before],
        page_of(out),
        out,
        (info, patches, *gathered, *before),
        [
            pltpu.VMEM((n_shards * gathered[0].shape[1], width), BF16),
            pltpu.SemaphoreType.DMA((2 * n_shards,)),
        ],
        flops=flops,
    )


def page_kernel(n_homes, info, table, rank, weight, patches, *refs):
    *words, loss, x_t, dq = refs
    pps, width = patches.shape[1:]
    cap = words[0].shape[2]
    n_rows = n_homes * cap
    scale = 2.0 / math.sqrt(width)
    x = jnp.concatenate([w[0, 0] for w in words], axis=0)
    scores = dot(x, weight[0]) * scale
    is_target = iota((n_rows, pps), 1) == table[0, :, TARGET : TARGET + 1].astype(jnp.int32)
    coef = table[0, :, COEF : COEF + 1]
    lanes = table[0]
    spread = iota((128, pps), 0) - BLOCKS == iota((128, pps), 1) >> SHIFT
    marks = jnp.where(iota(lanes.shape, 1) < BLOCKS, 0.0, lanes).astype(BF16)
    masked = jnp.where(dot(marks, spread.astype(BF16)) > 0.5, scores, -jnp.inf)
    top = jnp.max(masked, axis=1, keepdims=True)
    expo = jnp.exp(masked - top)
    total = jnp.sum(expo, axis=1, keepdims=True)
    target_score = jnp.sum(jnp.where(is_target, scores, 0.0), axis=1, keepdims=True)
    row_loss = jnp.where(coef > 0, top + jnp.log(total) - target_score, 0.0)
    share = expo * (1.0 / total)
    dscore = (coef * jnp.where(is_target, share - 1.0, share)).astype(BF16)
    back = (dot(dscore, patches[0]) * scale).astype(BF16)
    more = dq.shape[0] - n_rows
    if more:
        back = jnp.concatenate([back, jnp.zeros((more, width), BF16)], axis=0)
        x = jnp.concatenate([x, jnp.zeros((more, width), BF16)], axis=0)
    dq[...] = back
    slots = iota((cap, rank.shape[2]), 0).astype(F32)
    for r in range(n_homes):
        picked = jnp.where(slots == rank[0, r : r + 1, :], row_loss[r * cap : (r + 1) * cap], 0.0)
        loss[0, r : r + 1, :] = jnp.sum(picked, axis=0, keepdims=True)
    x_t[...] = x.T


def run_pages(info, weight, patches, table, words, first_page, n_pages, at=0):
    _, _, cap, width = words[0][0].shape
    wdev = table[1].shape[2]
    n_homes = len(words)
    n_rows = -(-n_homes * cap // 128) * 128
    out = [
        jax.ShapeDtypeStruct((n_pages, n_homes, wdev), F32),
        jax.ShapeDtypeStruct((width, n_pages * n_rows), BF16),
        jax.ShapeDtypeStruct((n_pages * n_rows, width), BF16),
    ]
    inputs = (*table, weight, patches)
    return call(
        functools.partial(page_kernel, n_homes),
        n_pages,
        [page_of(a, first_page) for a in inputs]
        + [pl.BlockSpec((1, 1, cap, width), lambda p, info, i=i: (i, p + at, 0, 0)) for _, i in words],
        [
            page_of(out[0]),
            pl.BlockSpec((width, n_rows), lambda p, info: (0, p)),
            pl.BlockSpec((n_rows, width), lambda p, info: (p, 0)),
        ],
        out,
        (info, *inputs, *(w for w, _ in words)),
    )


def gradient_kernel(core, info, *refs):
    *pairs, out = refs
    before = [pairs.pop()] if len(pairs) % 2 else []
    n_y, _, wcol = out.shape

    def block(y, _):
        column = pl.multiple_of((2 * y + jnp.bitwise_xor(info[CORE], core)) * wcol, wcol)
        got = sum(
            dot(pairs[i][...], pairs[i + 1][:, pl.ds(column, wcol)])
            for i in range(0, len(pairs), 2)
        )
        for part in before:
            got = got + part[y]
        out[y] = got.astype(out.dtype)
        return 0

    lax.fori_loop(0, n_y, block, 0)


def gradient(info, core, dtype, n_y, pairs, before=(), flops=0):
    width = pairs[0][0].shape[0]
    out = [jax.ShapeDtypeStruct((n_y, width, width // (2 * n_y)), dtype)]
    operands = (info, *(x for pair in pairs for x in pair), *before)
    return call_whole(functools.partial(gradient_kernel, core), out, operands, flops)[0]


def exchange(x, axis, offset):
    n = lax.axis_size(axis)
    return lax.ppermute(x, axis, [(i, i ^ offset) for i in range(n)])


def exchange_both(x, dp, seq):
    n_seq = lax.axis_size("seq")
    n = lax.axis_size("dp") * n_seq
    return lax.ppermute(x, ("dp", "seq"), [(i, i ^ (dp * n_seq + seq)) for i in range(n)])


def pick(x, places):
    places = list(places) + [None] * (x.ndim - len(places))
    start = [0 if i is None else i for i in places]
    size = [n if i is None else 1 for i, n in zip(places, x.shape)]
    got = lax.dynamic_slice(x, start, size, allow_negative_indices=False)
    return got.reshape([n for i, n in zip(places, x.shape) if i is None])


def local(words, patches, proj, routes, targets, counts, flags):
    pages, wdev, width = words.shape
    pps = patches.shape[1]
    n_seq = lax.axis_size("seq")
    n_dp = lax.axis_size("dp")
    n_y, n_high = n_seq // 2, n_dp // 2
    cap = 2 * wdev // n_seq
    shard_rows = proj.shape[0]
    near, far = (0, 1), tuple(range(2, n_seq))

    me, my_dp = lax.axis_index("seq"), lax.axis_index("dp")
    core, y, low, high = me & 1, me >> 1, my_dp & 1, my_dp >> 1
    own = {
        "low": [low ^ k for k in range(2)],
        "y": [y ^ k for k in range(n_y)],
        "high": [high ^ k for k in range(n_high)],
    }
    info = jnp.concatenate([jnp.stack([me, core, my_dp]).astype(jnp.int32), counts])
    info, own, proj = lax.optimization_barrier((info, own, proj))
    routes = routes.reshape(pages, 1, wdev)

    split = pages - 1
    both = first_dispatch(
        info, routes, words, [((2 * k, 2 * k + 1), 0, split) for k in range(1, n_y)], cap
    )
    info, proj, both = lax.optimization_barrier((info, proj, both))
    both = [exchange(rows, "seq", 2 * (k + 1)) for k, rows in enumerate(both)]
    piece = half_of(info, proj)
    pieces = [piece] + [exchange(piece, "dp", 2 * k) for k in range(1, n_high)]
    group = n_high // 2
    stay, across, *rest = dispatch(
        info,
        routes,
        words,
        [((r,), 0, pages) for r in near] + [((r,), split, pages - split) for r in far],
        cap,
        WORK,
    )
    pieces[1:group], rest, stay, across = lax.optimization_barrier(
        (pieces[1:group], rest, stay, across)
    )
    early = jnp.stack(pieces[:group])
    early = [early, exchange(early, "dp", 1)]
    late_offsets = [[2 * k + bit] for k in range(group, n_high) for bit in range(2)]

    pair = jnp.concatenate([routes, targets.reshape(pages, 1, wdev)], axis=1)
    meta_near = jnp.stack([pair, exchange(pair, "seq", 1)])
    table_near = tables(info, meta_near, flags, near, cap, pps, WORK)
    meta_far = jnp.concatenate([exchange(meta_near, "seq", 2 * k) for k in range(1, n_y)], axis=0)

    early, pieces[group:], table_near = lax.optimization_barrier(
        (early, pieces[group:], table_near)
    )
    late = [jnp.stack([piece]) for piece in pieces[group:]]

    early += [exchange(some, "seq", 1) for some in early]
    early, late[-1] = lax.optimization_barrier((early, late[-1]))
    weight = weights(
        info, patches, early, [[2 * k + bit for k in range(group)] for bit in range(2)], (), WORK
    )
    late = [x for piece in late for x in (piece, exchange(piece, "dp", 1))]
    late, weight = lax.optimization_barrier((late, weight))
    across = exchange(across, "seq", 1)
    late += [exchange(piece, "seq", 1) for piece in late]
    rest = [exchange(rows, "seq", r) for rows, r in zip(rest, far)]
    weight = weights(info, patches, late, late_offsets, [weight])
    run = functools.partial(run_pages, info, weight, patches)
    near_words = [(stay, 0), (across, 0)]
    some = pages // 2
    loss, *pair_0 = run(table_near, near_words, 0, some)
    both, meta_far, pair_0 = lax.optimization_barrier((both, meta_far, pair_0))
    first = [pair for rows in both for pair in ((rows, 0), (exchange(rows, "seq", 1), 1))]
    loss_1, *pair_1 = run(table_near, near_words, some, pages - some, some)
    loss = jnp.concatenate([loss, loss_1], axis=0)
    near_loss = [loss[:, 0], exchange(loss[:, 1], "seq", 1)]
    pair_1, meta_far = lax.optimization_barrier((pair_1, meta_far))
    table_far = tables(info, meta_far, flags, far, cap, pps)
    loss_a, *pair_a = run(table_far, first, 0, split)
    before = gradient(info, 1, F32, n_y, [pair_0, pair_1])
    rest, pair_a, before = lax.optimization_barrier((rest, pair_a, before))
    loss_b, *pair_b = run(table_far, [(rows, 0) for rows in rest], split, pages - split)
    losses = jnp.concatenate([loss_a, loss_b], axis=0)
    word_loss = near_loss + [exchange(losses[:, i], "seq", r) for i, r in enumerate(far)]

    pairs = [pair_0, pair_1, pair_a, pair_b]
    sent = gradient(info, 1, BF16, n_y, [pair_a, pair_b], [before])
    kept = gradient(info, 0, F32, n_y, pairs, (), MUCH)
    form = (n_y, n_high, 2, shard_rows, width // n_seq)
    terms = [kept.reshape(form), exchange(sent, "seq", 1).reshape(form)]
    part = lambda i, j: sum(
        pick(t, (own["y"][i], None, own["low"][j])).astype(F32) for t in terms
    )
    total = part(0, 0)
    for i, j in [(0, 1)] + [(i, j) for i in range(1, n_y) for j in (1, 0)]:
        total = total + exchange_both(part(i, j).astype(BF16), j, 2 * i)
    grad = pick(total, (own["high"][0],))
    for k in range(1, n_high):
        grad = grad + exchange(pick(total, (own["high"][k],)).astype(BF16), "dp", 2 * k)
    return (sum(word_loss), grad)


def solution(mesh):
    in_specs = (
        P("dp", "seq", None),
        P("dp", "seq", None),
        P("dp", None),
        P("dp", "seq", None),
        P("dp", "seq"),
        P("dp"),
        P("dp", None, None),
    )
    out_specs = (P("dp", "seq"), P("dp", "seq"))
    return jax.shard_map(local, mesh=mesh, in_specs=in_specs, out_specs=out_specs, check_vma=False)
```

```python
import functools
import math

import jax
import jax.numpy as jnp
from jax import lax
from jax.experimental import pallas as pl
from jax.experimental.pallas import tpu as pltpu
from jax.sharding import PartitionSpec as P

MARGIN_BLOCK_SIZE = 64
SHIFT = 6
VMEM_LIMIT = 16 * 1024 * 1024
FIRST_LIMIT = 54 * 1024 * 1024
WORK = 1<<31
MUCH = 1 << 35
ME, CORE, DP, COUNTS = 0, 1, 2, 3
TARGET, COEF, BLOCKS = 0, 1, 2
F32, BF16 = jnp.float32, jnp.bfloat16


def dot(a, b, contract=((1,), (0,))):
    return lax.dot_general(a, b, (contract, ((), ())), preferred_element_type=F32)


def iota(shape, axis):
    return lax.broadcasted_iota(jnp.int32, shape, axis)


def ranks(hits):
    n = hits.shape[1]
    before = (iota((n, n), 0) < iota((n, n), 1)).astype(BF16)
    return jnp.where(hits > 0, dot(hits.astype(BF16), before), -1.0)


def call(kernel, n_pages, in_specs, out_specs, out_shape, operands, scratch=(), aliases={}, flops=0):
    return pl.pallas_call(
        kernel,
        grid_spec=pltpu.PrefetchScalarGridSpec(
            num_scalar_prefetch=1,
            grid=(n_pages,),
            in_specs=in_specs,
            out_specs=out_specs,
            scratch_shapes=scratch,
        ),
        out_shape=out_shape,
        compiler_params=pltpu.CompilerParams(vmem_limit_bytes=VMEM_LIMIT),
        cost_estimate=pl.CostEstimate(flops=flops, bytes_accessed=0, transcendentals=0),
        input_output_aliases=aliases,
    )(*operands)


def call_whole(kernel, out_shape, operands, flops=0):
    vmem = pl.BlockSpec(memory_space=pltpu.VMEM)
    return pl.pallas_call(
        kernel,
        in_specs=[pl.BlockSpec(memory_space=pltpu.SMEM)] + [vmem] * (len(operands) - 1),
        out_specs=[vmem] * len(out_shape),
        out_shape=out_shape,
        compiler_params=pltpu.CompilerParams(vmem_limit_bytes=VMEM_LIMIT),
        cost_estimate=pl.CostEstimate(flops=flops, bytes_accessed=0, transcendentals=0),
    )(*operands)


def page_of(array, first_page=0):
    rest = array.shape[1:]
    return pl.BlockSpec((1,) + rest, lambda p, info: (p + first_page,) + (0,) * len(rest))


def all_of(array):
    return pl.BlockSpec(array.shape, lambda p, info: (0,) * len(array.shape))


def pad_rows(n):
    return -(-n // 8) * 8


def stacked(rows):
    n, width = pad_rows(len(rows)), rows[0].shape[1]
    row = iota((n, width), 0)
    out = jnp.zeros((n, width), rows[0].dtype)
    for i, r in enumerate(rows):
        out = jnp.where(row == i, r, out)
    return out


def dispatch_kernel(plan, cap, info, routes, words, *outs, ready=lambda page: None):
    wdev = words.shape[1]
    slots = iota((cap, wdev), 0).astype(F32)
    by_page = {}
    for out, (offsets, first_page, n_pages) in zip(outs, plan):
        for p in range(n_pages):
            for i, offset in enumerate(offsets):
                by_page.setdefault(first_page + p, []).append((offset, out, i, p))
    tasks = [(page, *task) for page in by_page for task in by_page[page]]
    rank = ranks(
        stacked(
            [
                (routes[page] == jnp.bitwise_xor(info[ME], offset)).astype(F32)
                for page, offset, *_ in tasks
            ]
        )
    )
    n = 0
    for page, some in by_page.items():
        picks = [
            (slots == rank[n + i : n + i + 1]).astype(BF16) for i in range(len(some))
        ]
        ready(page)
        rows = dot(jnp.concatenate(picks, axis=0), words[page]).astype(BF16)
        for i, (_, out, place, p) in enumerate(some):
            out[place, p] = rows[i * cap : (i + 1) * cap]
        n += len(some)


def dispatch(info, routes, words, plan, cap, flops=0):
    width = words.shape[2]
    out = [
        jax.ShapeDtypeStruct((len(offsets), n_pages, cap, width), BF16)
        for offsets, _, n_pages in plan
    ]
    return call_whole(
        functools.partial(dispatch_kernel, plan, cap), out, (info, routes, words), flops
    )


def first_dispatch_kernel(plan, cap, info, routes, words, *refs):
    *outs, held_routes, held_words, sems = refs
    n_pages = held_words.shape[0]
    get_routes = pltpu.make_async_copy(routes, held_routes, sems.at[n_pages])
    get_words = [
        pltpu.make_async_copy(words.at[p], held_words.at[p], sems.at[p]) for p in range(n_pages)
    ]
    get_routes.start()
    for copy in get_words:
        copy.start()
    get_routes.wait()
    ready = lambda page: get_words[page].wait()
    dispatch_kernel(plan, cap, info, held_routes, held_words, *outs, ready=ready)


def first_dispatch(info, routes, words, plan, cap):
    _, wdev, width = words.shape
    n_pages = max(first_page + n for _, first_page, n in plan)
    out = [
        jax.ShapeDtypeStruct((len(offsets), n, cap, width), BF16) for offsets, _, n in plan
    ]
    anywhere, vmem = pl.BlockSpec(memory_space=pl.ANY), pl.BlockSpec(memory_space=pltpu.VMEM)
    return pl.pallas_call(
        functools.partial(first_dispatch_kernel, plan, cap),
        in_specs=[pl.BlockSpec(memory_space=pltpu.SMEM), anywhere, anywhere],
        out_specs=[vmem] * len(out),
        out_shape=out,
        scratch_shapes=[
            pltpu.VMEM(routes.shape, jnp.int32),
            pltpu.VMEM((n_pages, wdev, width), BF16),
            pltpu.SemaphoreType.DMA((n_pages + 1,)),
        ],
        compiler_params=pltpu.CompilerParams(vmem_limit_bytes=FIRST_LIMIT),
        cost_estimate=pl.CostEstimate(flops=0, bytes_accessed=0, transcendentals=0),
    )(info, routes, words)


def table_kernel(offsets, cap, own_blk, info, meta, flags, table, rank_out):
    me = info[ME]
    n_homes, pages, _, wdev = meta.shape
    nblk, all_blk = flags.shape[1:]
    n_rows = table.shape[1]
    slots = iota((cap, wdev), 0).astype(F32)
    rank = ranks(
        stacked(
            [
                (meta[i, p, 0:1, :] == me).astype(F32)
                for p in range(pages)
                for i in range(n_homes)
            ]
        )
    )
    lane = iota((n_rows, 128), 1)
    own = iota((all_blk, 128), 1) - BLOCKS
    chosen = (own >= 0) & (own < own_blk) & (iota((all_blk, 128), 0) == me * own_blk + own)
    chosen = chosen.astype(BF16)
    place = iota((1, wdev), 1) + 1
    for p in range(pages):
        t, idx = [], []
        for i, offset in enumerate(offsets):
            own = rank[p * n_homes + i : p * n_homes + i + 1]
            rank_out[p, i : i + 1] = own
            target = meta[i, p, 1:2, :]
            values = stacked([target >> 6, target & 63, place >> 6, place & 63]).astype(F32)
            got = dot((slots == own).astype(BF16), values.astype(BF16), ((1,), (1,)))
            got = got.astype(jnp.int32)
            t.append(got[:, 0:1] * 64 + got[:, 1:2])
            at = got[:, 2:3] * 64 + got[:, 3:4]
            idx.append(jnp.where(at > 0, at - 1 + jnp.bitwise_xor(me, offset) * wdev, -1))
        t, idx = jnp.concatenate(t, axis=0), jnp.concatenate(idx, axis=0)
        word_block = jnp.maximum(idx, 0) >> SHIFT == iota((n_rows, nblk), 1)
        margin = dot(word_block.astype(BF16), flags[p].astype(BF16)).astype(BF16)
        allowed = (dot(margin, chosen) > 0.5) | (lane - BLOCKS == t >> SHIFT)
        count = info[COUNTS + p]
        valid = (idx >= 0) & (idx < count)
        coef = jnp.where(valid, 64.0 / count.astype(F32), 0.0)
        value = jnp.where(allowed, 1.0, 0.0)
        table[p] = jnp.where(lane == TARGET, t.astype(F32), jnp.where(lane == COEF, coef, value))


def tables(info, meta, flags, offsets, cap, pps, flops=0):
    n_homes, pages, _, wdev = meta.shape
    out = [
        jax.ShapeDtypeStruct((pages, n_homes * cap, 128), F32),
        jax.ShapeDtypeStruct((pages, pad_rows(n_homes), wdev), F32),
    ]
    return call_whole(
        functools.partial(table_kernel, offsets, cap, pps // MARGIN_BLOCK_SIZE),
        out,
        (info, meta, flags),
        flops,
    )


def half_kernel(info, proj, out):
    half = out.shape[1]
    out[...] = proj[:, pl.ds(pl.multiple_of(info[CORE] * half, half), half)]


def half_of(info, proj):
    rows, width = proj.shape
    out = [jax.ShapeDtypeStruct((rows, width // 2), BF16)]
    return call_whole(half_kernel, out, (info, proj), MUCH)[0]


def weights_kernel(offsets, info, patches, *refs):
    gathered, (*before, out, proj, sems) = refs[: 2 * len(offsets)], refs[2 * len(offsets) :]
    half = proj.shape[1] // 2
    rows = gathered[0].shape[1]
    shards = [offset for some in offsets for offset in some]

    def copies():
        n = 0
        for core in range(2):
            at = 0
            for some, ref in zip(offsets, gathered[core * len(offsets) :]):
                for i in range(len(some)):
                    first = jnp.bitwise_xor(info[CORE], core) * half
                    to = proj.at[pl.ds(at * rows, rows), pl.ds(pl.multiple_of(first, half), half)]
                    yield pltpu.make_async_copy(ref.at[i], to, sems.at[n])
                    at, n = at + 1, n + 1

    @pl.when(pl.program_id(0) == 0)
    def _():
        started = list(copies())
        for copy in started:
            copy.start()
        for copy in started:
            copy.wait()

    for other in before:
        out[...] = other[...]
    got = dot(proj[...], patches[0], ((1,), (1,))).astype(BF16)
    for i, offset in enumerate(shards):
        to = pl.multiple_of(jnp.bitwise_xor(info[DP], offset) * rows, rows)
        out[0, pl.ds(to, rows)] = got[i * rows : (i + 1) * rows]


def weights(info, patches, gathered, offsets, before=(), flops=0):
    pages, pps, width = patches.shape
    n_shards = sum(len(some) for some in offsets)
    out = jax.ShapeDtypeStruct((pages, width, pps), BF16)
    return call(
        functools.partial(weights_kernel, offsets),
        pages,
        [page_of(patches)]
        + [pl.BlockSpec(memory_space=pl.ANY)] * len(gathered)
        + [page_of(b) for b in before],
        page_of(out),
        out,
        (info, patches, *gathered, *before),
        [
            pltpu.VMEM((n_shards * gathered[0].shape[1], width), BF16),
            pltpu.SemaphoreType.DMA((2 * n_shards,)),
        ],
        flops=flops,
    )


def page_kernel(n_homes, info, table, rank, weight, patches, *refs):
    *words, loss, x_t, dq = refs
    pps, width = patches.shape[1:]
    cap = words[0].shape[2]
    n_rows = n_homes * cap
    scale = 2.0 / math.sqrt(width)
    x = jnp.concatenate([w[0, 0] for w in words], axis=0)
    scores = dot(x, weight[0]) * scale
    is_target = iota((n_rows, pps), 1) == table[0, :, TARGET : TARGET + 1].astype(jnp.int32)
    coef = table[0, :, COEF : COEF + 1]
    lanes = table[0]
    spread = iota((128, pps), 0) - BLOCKS == iota((128, pps), 1) >> SHIFT
    marks = jnp.where(iota(lanes.shape, 1) < BLOCKS, 0.0, lanes).astype(BF16)
    masked = jnp.where(dot(marks, spread.astype(BF16)) > 0.5, scores, -jnp.inf)
    top = jnp.max(masked, axis=1, keepdims=True)
    expo = jnp.exp(masked - top)
    total = jnp.sum(expo, axis=1, keepdims=True)
    target_score = jnp.sum(jnp.where(is_target, scores, 0.0), axis=1, keepdims=True)
    row_loss = jnp.where(coef > 0, top + jnp.log(total) - target_score, 0.0)
    share = expo * (1.0 / total)
    dscore = (coef * jnp.where(is_target, share - 1.0, share)).astype(BF16)
    back = (dot(dscore, patches[0]) * scale).astype(BF16)
    more = dq.shape[0] - n_rows
    if more:
        back = jnp.concatenate([back, jnp.zeros((more, width), BF16)], axis=0)
        x = jnp.concatenate([x, jnp.zeros((more, width), BF16)], axis=0)
    dq[...] = back
    slots = iota((cap, rank.shape[2]), 0).astype(F32)
    for r in range(n_homes):
        picked = jnp.where(slots == rank[0, r : r + 1, :], row_loss[r * cap : (r + 1) * cap], 0.0)
        loss[0, r : r + 1, :] = jnp.sum(picked, axis=0, keepdims=True)
    x_t[...] = x.T


def run_pages(info, weight, patches, table, words, first_page, n_pages, at=0):
    _, _, cap, width = words[0][0].shape
    wdev = table[1].shape[2]
    n_homes = len(words)
    n_rows = -(-n_homes * cap // 128) * 128
    out = [
        jax.ShapeDtypeStruct((n_pages, n_homes, wdev), F32),
        jax.ShapeDtypeStruct((width, n_pages * n_rows), BF16),
        jax.ShapeDtypeStruct((n_pages * n_rows, width), BF16),
    ]
    inputs = (*table, weight, patches)
    return call(
        functools.partial(page_kernel, n_homes),
        n_pages,
        [page_of(a, first_page) for a in inputs]
        + [pl.BlockSpec((1, 1, cap, width), lambda p, info, i=i: (i, p + at, 0, 0)) for _, i in words],
        [
            page_of(out[0]),
            pl.BlockSpec((width, n_rows), lambda p, info: (0, p)),
            pl.BlockSpec((n_rows, width), lambda p, info: (p, 0)),
        ],
        out,
        (info, *inputs, *(w for w, _ in words)),
    )


def gradient_kernel(core, info, *refs):
    *pairs, out = refs
    before = [pairs.pop()] if len(pairs) % 2 else []
    n_y, _, wcol = out.shape

    def block(y, _):
        column = pl.multiple_of((2 * y + jnp.bitwise_xor(info[CORE], core)) * wcol, wcol)
        got = sum(
            dot(pairs[i][...], pairs[i + 1][:, pl.ds(column, wcol)])
            for i in range(0, len(pairs), 2)
        )
        for part in before:
            got = got + part[y]
        out[y] = got.astype(out.dtype)
        return 0

    lax.fori_loop(0, n_y, block, 0)


def gradient(info, core, dtype, n_y, pairs, before=(), flops=0):
    width = pairs[0][0].shape[0]
    out = [jax.ShapeDtypeStruct((n_y, width, width // (2 * n_y)), dtype)]
    operands = (info, *(x for pair in pairs for x in pair), *before)
    return call_whole(functools.partial(gradient_kernel, core), out, operands, flops)[0]


def exchange(x, axis, offset):
    n = lax.axis_size(axis)
    return lax.ppermute(x, axis, [(i, i ^ offset) for i in range(n)])


def exchange_both(x, dp, seq):
    n_seq = lax.axis_size("seq")
    n = lax.axis_size("dp") * n_seq
    return lax.ppermute(x, ("dp", "seq"), [(i, i ^ (dp * n_seq + seq)) for i in range(n)])


def pick(x, places):
    places = list(places) + [None] * (x.ndim - len(places))
    start = [0 if i is None else i for i in places]
    size = [n if i is None else 1 for i, n in zip(places, x.shape)]
    got = lax.dynamic_slice(x, start, size, allow_negative_indices=False)
    return got.reshape([n for i, n in zip(places, x.shape) if i is None])


def local(words, patches, proj, routes, targets, counts, flags):
    pages, wdev, width = words.shape
    pps = patches.shape[1]
    n_seq = lax.axis_size("seq")
    n_dp = lax.axis_size("dp")
    n_y, n_high = n_seq // 2, n_dp // 2
    cap = 2 * wdev // n_seq
    shard_rows = proj.shape[0]
    near, far = (0, 1), tuple(range(2, n_seq))

    me, my_dp = lax.axis_index("seq"), lax.axis_index("dp")
    core, y, low, high = me & 1, me >> 1, my_dp & 1, my_dp >> 1
    own = {
        "low": [low ^ k for k in range(2)],
        "y": [y ^ k for k in range(n_y)],
        "high": [high ^ k for k in range(n_high)],
    }
    info = jnp.concatenate([jnp.stack([me, core, my_dp]).astype(jnp.int32), counts])
    info, own, proj = lax.optimization_barrier((info, own, proj))
    routes = routes.reshape(pages, 1, wdev)

    split = pages - 1
    both = dispatch(
        info, routes, words, [((2 * k, 2 * k + 1), 0, split) for k in range(1, n_y)], cap
    )
    info, proj, both = lax.optimization_barrier((info, proj, both))
    both = [exchange(rows, "seq", 2 * (k + 1)) for k, rows in enumerate(both)]
    piece = half_of(info, proj)
    pieces = [piece] + [exchange(piece, "dp", 2 * k) for k in range(1, n_high)]
    group = n_high // 2
    stay, across, *rest = dispatch(
        info,
        routes,
        words,
        [((r,), 0, pages) for r in near] + [((r,), split, pages - split) for r in far],
        cap,
        WORK,
    )
    pieces[1:group], rest, stay, across = lax.optimization_barrier(
        (pieces[1:group], rest, stay, across)
    )
    early = jnp.stack(pieces[:group])
    early = [early, exchange(early, "dp", 1)]
    late_offsets = [[2 * k + bit] for k in range(group, n_high) for bit in range(2)]

    pair = jnp.concatenate([routes, targets.reshape(pages, 1, wdev)], axis=1)
    meta_near = jnp.stack([pair, exchange(pair, "seq", 1)])
    table_near = tables(info, meta_near, flags, near, cap, pps, WORK)
    meta_far = jnp.concatenate([exchange(meta_near, "seq", 2 * k) for k in range(1, n_y)], axis=0)

    early, pieces[group:], table_near = lax.optimization_barrier(
        (early, pieces[group:], table_near)
    )
    late = [jnp.stack([piece]) for piece in pieces[group:]]

    early += [exchange(some, "seq", 1) for some in early]
    early, late[-1] = lax.optimization_barrier((early, late[-1]))
    weight = weights(
        info, patches, early, [[2 * k + bit for k in range(group)] for bit in range(2)], (), WORK
    )
    late = [x for piece in late for x in (piece, exchange(piece, "dp", 1))]
    late, weight = lax.optimization_barrier((late, weight))
    across = exchange(across, "seq", 1)
    late += [exchange(piece, "seq", 1) for piece in late]
    rest = [exchange(rows, "seq", r) for rows, r in zip(rest, far)]
    weight = weights(info, patches, late, late_offsets, [weight])
    run = functools.partial(run_pages, info, weight, patches)
    near_words = [(stay, 0), (across, 0)]
    some = pages // 2
    loss, *pair_0 = run(table_near, near_words, 0, some)
    both, meta_far, pair_0 = lax.optimization_barrier((both, meta_far, pair_0))
    first = [pair for rows in both for pair in ((rows, 0), (exchange(rows, "seq", 1), 1))]
    loss_1, *pair_1 = run(table_near, near_words, some, pages - some, some)
    loss = jnp.concatenate([loss, loss_1], axis=0)
    near_loss = [loss[:, 0], exchange(loss[:, 1], "seq", 1)]
    pair_1, meta_far = lax.optimization_barrier((pair_1, meta_far))
    table_far = tables(info, meta_far, flags, far, cap, pps)
    loss_a, *pair_a = run(table_far, first, 0, split)
    before = gradient(info, 1, F32, n_y, [pair_0, pair_1])
    rest, pair_a, before = lax.optimization_barrier((rest, pair_a, before))
    loss_b, *pair_b = run(table_far, [(rows, 0) for rows in rest], split, pages - split)
    losses = jnp.concatenate([loss_a, loss_b], axis=0)
    word_loss = near_loss + [exchange(losses[:, i], "seq", r) for i, r in enumerate(far)]

    pairs = [pair_0, pair_1, pair_a, pair_b]
    sent = gradient(info, 1, BF16, n_y, [pair_a, pair_b], [before])
    kept = gradient(info, 0, F32, n_y, pairs, (), MUCH)
    form = (n_y, n_high, 2, shard_rows, width // n_seq)
    terms = [kept.reshape(form), exchange(sent, "seq", 1).reshape(form)]
    part = lambda i, j: sum(
        pick(t, (own["y"][i], None, own["low"][j])).astype(F32) for t in terms
    )
    total = part(0, 0)
    for i, j in [(0, 1)] + [(i, j) for i in range(1, n_y) for j in (1, 0)]:
        total = total + exchange_both(part(i, j).astype(BF16), j, 2 * i)
    grad = pick(total, (own["high"][0],))
    for k in range(1, n_high):
        grad = grad + exchange(pick(total, (own["high"][k],)).astype(BF16), "dp", 2 * k)
    return (sum(word_loss), grad)


def solution(mesh):
    in_specs = (
        P("dp", "seq", None),
        P("dp", "seq", None),
        P("dp", None),
        P("dp", "seq", None),
        P("dp", "seq"),
        P("dp"),
        P("dp", None, None),
    )
    out_specs = (P("dp", "seq"), P("dp", "seq"))
    return jax.shard_map(local, mesh=mesh, in_specs=in_specs, out_specs=out_specs, check_vma=False)
```
